32 devices in a mesh: section: 2 (over core), group: 4 (over y, x), tensor: 4 (over z).
Axes of the slice: x: 2, y: 2, z: 4, core: 2. Of those that a mesh axis runs over, the one named last changes fastest.
Arguments:
- queries: bfloat16 [64, 3072], P(('section', 'group'), 'tensor'), may hold values from -140 to 140
- new_kv: bfloat16 [64, 2048], P(('section', 'group'), 'tensor'), may hold values from -10 to 10
- kv_cache: bfloat16 [8, 2048, 2048], P(('section', 'group'), None, 'tensor'), may hold values from -4.5 to 4.5
- cache_len: int32 [8], P(('section', 'group')), may hold values from 1 to 2048, 10240 in all
- residual: bfloat16 [64, 3072], P(('section', 'group'), 'tensor'), may hold values from -28 to 28
- norm_gain: bfloat16 [3072], P('tensor'), may hold values from 0.099609375 to 1.8984375
- router: bfloat16 [8, 3072], P(None, 'tensor'), may hold values from -0.23925781 to 0.23925781
- routes: int32 [64, 4], P(('section', 'group')), may hold values from 0 to 7, all different within a row; in each aligned block of 8 rows (0 to 7, 8 to 15, ...) at most 8 rows name the same one
- gate_w: bfloat16 [8, 6912, 3072], P(('section', 'tensor'), 'group'), may hold values from -0.109375 to 0.109375
- up_w: bfloat16 [8, 6912, 3072], P(('section', 'tensor'), 'group'), may hold values from -0.109375 to 0.109375
- down_w: bfloat16 [8, 6912, 3072], P(('section', 'tensor'), 'group'), may hold values from -0.078125 to 0.078125
Outputs:
- mixed: bfloat16 [64, 3072], P(('section', 'group'), 'tensor')
The draws below stay inside these ranges and needn't reach their ends.
Inputs may be any that keep to these rules, and one draw needn't show every extreme that they name: `routes`: each token names 4 different experts; in each aligned block of 8 tokens (the branches of one prefix) no expert is named by more than 8 tokens, and in some block one expert is named by exactly 8. `cache_len`: the largest is 2048.
All inputs are finite; a program needn't handle non-finite values. No bound on the sum of `cache_len` on one device may be relied on, other than what follows from the above.
Results may differ from the reference program's by a relative error of at most 0.0065.
Values may be sent and summed in bfloat16 or wider, within the bound.
No kernel may reach another device: no remote copies, remote signals or barrier semaphores. Data moves between devices by JAX's collectives and lax.ppermute only.
A program may use at most 128 MiB of HBM per device.

```python
import math
import jax
import jax.numpy as jnp
import numpy as np
from jax import lax

D = 3072
HEADS = 24
KV_HEADS = 8
HEAD_DIM = 128
FF = 6912
TOPK = 4
CTX = 2048
BRANCH = 8
EXPERTS = 8
PREFIXES = 8
TOKENS = 64
CAP = 8
ROWS_E = 64
N_GROUP = 4


def shared_keys(key):
    return jnp.clip(jax.random.normal(jax.random.fold_in(key, 7), (PREFIXES, KV_HEADS, HEAD_DIM), jnp.float32), -4.5, 4.5)


def draw_queries(key, part):
    key = jax.random.fold_in(key, 31)
    sample = jnp.clip(2.0 * jax.random.normal(key, (PREFIXES, BRANCH, HEADS * HEAD_DIM), jnp.float32), -8.0, 8.0)
    return sample.reshape(TOKENS, HEADS * HEAD_DIM).astype(jnp.bfloat16)


def draw_kv_cache(key, part):
    anchor = shared_keys(key)
    key = jax.random.fold_in(key, 53)
    cache_shape = (PREFIXES, CTX, KV_HEADS, 2, HEAD_DIM)
    filled = jnp.clip(jax.random.normal(key, cache_shape, jnp.float32), -4.5, 4.5)
    filled = filled.at[:, 0, :, 0].set(anchor)
    return filled.reshape(PREFIXES, CTX, KV_HEADS * 2 * HEAD_DIM).astype(jnp.bfloat16)


def draw_residual(key, part):
    key = jax.random.fold_in(key, 71)
    jitter = jax.random.uniform(jax.random.fold_in(key, 2), (D,), jnp.float32, 0.7, 1.4)
    col_scale = 0.5 * 3.0 ** (jnp.arange(D).astype(jnp.float32) / D) * jitter
    row_scale = jnp.exp(jax.random.uniform(jax.random.fold_in(key, 1), (TOKENS,), jnp.float32, jnp.log(0.25), jnp.log(2.5)))
    values = jnp.clip(jax.random.normal(key, (TOKENS, D), jnp.float32), -4.0, 4.0)
    return (values * row_scale[:, None] * col_scale[None, :]).astype(jnp.bfloat16)


def levels(own_key, dims, split, least, high):
    def one(axis_at, shards_of):
        draws = jax.random.uniform(jax.random.fold_in(jax.random.fold_in(own_key, 6), axis_at), (shards_of,), jnp.float32, least / len(split), high / len(split))
        return jnp.repeat(jnp.exp(draws), dims[axis_at] // shards_of).reshape((-1,) + (1,) * (len(dims) - axis_at - 1))

    level = one(*split[0])
    for cut in split[1:]:
        level = level * one(*cut)
    return level


def length_profile(count, total, limit, skew):
    loads = [(1 << 20) // math.isqrt(standing ** skew) + 1 for standing in range(2, count + 1)]
    surplus, holding = total - limit - (count - 1), [1] * (count - 1)
    while surplus > 0:
        candidates = [i for i in range(count - 1) if holding[i] < limit]
        pool, budget = sum([loads[i] for i in candidates]), surplus
        for i in candidates:
            addition = min(limit - holding[i], max(1, budget * loads[i] // pool), surplus)
            holding[i] = holding[i] + addition
            surplus = surplus - addition
    return np.array([limit] + holding)


def ragged(key, count, total, bound, skew):
    if count == 2:
        one = jax.random.randint(key, (), max(1, total - bound), min(bound, total - 1) + 1)
        return jnp.stack([one, total - one])
    tallies = jnp.asarray(length_profile(count, total, bound, skew), jnp.int32)
    couples = (count - 1) // 2
    giver, sink = tallies[1:1 + 2 * couples:2], tallies[2:2 + 2 * couples:2]
    room = jnp.minimum(giver - 1, bound - sink)
    passed = jax.random.randint(jax.random.fold_in(key, 1), (couples,), 0, 1 << 20) % (room + 1)
    tallies = tallies.at[1:1 + 2 * couples:2].set(giver - passed).at[2:2 + 2 * couples:2].set(sink + passed)
    return tallies[jax.random.permutation(jax.random.fold_in(key, 2), count)]


def assign_block(own_key, own, number, rows, amount, top, bound, slope):
    order = jax.random.permutation(own_key, amount)
    heavy_load, ordinary = shares(amount, rows * top, bound, slope, True), shares(amount, rows * top, bound, slope, False)
    places = jnp.arange(amount)

    def named(tallies, turn):
        used = int((tallies > 0).sum())
        fixed = max(1, used // 4)
        moved = fixed + (places - fixed + turn * (used - fixed)) % max(1, amount - fixed)
        return jnp.zeros((amount,), jnp.int32).at[order[jnp.where(places < fixed, places, moved)]].set(jnp.asarray(tallies, jnp.int32))

    tallies = jnp.where(number % 4 == 0, named(heavy_load, number // 4), named(ordinary, number - number // 4 - 1))
    mixed = jax.random.permutation(jax.random.fold_in(own, 3), amount)
    giver, sink = mixed[0:amount // 2 * 2:2], mixed[1:amount // 2 * 2:2]
    margin = jnp.minimum(tallies[giver] - 1, bound - tallies[sink]) // 2
    margin = jnp.where((giver == order[0]) | (sink == order[0]) | (tallies[sink] == 0), 0, jnp.maximum(margin, 0))
    moved = jax.random.randint(jax.random.fold_in(own, 4), (amount // 2,), 0, 1 << 20) % (margin + 1)
    tallies = tallies.at[giver].add(-moved).at[sink].add(moved)
    members = jnp.searchsorted(jnp.cumsum(tallies), jnp.arange(rows * top), side="right").astype(jnp.int32)
    grid = members.reshape(top, rows).T
    grid = grid[jax.random.permutation(jax.random.fold_in(own, 1), rows)]
    turn = jax.random.randint(jax.random.fold_in(own, 2), (rows, 1), 0, top)
    return jnp.take_along_axis(grid, (jnp.arange(top)[None, :] + turn) % top, axis=1)


def shares(amount, total, limit, skew, full):
    loads = [(1 << 20) // math.isqrt(grade ** skew) + 1 for grade in range(1, amount + 1)]
    largest = limit if full else min(limit, max(-(-total // amount), total * loads[0] // sum(loads)))
    least = 1 if total - largest >= amount - 1 else 0
    given, rest = [largest] + [least] * (amount - 1), total - largest - least * (amount - 1)
    while rest > 0:
        free = [i for i in range(1, amount) if given[i] < largest] or [i for i in range(1, amount) if given[i] < limit]
        whole, budget = sum([loads[i] for i in free]), rest
        for i in free:
            extra = min(limit - given[i], max(1, budget * loads[i] // whole), rest)
            given[i] = given[i] + extra
            rest = rest - extra
    return np.array(given)


def scatter_about(own_key, extent, spread, bound, split=(), kind=jnp.bfloat16):
    result = jax.random.normal(own_key, extent, jnp.float32) * spread
    if len(split) > 0:
        result = levels(own_key, extent, split, -0.22, 0.18) * result
    return jnp.clip(result, min=-bound, max=bound).astype(kind)


def setup_inputs(seed: int = 0) -> dict:
    seeds = jax.random.split(jax.random.key(seed), 12)
    queries = draw_queries(jax.random.fold_in(seeds[11], 71), 0)
    new_kv = scatter_about(seeds[1], (TOKENS, KV_HEADS * 2 * HEAD_DIM), 2.0, 10.0, ((0, 8), (1, 4)))
    kv_cache = draw_kv_cache(jax.random.fold_in(seeds[11], 71), 0)
    cache_len = ragged(seeds[3], PREFIXES, PREFIXES * CTX * 5 // 8, CTX, 1).astype(jnp.int32)
    residual = draw_residual(jax.random.fold_in(seeds[11], 71), 0)
    norm_gain = jnp.clip(1.0 + 0.18 * jax.random.normal(seeds[5], (D,), jnp.float32), 0.099609375, 1.8984375).astype(jnp.bfloat16)
    router = scatter_about(seeds[6], (EXPERTS, D), 0.04, 0.23925781, ((1, 4),))
    routes_keys = jax.random.split(jax.random.fold_in(seeds[7], 1), TOKENS // BRANCH)
    routes_turns = jax.random.permutation(jax.random.fold_in(seeds[7], 3), TOKENS // BRANCH)
    routes = jax.vmap(lambda own, number: assign_block(jax.random.fold_in(seeds[7], 2), own, number, BRANCH, EXPERTS, TOPK, CAP, 2))(routes_keys, routes_turns).reshape((TOKENS, TOPK))
    gate_w = scatter_about(seeds[8], (EXPERTS, FF, D), D ** -0.5, 0.109375, ((0, 8), (1, 4)))
    up_w = scatter_about(seeds[9], (EXPERTS, FF, D), D ** -0.5, 0.109375, ((0, 8), (1, 4)))
    down_w = scatter_about(seeds[10], (EXPERTS, FF, D), FF ** -0.5, 0.078125, ((0, 8), (1, 4)))
    return dict(queries=queries, new_kv=new_kv, kv_cache=kv_cache, cache_len=cache_len, residual=residual, norm_gain=norm_gain, router=router, routes=routes, gate_w=gate_w, up_w=up_w, down_w=down_w)


def attend_prefix(query_rows, fresh_rows, cache_rows, length):
    grouped = HEADS // KV_HEADS
    query_head_rows = query_rows.astype(jnp.float32).reshape(BRANCH, KV_HEADS, grouped, HEAD_DIM)
    latest_token_view = fresh_rows.astype(jnp.float32).reshape(BRANCH, KV_HEADS, 2, HEAD_DIM)
    cache_view = cache_rows.astype(jnp.float32).reshape(CTX, KV_HEADS, 2, HEAD_DIM)
    logit_scale_factor = HEAD_DIM ** (-0.5)
    scores = jnp.einsum('bkgd,jkd->bkgj', query_head_rows, cache_view[:, :, 0]) * logit_scale_factor
    scores = jnp.where(jnp.arange(CTX) < length, scores, -jnp.inf)
    self_token_score = jnp.einsum('eacx,eax->eac', query_head_rows, latest_token_view[:, :, 0]) * logit_scale_factor
    row_max = jnp.maximum(lax.optimization_barrier(jnp.max(scores, -1)), self_token_score)
    weights = jnp.exp(scores - row_max[..., None]).astype(jnp.bfloat16)
    own_weight = jnp.exp(self_token_score - row_max).astype(jnp.bfloat16)
    weights, own_weight = lax.optimization_barrier((weights, own_weight))
    weights_wide = weights.astype(jnp.float32)
    own_wide = own_weight.astype(jnp.float32)
    numerator = jnp.einsum('bkgj,jkd->bkgd', weights_wide, cache_view[:, :, 1])
    numerator = numerator + own_wide[..., None] * latest_token_view[:, :, 1][:, :, None, :]
    softmax_divisor = lax.optimization_barrier(jnp.sum(weights_wide, -1)) + own_wide
    return (numerator / softmax_divisor[..., None]).reshape(BRANCH, HEADS * HEAD_DIM)

def attend_packed(packed):
    return attend_prefix(packed[0], packed[1], packed[2], packed[3])

def reference(queries, new_kv, kv_cache, cache_len, residual, norm_gain, router, routes, gate_w, up_w, down_w):
    attention = lax.map(attend_packed, (queries.reshape(PREFIXES, BRANCH, -1), new_kv.reshape(PREFIXES, BRANCH, -1), kv_cache, cache_len))
    attention = attention.reshape(TOKENS, D)
    stream = (residual.astype(jnp.float32) + attention).astype(jnp.bfloat16)
    stream_float = stream.astype(jnp.float32)
    mean_value = lax.optimization_barrier(jnp.sum(stream_float, 1)) / D
    variance = lax.optimization_barrier(jnp.sum(stream_float * stream_float, 1)) / D - mean_value * mean_value
    inv_std = lax.rsqrt(variance + 1e-05)
    normed = ((stream_float - mean_value[:, None]) * inv_std[:, None] * norm_gain.astype(jnp.float32)).astype(jnp.bfloat16)
    logits = jnp.dot(normed, router.T, preferred_element_type=jnp.float32)
    single_hot_mask = routes[..., None] == jnp.arange(EXPERTS, dtype=jnp.int32)
    picked = lax.optimization_barrier(jnp.sum(jnp.where(single_hot_mask, logits[:, None, :], 0.0), -1))
    raised = jnp.exp(picked)
    gate_share = raised / lax.optimization_barrier(jnp.sum(raised, -1, keepdims=True))

    def expert_step(mixture, packed):
        expert_id, gate_local, up_local, down_local = packed
        routed_mask = routes == expert_id
        token_share = lax.optimization_barrier(jnp.sum(jnp.where(routed_mask, gate_share, 0.0), 1))
        chosen_rows = jnp.any(routed_mask, 1)
        index_rows = jnp.nonzero(chosen_rows, size=ROWS_E, fill_value=0)[0].astype(jnp.int32)
        valid_rows = jnp.arange(ROWS_E) < jnp.sum(chosen_rows.astype(jnp.int32))
        selected = normed[index_rows]
        gate_part = jnp.dot(selected, gate_local.T, preferred_element_type=jnp.float32)
        upward = jnp.dot(selected, up_local.T, preferred_element_type=jnp.float32)
        hidden = (jax.nn.silu(gate_part) * upward).astype(jnp.bfloat16)
        pieces = jnp.einsum('rgf,gfd->rgd', hidden.astype(jnp.float32).reshape(ROWS_E, N_GROUP, -1), down_local.astype(jnp.float32).reshape(N_GROUP, -1, D)).astype(jnp.bfloat16)
        pieces = lax.optimization_barrier(pieces)
        output = lax.optimization_barrier(jnp.sum(pieces.astype(jnp.float32), 1)).astype(jnp.bfloat16)
        output = lax.optimization_barrier(output)
        contribution = jnp.where(valid_rows, token_share[index_rows], 0.0)[:, None] * output.astype(jnp.float32)
        return (mixture.at[index_rows].add(contribution), None)
    mixture, unused = lax.scan(expert_step, jnp.zeros((TOKENS, D), jnp.float32), (jnp.arange(EXPERTS, dtype=jnp.int32), gate_w, up_w, down_w))
    return (stream_float + mixture).astype(jnp.bfloat16)
```

```python
import functools

import jax
import jax.numpy as jnp
from jax import lax
from jax.experimental import pallas as pl
from jax.experimental.pallas import tpu as pltpu
from jax.sharding import PartitionSpec as P

HEAD_DIM = 128
NORM_EPS = 1e-05
LANES = 128
MIB = 1 << 20


def attention_kernel(len_ref, q_ref, new_ref, kv_hbm, res_ref, routes_ref, out_ref, kv, scores, sems, *, chunks):
    slots = kv_hbm.shape[1]
    part = slots // chunks
    copies = []
    for c in range(chunks):
        rows = pl.ds(c * part, part)
        copies.append(pltpu.make_async_copy(kv_hbm.at[0, rows], kv.at[rows], sems.at[c]))
        copies[-1].start()
    tokens, columns = q_ref.shape
    key_heads = new_ref.shape[1] // (2 * HEAD_DIM)
    grouped = columns // HEAD_DIM // key_heads
    rows = grouped * tokens
    scale = HEAD_DIM ** (-0.5)
    queries, selves = [], []
    for h in range(key_heads):
        first = h * grouped * HEAD_DIM
        q = jnp.concatenate(
            [
                q_ref[:, first + j * HEAD_DIM : first + (j + 1) * HEAD_DIM].astype(jnp.float32)
                for j in range(grouped)
            ],
            axis=0,
        )
        own_key = new_ref[:, 2 * h * HEAD_DIM : (2 * h + 1) * HEAD_DIM].astype(jnp.float32)
        own_key = jnp.concatenate([own_key] * grouped, axis=0)
        selves.append(jnp.sum(q * own_key, axis=1, keepdims=True) * scale)
        queries.append(q.astype(jnp.bfloat16))
    experts = LANES
    routes = routes_ref[...]
    expert_at = lax.broadcasted_iota(jnp.int32, (experts, tokens), 0)
    named = jnp.zeros((experts, tokens), jnp.float32)
    for k in range(routes.shape[0]):
        named = jnp.where(expert_at == routes[k : k + 1, :], 1.0, named)
    out_ref[:, columns:] = named.T.astype(out_ref.dtype)
    live = len_ref[0]
    for c in range(chunks):
        copies[c].wait()
        for h in range(key_heads):
            keys = kv[c * part : (c + 1) * part, 2 * h * HEAD_DIM : (2 * h + 1) * HEAD_DIM]
            s = lax.dot_general(
                queries[h], keys, (((1,), (1,)), ((), ())), preferred_element_type=jnp.float32
            )
            at = lax.broadcasted_iota(jnp.int32, (rows, part), 1) + c * part
            scores[h, :, c * part : (c + 1) * part] = jnp.where(at < live, s * scale, -jnp.inf)
    for h in range(key_heads):
        s = scores[h]
        top = jnp.maximum(jnp.max(s, axis=1, keepdims=True), selves[h])
        weights = jnp.exp(s - top).astype(jnp.bfloat16)
        own = jnp.exp(selves[h] - top).astype(jnp.bfloat16).astype(jnp.float32)
        total = jnp.sum(weights.astype(jnp.float32), axis=1, keepdims=True) + own
        value_at = (2 * h + 1) * HEAD_DIM
        mixed = jnp.dot(weights, kv[:, value_at : value_at + HEAD_DIM], preferred_element_type=jnp.float32)
        own_value = new_ref[:, value_at : value_at + HEAD_DIM].astype(jnp.float32)
        mixed = (mixed + own * jnp.concatenate([own_value] * grouped, axis=0)) / total
        for j in range(grouped):
            at = (h * grouped + j) * HEAD_DIM
            got = res_ref[:, at : at + HEAD_DIM].astype(jnp.float32) + mixed[j * tokens : (j + 1) * tokens]
            out_ref[:, at : at + HEAD_DIM] = got.astype(out_ref.dtype)


def attend(cache_len, queries, new_kv, kv_cache, residual, routes):
    tokens, columns = queries.shape
    slots, width = kv_cache.shape[1:]
    key_heads = new_kv.shape[1] // (2 * HEAD_DIM)
    rows = columns // HEAD_DIM // key_heads * tokens
    chunks = 4
    vmem = pl.BlockSpec(memory_space=pltpu.VMEM)
    return pl.pallas_call(
        functools.partial(attention_kernel, chunks=chunks),
        out_shape=jax.ShapeDtypeStruct((tokens, columns + LANES), jnp.bfloat16),
        in_specs=[
            pl.BlockSpec(memory_space=pltpu.SMEM),
            vmem,
            vmem,
            pl.BlockSpec(memory_space=pl.ANY),
            vmem,
            vmem,
        ],
        out_specs=vmem,
        scratch_shapes=[
            pltpu.VMEM((slots, width), kv_cache.dtype),
            pltpu.VMEM((key_heads, rows, slots), jnp.float32),
            pltpu.SemaphoreType.DMA((chunks,)),
        ],
        compiler_params=pltpu.CompilerParams(vmem_limit_bytes=8 * MIB),
        cost_estimate=pl.CostEstimate(
            flops=4 * rows * slots * HEAD_DIM * key_heads,
            bytes_accessed=slots * width * 2,
            transcendentals=rows * slots * key_heads,
        ),
        name="attention",
    )(cache_len, queries, new_kv, kv_cache, residual, routes.T)


def expert_kernel(place_ref, near_ref, far_ref, *refs, ranks, tensors, experts):
    params = refs[:tensors]
    gate_ref, up_ref, down_ref, near_out, far_out, normed, hidden, share = refs[tensors:]
    place, expert = place_ref[0], place_ref[1]
    tokens, block = near_ref.shape[2], near_out.shape[3]
    model = tensors * block
    half = ranks * tokens

    def column(k):
        return pl.multiple_of(lax.rem(place - k + tensors, tensors) * block, block)

    pair = 2
    for side, ref in enumerate((near_ref, far_ref)):
        for g in range(0, ranks, pair):
            pieces = [
                jnp.concatenate(
                    [ref[g + p, k, :, :block].astype(jnp.float32) for p in range(pair)], axis=0
                )
                for k in range(tensors)
            ]
            mean = sum(jnp.sum(x, axis=1, keepdims=True) for x in pieces) / model
            square = sum(jnp.sum(x * x, axis=1, keepdims=True) for x in pieces) / model
            inv = lax.rsqrt(square - mean * mean + NORM_EPS)
            at = side * half + g * tokens
            logits = jnp.zeros((pair * tokens, experts), jnp.float32)
            for k in range(tensors):
                gain = params[k][experts : experts + 1, :].astype(jnp.float32)
                x = ((pieces[k] - mean) * inv * gain).astype(jnp.bfloat16)
                normed[at : at + pair * tokens, pl.ds(column(k), block)] = x
                logits += lax.dot_general(
                    x, params[k][:experts, :], (((1,), (1,)), ((), ())), preferred_element_type=jnp.float32
                )
            named = jnp.concatenate(
                [ref[g + p, 0, :, block:].astype(jnp.float32)[:, :experts] for p in range(pair)], axis=0
            )
            raised = jnp.where(named > 0, jnp.exp(logits), 0.0)
            lane = lax.broadcasted_iota(jnp.int32, raised.shape, 1)
            mine = jnp.sum(jnp.where(lane == expert, raised, 0.0), axis=1, keepdims=True)
            share[at : at + pair * tokens, :] = jnp.broadcast_to(
                mine / jnp.sum(raised, axis=1, keepdims=True), (pair * tokens, LANES)
            )

    units = gate_ref.shape[1]
    step = 256

    def up_block(at, size):
        x = normed[...]
        contract = (((1,), (1,)), ((), ()))
        a = lax.dot_general(x, gate_ref[0, pl.ds(at, size), :], contract, preferred_element_type=jnp.float32)
        b = lax.dot_general(x, up_ref[0, pl.ds(at, size), :], contract, preferred_element_type=jnp.float32)
        hidden[:, pl.ds(at, size)] = (a / (1.0 + jnp.exp(-a)) * b).astype(jnp.bfloat16)

    @pl.loop(0, units // step)
    def _(i):
        up_block(pl.multiple_of(i * step, step), step)

    if units % step:
        up_block(units // step * step, units % step)

    for k in range(tensors):
        part = jnp.dot(hidden[...], down_ref[0, :, pl.ds(column(k), block)], preferred_element_type=jnp.float32)
        part = part * share[:, :1]
        for side, ref in enumerate((near_out, far_out)):
            for g in range(ranks):
                at = side * half + g * tokens
                ref[g, k] = part[at : at + tokens].astype(ref.dtype)


def run_expert(place, near, far, params, gate_w, up_w, down_w, experts):
    ranks, tensors, tokens, wide = near.shape
    block = wide - LANES
    units, model = gate_w.shape[1:]
    rows = 2 * ranks * tokens
    vmem = pl.BlockSpec(memory_space=pltpu.VMEM)
    weight = pl.BlockSpec(memory_space=pltpu.VMEM)
    shape = jax.ShapeDtypeStruct((ranks, tensors, tokens, block), jnp.bfloat16)
    weights = [pltpu.with_memory_space_constraint(w, pltpu.VMEM) for w in (gate_w, up_w, down_w)]
    return pl.pallas_call(
        functools.partial(expert_kernel, ranks=ranks, tensors=tensors, experts=experts),
        out_shape=(shape, shape),
        in_specs=[pl.BlockSpec(memory_space=pltpu.SMEM), vmem, vmem] + [vmem] * tensors + [weight] * 3,
        out_specs=(vmem, vmem),
        scratch_shapes=[
            pltpu.VMEM((rows, model), jnp.bfloat16),
            pltpu.VMEM((rows, units), jnp.bfloat16),
            pltpu.VMEM((rows, LANES), jnp.float32),
        ],
        compiler_params=pltpu.CompilerParams(vmem_limit_bytes=(10 if rows <= 64 else 24) * MIB),
        cost_estimate=pl.CostEstimate(
            flops=6 * rows * units * model, bytes_accessed=6 * units * model, transcendentals=rows * units
        ),
        name="experts",
    )(place, near, far, *params, *weights)


def shift(x, axis, by):
    size = lax.axis_size(axis)
    return lax.ppermute(x, axis, [(i, (i + by) % size) for i in range(size)])


def add(*terms):
    return sum(t.astype(jnp.float32) for t in terms)


def per_device(
    queries, new_kv, kv_cache, cache_len, residual, norm_gain, router, routes, gate_w, up_w, down_w
):
    groups, tensors = lax.axis_size("group"), lax.axis_size("tensor")
    experts, block = router.shape
    own_params = jnp.concatenate([router, norm_gain[None, :], jnp.zeros((7, block), router.dtype)], axis=0)
    params = [own_params] + [shift(own_params, "tensor", k) for k in range(1, tensors)]
    place = lax.axis_index("tensor")
    where = jnp.stack([place, lax.axis_index("section") * tensors + place]).astype(jnp.int32)

    fresh = attend(cache_len, queries, new_kv, kv_cache, residual, routes)
    rows = jnp.stack([fresh] + [shift(fresh, "tensor", k) for k in range(1, tensors)])
    near = jnp.stack([rows] + [shift(rows, "group", k) for k in range(1, groups)])
    far = shift(near, "section", 1)

    mine, theirs = run_expert(where, near, far, params, gate_w, up_w, down_w, experts)
    both = add(mine, shift(theirs, "section", 1)).astype(jnp.bfloat16)
    got = add(both[0], *[shift(both[k], "group", -k) for k in range(1, groups)]).astype(jnp.bfloat16)
    mixed = add(fresh[:, :block], got[0], *[shift(got[k], "tensor", -k) for k in range(1, tensors)])
    return mixed.astype(jnp.bfloat16)


def solution(mesh):
    rows = P(("section", "group"), "tensor")
    weights = P(("section", "tensor"), "group", None)
    in_specs = (
        rows,
        rows,
        P(("section", "group"), None, "tensor"),
        P(("section", "group")),
        rows,
        P("tensor"),
        P(None, "tensor"),
        P(("section", "group"), None),
        weights,
        weights,
        weights,
    )
    return jax.shard_map(per_device, mesh=mesh, in_specs=in_specs, out_specs=rows, check_vma=False)
```

```python
import functools

import jax
import jax.numpy as jnp
from jax import lax
from jax.experimental import pallas as pl
from jax.experimental.pallas import tpu as pltpu
from jax.sharding import PartitionSpec as P

HEAD_DIM = 128
NORM_EPS = 1e-05
LANES = 128
SLOT = 36
MASK_AT = 3 * SLOT
MIB = 1 << 20
BY_ROW = (((1,), (1,)), ((), ()))


def split_terms(value):
    high = value.astype(jnp.bfloat16).astype(jnp.float32)
    rest = value - high
    middle = rest.astype(jnp.bfloat16).astype(jnp.float32)
    return high, middle, rest - middle


def attention_kernel(
    len_ref,
    q_hbm,
    new_hbm,
    kv_hbm,
    res_hbm,
    routes_hbm,
    router_hbm,
    gain_hbm,
    out_ref,
    q_ref,
    new_ref,
    kv,
    res_ref,
    routes_ref,
    router_ref,
    gain_ref,
    scores,
    sems,
    *,
    chunks,
):
    slots = kv_hbm.shape[1]
    part = slots // chunks
    sources = [q_hbm, new_hbm] + [kv_hbm.at[0, pl.ds(c * part, part)] for c in range(chunks)]
    targets = [q_ref, new_ref] + [kv.at[pl.ds(c * part, part)] for c in range(chunks)]
    sources += [res_hbm, routes_hbm, router_hbm, gain_hbm]
    targets += [res_ref, routes_ref, router_ref, gain_ref]
    copies = [pltpu.make_async_copy(a, b, sems.at[i]) for i, (a, b) in enumerate(zip(sources, targets))]
    for copy in copies:
        copy.start()
    tokens, columns = q_ref.shape
    key_heads = new_ref.shape[1] // (2 * HEAD_DIM)
    grouped = columns // HEAD_DIM // key_heads
    rows = grouped * tokens
    scale = HEAD_DIM ** (-0.5)
    copies[0].wait()
    copies[1].wait()
    queries, selves = [], []
    for h in range(key_heads):
        first = h * grouped * HEAD_DIM
        q = jnp.concatenate(
            [
                q_ref[:, first + j * HEAD_DIM : first + (j + 1) * HEAD_DIM].astype(jnp.float32)
                for j in range(grouped)
            ],
            axis=0,
        )
        own_key = new_ref[:, 2 * h * HEAD_DIM : (2 * h + 1) * HEAD_DIM].astype(jnp.float32)
        own_key = jnp.concatenate([own_key] * grouped, axis=0)
        selves.append(jnp.sum(q * own_key, axis=1, keepdims=True) * scale)
        queries.append(q.astype(jnp.bfloat16))
    live = len_ref[0]
    for c in range(chunks):
        copies[2 + c].wait()
        for h in range(key_heads):
            keys = kv[c * part : (c + 1) * part, 2 * h * HEAD_DIM : (2 * h + 1) * HEAD_DIM]
            s = lax.dot_general(queries[h], keys, BY_ROW, preferred_element_type=jnp.float32)
            at = lax.broadcasted_iota(jnp.int32, (rows, part), 1) + c * part
            scores[h, :, c * part : (c + 1) * part] = jnp.where(at < live, s * scale, -jnp.inf)
    for copy in copies[2 + chunks :]:
        copy.wait()

    experts = router_ref.shape[0]
    routes = routes_ref[...]
    expert_at = lax.broadcasted_iota(jnp.int32, (LANES, tokens), 0) - MASK_AT
    named = jnp.zeros((LANES, tokens), jnp.float32)
    for k in range(routes.shape[0]):
        named = jnp.where(expert_at == routes[k : k + 1, :], 1.0, named)
    side = named.T

    streams = []
    for h in range(key_heads):
        s = scores[h]
        top = jnp.maximum(jnp.max(s, axis=1, keepdims=True), selves[h])
        weights = jnp.exp(s - top).astype(jnp.bfloat16)
        own = jnp.exp(selves[h] - top).astype(jnp.bfloat16).astype(jnp.float32)
        total = jnp.sum(weights.astype(jnp.float32), axis=1, keepdims=True) + own
        value_at = (2 * h + 1) * HEAD_DIM
        mixed = jnp.dot(weights, kv[:, value_at : value_at + HEAD_DIM], preferred_element_type=jnp.float32)
        own_value = new_ref[:, value_at : value_at + HEAD_DIM].astype(jnp.float32)
        mixed = (mixed + own * jnp.concatenate([own_value] * grouped, axis=0)) / total
        for j in range(grouped):
            at = (h * grouped + j) * HEAD_DIM
            got = res_ref[:, at : at + HEAD_DIM].astype(jnp.float32) + mixed[j * tokens : (j + 1) * tokens]
            got = got.astype(jnp.bfloat16)
            out_ref[:, at : at + HEAD_DIM] = got
            streams.append(got.astype(jnp.float32))

    lane = lax.broadcasted_iota(jnp.int32, (tokens, LANES), 1)
    sums = jnp.zeros((tokens, LANES), jnp.float32)

    def put(sums, at, pieces):
        total = pieces[0]
        for piece in pieces[1:]:
            total = total + piece
        return jnp.where(lane == at, jnp.sum(total, axis=1, keepdims=True), sums)

    blocks = range(len(streams))
    sums = put(sums, experts, streams)
    sums = put(sums, experts + 1, [x * x for x in streams])
    gains = [gain_ref[:, b * HEAD_DIM : (b + 1) * HEAD_DIM].astype(jnp.float32) for b in blocks]
    scaled = [x * g for x, g in zip(streams, gains)]
    for e in range(experts):
        weights = [router_ref[e : e + 1, b * HEAD_DIM : (b + 1) * HEAD_DIM].astype(jnp.float32) for b in blocks]
        sums = put(sums, e, [x * w for x, w in zip(scaled, weights)])
        plain = [jnp.broadcast_to(g * w, (tokens, HEAD_DIM)) for g, w in zip(gains, weights)]
        sums = put(sums, experts + 2 + e, plain)
    for i, term in enumerate(split_terms(sums)):
        side = side + (pltpu.roll(term, i * SLOT, 1) if i else term)
    out_ref[:, columns : columns + LANES] = side.astype(out_ref.dtype)
    gain_rows = jnp.concatenate(
        gains + [jnp.zeros((1, LANES), jnp.float32)] * (tokens - len(gains)), axis=0
    )
    out_ref[:, columns + LANES :] = gain_rows.astype(out_ref.dtype)


def attend(cache_len, queries, new_kv, kv_cache, residual, routes, router, norm_gain):
    tokens, columns = queries.shape
    slots, width = kv_cache.shape[1:]
    key_heads = new_kv.shape[1] // (2 * HEAD_DIM)
    rows = columns // HEAD_DIM // key_heads * tokens
    chunks = 4
    operands = [queries, new_kv, kv_cache, residual, routes.T, router, norm_gain.reshape(1, -1)]
    operands = [pltpu.with_memory_space_constraint(x, pltpu.HBM) for x in operands]
    kept = [pltpu.VMEM(x.shape, x.dtype) for x in operands]
    kept[2] = pltpu.VMEM((slots, width), kv_cache.dtype)
    return pl.pallas_call(
        functools.partial(attention_kernel, chunks=chunks),
        out_shape=jax.ShapeDtypeStruct((tokens, columns + 2 * LANES), jnp.bfloat16),
        in_specs=[pl.BlockSpec(memory_space=pltpu.SMEM)]
        + [pl.BlockSpec(memory_space=pl.ANY)] * len(operands),
        out_specs=pl.BlockSpec(memory_space=pltpu.VMEM),
        scratch_shapes=kept
        + [
            pltpu.VMEM((key_heads, rows, slots), jnp.float32),
            pltpu.SemaphoreType.DMA((chunks + len(operands) - 1,)),
        ],
        compiler_params=pltpu.CompilerParams(vmem_limit_bytes=8 * MIB),
        cost_estimate=pl.CostEstimate(
            flops=4 * rows * slots * HEAD_DIM * key_heads,
            bytes_accessed=slots * width * 2,
            transcendentals=rows * slots * key_heads,
        ),
        name="attention",
    )(cache_len, *operands)


def norm_kernel(place_ref, near_ref, far_ref, out_ref, *, masks, experts):
    tokens = near_ref.shape[1]
    tensors = len(masks)
    block = near_ref.shape[2] - 2 * LANES
    model = tensors * block
    pieces = [ref.at[i] for ref in (near_ref, far_ref) for i in range(tensors // 2)]
    total = jnp.zeros((tokens, LANES), jnp.float32)
    for piece in pieces:
        total = total + piece[:, block : block + LANES].astype(jnp.float32)
    sums = total + pltpu.roll(total, LANES - SLOT, 1) + pltpu.roll(total, LANES - 2 * SLOT, 1)
    mean = sums[:, experts : experts + 1] / model
    variance = sums[:, experts + 1 : experts + 2] / model - mean * mean
    inv = lax.rsqrt(variance + NORM_EPS)
    plain = pltpu.roll(sums, LANES - experts - 2, 1)
    logits = (sums - mean * plain) * inv
    lane = lax.broadcasted_iota(jnp.int32, (tokens, LANES), 1)
    named = (pltpu.roll(total, LANES - MASK_AT, 1) > 0) & (lane < experts)
    raised = jnp.where(named, jnp.exp(logits), 0.0)
    share = raised / jnp.sum(raised, axis=1, keepdims=True)
    high = share.astype(jnp.bfloat16).astype(jnp.float32)
    side = high + pltpu.roll(share - high, experts, 1)
    out_ref[:, model:] = side.astype(out_ref.dtype)
    for piece, mask in zip(pieces, masks):
        gain = piece[:, block + LANES :].astype(jnp.float32)
        gain = jnp.concatenate([gain[j : j + 1, :] for j in range(block // LANES)], axis=1)
        x = (piece[:, :block].astype(jnp.float32) - mean) * inv * gain
        at = pl.multiple_of(lax.bitwise_xor(place_ref[0], mask) * block, block)
        out_ref[:, pl.ds(at, block)] = x.astype(out_ref.dtype)


def norm_rows(place, near, far, masks, experts):
    tokens, wide = near.shape[1:]
    model = (wide - 2 * LANES) * len(masks)
    vmem = pl.BlockSpec(memory_space=pltpu.VMEM)
    return pl.pallas_call(
        functools.partial(norm_kernel, masks=masks, experts=experts),
        out_shape=jax.ShapeDtypeStruct((tokens, model + LANES), jnp.bfloat16),
        in_specs=[pl.BlockSpec(memory_space=pltpu.SMEM), vmem, vmem],
        out_specs=vmem,
        compiler_params=pltpu.CompilerParams(vmem_limit_bytes=4 * MIB),
        name="norm",
    )(place, near, far)


def expert_kernel(
    place_ref,
    near_ref,
    far_ref,
    gate_hbm,
    up_hbm,
    down_hbm,
    near_out,
    far_out,
    gate,
    up,
    down,
    normed,
    hidden,
    sems,
    *,
    masks,
    experts,
    ahead,
):
    place, expert = place_ref[0], place_ref[1]
    half = near_ref.shape[0]
    units, model = gate.shape
    tensors = len(masks)
    block = model // tensors
    step = 256
    tiles = [(at, min(step, units - at)) for at in range(0, units, step)]
    copies = []
    for at, size in tiles:
        for source, target in ((gate_hbm, gate), (up_hbm, up)):
            copies.append((source.at[0, pl.ds(at, size)], target.at[pl.ds(at, size)]))
    for c in range(tensors):
        columns = pl.ds(c * block, block)
        copies.append((down_hbm.at[0, :, columns], down.at[:, columns]))
    copies = [pltpu.make_async_copy(a, b, sems.at[i]) for i, (a, b) in enumerate(copies)]
    for copy in copies[:ahead]:
        copy.start()

    def take(i):
        copies[i].wait()
        if i + ahead < len(copies):
            copies[i + ahead].start()

    normed[:half, :] = near_ref[:, :model]
    normed[half:, :] = far_ref[:, :model]
    shares = []
    for ref in (near_ref, far_ref):
        side = ref[:, model:].astype(jnp.float32)
        lane = lax.broadcasted_iota(jnp.int32, side.shape, 1)
        mine = (lane == expert) | (lane == expert + experts)
        shares.append(jnp.sum(jnp.where(mine, side, 0.0), axis=1, keepdims=True))

    for i, (at, size) in enumerate(tiles):
        x = normed[...]
        take(2 * i)
        a = lax.dot_general(x, gate[at : at + size, :], BY_ROW, preferred_element_type=jnp.float32)
        take(2 * i + 1)
        b = lax.dot_general(x, up[at : at + size, :], BY_ROW, preferred_element_type=jnp.float32)
        hidden[:, at : at + size] = (a / (1.0 + jnp.exp(-a)) * b).astype(jnp.bfloat16)

    for c in range(tensors):
        take(2 * len(tiles) + c)
        part = jnp.dot(hidden[...], down[:, c * block : (c + 1) * block], preferred_element_type=jnp.float32)
        slot = jnp.int32(0)
        for r, mask in enumerate(masks):
            slot = jnp.where(lax.bitwise_xor(place, mask) == c, r, slot)
        to = pl.ds(pl.multiple_of(slot * block, block), block)
        near_out[:, to] = (part[:half] * shares[0]).astype(near_out.dtype)
        far_out[:, to] = (part[half:] * shares[1]).astype(far_out.dtype)


def run_expert(place, near, far, gate_w, up_w, down_w, masks, experts):
    half = near.shape[0]
    units, model = gate_w.shape[1:]
    rows = 2 * half
    vmem = pl.BlockSpec(memory_space=pltpu.VMEM)
    shape = jax.ShapeDtypeStruct((half, model), jnp.bfloat16)
    weights = [pltpu.with_memory_space_constraint(w, pltpu.HBM) for w in (gate_w, up_w, down_w)]
    count = 2 * pl.cdiv(units, 256) + len(masks)
    return pl.pallas_call(
        functools.partial(expert_kernel, masks=masks, experts=experts, ahead=4),
        out_shape=(shape, shape),
        in_specs=[pl.BlockSpec(memory_space=pltpu.SMEM), vmem, vmem]
        + [pl.BlockSpec(memory_space=pl.ANY)] * 3,
        out_specs=(vmem, vmem),
        scratch_shapes=[
            pltpu.VMEM((units, model), gate_w.dtype),
            pltpu.VMEM((units, model), gate_w.dtype),
            pltpu.VMEM((units, model), gate_w.dtype),
            pltpu.VMEM((rows, model), jnp.bfloat16),
            pltpu.VMEM((rows, units), jnp.bfloat16),
            pltpu.SemaphoreType.DMA((count,)),
        ],
        compiler_params=pltpu.CompilerParams(vmem_limit_bytes=42 * MIB),
        cost_estimate=pl.CostEstimate(
            flops=6 * rows * units * model, bytes_accessed=6 * units * model, transcendentals=rows * units
        ),
        name="experts",
    )(place, near, far, *weights)


def doubling(size):
    step = size // 2
    while step:
        yield step
        step //= 2


def exchange(x, axis, pairs):
    return lax.ppermute(x, axis, pairs)


def add(*terms):
    return sum(t.astype(jnp.float32) for t in terms)


def per_device(
    queries, new_kv, kv_cache, cache_len, residual, norm_gain, router, routes, gate_w, up_w, down_w
):
    sections, groups, tensors = (lax.axis_size(a) for a in ("section", "group", "tensor"))
    experts, block = router.shape
    tokens = queries.shape[0]
    across = [(i, (i + 1) % sections) for i in range(sections)]
    tensor_steps = list(doubling(tensors))
    tensor_pairs = [[(i, i ^ step) for i in range(tensors)] for step in tensor_steps]
    masks = [0]
    for step in tensor_steps:
        masks = masks + [m ^ step for m in masks]
    group_steps = list(doubling(groups))
    orders = [group_steps if s % 2 == 0 else group_steps[::-1] for s in range(sections)]
    group_pairs = [
        [(s * groups + g, s * groups + (g ^ orders[s][i])) for s in range(sections) for g in range(groups)]
        for i in range(len(group_steps))
    ]
    place = lax.axis_index("tensor")
    where = jnp.stack([place, lax.axis_index("section") * tensors + place]).astype(jnp.int32)

    fresh = attend(cache_len, queries, new_kv, kv_cache, residual, routes, router, norm_gain)
    rows = fresh[None]
    for pairs in tensor_pairs[:-1]:
        rows = jnp.concatenate([rows, exchange(rows, "tensor", pairs)], axis=0)
    near = norm_rows(where, rows, exchange(rows, "tensor", tensor_pairs[-1]), masks, experts)
    for pairs in group_pairs:
        near = jnp.concatenate([near, exchange(near, ("section", "group"), pairs)], axis=0)
    far = exchange(near, "section", across)

    mine, theirs = run_expert(where, near, far, gate_w, up_w, down_w, masks, experts)
    both = add(mine, exchange(theirs, "section", across)).astype(jnp.bfloat16)
    for pairs in group_pairs[::-1]:
        half = both.shape[0] // 2
        both = add(both[:half], exchange(both[half:], ("section", "group"), pairs)).astype(jnp.bfloat16)
    for pairs in tensor_pairs[:0:-1]:
        half = both.shape[1] // 2
        both = add(both[:, :half], exchange(both[:, half:], "tensor", pairs)).astype(jnp.bfloat16)
    last = exchange(both[:, block:], "tensor", tensor_pairs[0])
    return add(fresh[:, :block], both[:, :block], last).astype(jnp.bfloat16)


def solution(mesh):
    rows = P(("section", "group"), "tensor")
    weights = P(("section", "tensor"), "group", None)
    in_specs = (
        rows,
        rows,
        P(("section", "group"), None, "tensor"),
        P(("section", "group")),
        rows,
        P("tensor"),
        P(None, "tensor"),
        P(("section", "group"), None),
        weights,
        weights,
        weights,
    )
    return jax.shard_map(per_device, mesh=mesh, in_specs=in_specs, out_specs=rows, check_vma=False)
```

```python
import functools

import jax
import jax.numpy as jnp
from jax import lax
from jax.experimental import pallas as pl
from jax.experimental.pallas import tpu as pltpu
from jax.sharding import PartitionSpec as P

HEAD_DIM = 128
NORM_EPS = 1e-05
LANES = 128
SLOT = 36
MASK_AT = 3 * SLOT
MIB = 1 << 20
BY_ROW = (((1,), (1,)), ((), ()))


def split_terms(value):
    high = value.astype(jnp.bfloat16).astype(jnp.float32)
    rest = value - high
    middle = rest.astype(jnp.bfloat16).astype(jnp.float32)
    return high, middle, rest - middle


def attention_kernel(
    len_ref,
    q_hbm,
    new_hbm,
    kv_hbm,
    res_hbm,
    routes_hbm,
    router_hbm,
    gain_hbm,
    out_ref,
    q_ref,
    new_ref,
    kv,
    res_ref,
    routes_ref,
    router_ref,
    gain_ref,
    scores,
    sems,
    *,
    chunks,
):
    slots = kv_hbm.shape[1]
    part = slots // chunks
    sources = [q_hbm, new_hbm] + [kv_hbm.at[0, pl.ds(c * part, part)] for c in range(chunks)]
    targets = [q_ref, new_ref] + [kv.at[pl.ds(c * part, part)] for c in range(chunks)]
    sources += [res_hbm, routes_hbm, router_hbm, gain_hbm]
    targets += [res_ref, routes_ref, router_ref, gain_ref]
    copies = [pltpu.make_async_copy(a, b, sems.at[i]) for i, (a, b) in enumerate(zip(sources, targets))]
    for copy in copies:
        copy.start()
    tokens, columns = q_ref.shape
    key_heads = new_ref.shape[1] // (2 * HEAD_DIM)
    grouped = columns // HEAD_DIM // key_heads
    rows = grouped * tokens
    scale = HEAD_DIM ** (-0.5)
    copies[0].wait()
    copies[1].wait()
    queries, selves = [], []
    for h in range(key_heads):
        first = h * grouped * HEAD_DIM
        q = jnp.concatenate(
            [
                q_ref[:, first + j * HEAD_DIM : first + (j + 1) * HEAD_DIM].astype(jnp.float32)
                for j in range(grouped)
            ],
            axis=0,
        )
        own_key = new_ref[:, 2 * h * HEAD_DIM : (2 * h + 1) * HEAD_DIM].astype(jnp.float32)
        own_key = jnp.concatenate([own_key] * grouped, axis=0)
        selves.append(jnp.sum(q * own_key, axis=1, keepdims=True) * scale)
        queries.append(q.astype(jnp.bfloat16))
    live = len_ref[0]
    for c in range(chunks):
        copies[2 + c].wait()
        for h in range(key_heads):
            keys = kv[c * part : (c + 1) * part, 2 * h * HEAD_DIM : (2 * h + 1) * HEAD_DIM]
            s = lax.dot_general(queries[h], keys, BY_ROW, preferred_element_type=jnp.float32)
            at = lax.broadcasted_iota(jnp.int32, (rows, part), 1) + c * part
            scores[h, :, c * part : (c + 1) * part] = jnp.where(at < live, s * scale, -jnp.inf)
    for copy in copies[2 + chunks :]:
        copy.wait()

    experts = router_ref.shape[0]
    routes = routes_ref[...]
    expert_at = lax.broadcasted_iota(jnp.int32, (LANES, tokens), 0) - MASK_AT
    named = jnp.zeros((LANES, tokens), jnp.float32)
    for k in range(routes.shape[0]):
        named = jnp.where(expert_at == routes[k : k + 1, :], 1.0, named)
    side = named.T

    streams = []
    for h in range(key_heads):
        s = scores[h]
        top = jnp.maximum(jnp.max(s, axis=1, keepdims=True), selves[h])
        weights = jnp.exp(s - top).astype(jnp.bfloat16)
        own = jnp.exp(selves[h] - top).astype(jnp.bfloat16).astype(jnp.float32)
        total = jnp.sum(weights.astype(jnp.float32), axis=1, keepdims=True) + own
        value_at = (2 * h + 1) * HEAD_DIM
        mixed = jnp.dot(weights, kv[:, value_at : value_at + HEAD_DIM], preferred_element_type=jnp.float32)
        own_value = new_ref[:, value_at : value_at + HEAD_DIM].astype(jnp.float32)
        mixed = (mixed + own * jnp.concatenate([own_value] * grouped, axis=0)) / total
        for j in range(grouped):
            at = (h * grouped + j) * HEAD_DIM
            got = res_ref[:, at : at + HEAD_DIM].astype(jnp.float32) + mixed[j * tokens : (j + 1) * tokens]
            got = got.astype(jnp.bfloat16)
            out_ref[:, at : at + HEAD_DIM] = got
            streams.append(got.astype(jnp.float32))

    lane = lax.broadcasted_iota(jnp.int32, (tokens, LANES), 1)
    sums = jnp.zeros((tokens, LANES), jnp.float32)

    def put(sums, at, pieces):
        total = pieces[0]
        for piece in pieces[1:]:
            total = total + piece
        return jnp.where(lane == at, jnp.sum(total, axis=1, keepdims=True), sums)

    blocks = range(len(streams))
    sums = put(sums, experts, streams)
    sums = put(sums, experts + 1, [x * x for x in streams])
    gains = [gain_ref[:, b * HEAD_DIM : (b + 1) * HEAD_DIM].astype(jnp.float32) for b in blocks]
    scaled = [x * g for x, g in zip(streams, gains)]
    for e in range(experts):
        weights = [router_ref[e : e + 1, b * HEAD_DIM : (b + 1) * HEAD_DIM].astype(jnp.float32) for b in blocks]
        sums = put(sums, e, [x * w for x, w in zip(scaled, weights)])
        plain = [jnp.broadcast_to(g * w, (tokens, HEAD_DIM)) for g, w in zip(gains, weights)]
        sums = put(sums, experts + 2 + e, plain)
    for i, term in enumerate(split_terms(sums)):
        side = side + (pltpu.roll(term, i * SLOT, 1) if i else term)
    out_ref[:, columns : columns + LANES] = side.astype(out_ref.dtype)
    gain_rows = jnp.concatenate(
        gains + [jnp.zeros((1, LANES), jnp.float32)] * (tokens - len(gains)), axis=0
    )
    out_ref[:, columns + LANES :] = gain_rows.astype(out_ref.dtype)


def attend(cache_len, queries, new_kv, kv_cache, residual, routes, router, norm_gain):
    tokens, columns = queries.shape
    slots, width = kv_cache.shape[1:]
    key_heads = new_kv.shape[1] // (2 * HEAD_DIM)
    rows = columns // HEAD_DIM // key_heads * tokens
    chunks = 4
    operands = [queries, new_kv, kv_cache, residual, routes.T, router, norm_gain.reshape(1, -1)]
    operands = [pltpu.with_memory_space_constraint(x, pltpu.HBM) for x in operands]
    kept = [pltpu.VMEM(x.shape, x.dtype) for x in operands]
    kept[2] = pltpu.VMEM((slots, width), kv_cache.dtype)
    return pl.pallas_call(
        functools.partial(attention_kernel, chunks=chunks),
        out_shape=jax.ShapeDtypeStruct((tokens, columns + 2 * LANES), jnp.bfloat16),
        in_specs=[pl.BlockSpec(memory_space=pltpu.SMEM)]
        + [pl.BlockSpec(memory_space=pl.ANY)] * len(operands),
        out_specs=pl.BlockSpec(memory_space=pltpu.VMEM),
        scratch_shapes=kept
        + [
            pltpu.VMEM((key_heads, rows, slots), jnp.float32),
            pltpu.SemaphoreType.DMA((chunks + len(operands) - 1,)),
        ],
        compiler_params=pltpu.CompilerParams(vmem_limit_bytes=8 * MIB),
        cost_estimate=pl.CostEstimate(
            flops=4 * rows * slots * HEAD_DIM * key_heads,
            bytes_accessed=slots * width * 2,
            transcendentals=rows * slots * key_heads,
        ),
        name="attention",
    )(cache_len, *operands)


def norm_kernel(place_ref, *refs, experts):
    pieces, out_ref = refs[:-1], refs[-1]
    tokens, wide = pieces[0].shape
    block = wide - 2 * LANES
    model = len(pieces) * block
    total = jnp.zeros((tokens, LANES), jnp.float32)
    for piece in pieces:
        total = total + piece[:, block : block + LANES].astype(jnp.float32)
    sums = total + pltpu.roll(total, LANES - SLOT, 1) + pltpu.roll(total, LANES - 2 * SLOT, 1)
    mean = sums[:, experts : experts + 1] / model
    variance = sums[:, experts + 1 : experts + 2] / model - mean * mean
    inv = lax.rsqrt(variance + NORM_EPS)
    plain = pltpu.roll(sums, LANES - experts - 2, 1)
    logits = (sums - mean * plain) * inv
    lane = lax.broadcasted_iota(jnp.int32, (tokens, LANES), 1)
    named = (pltpu.roll(total, LANES - MASK_AT, 1) > 0) & (lane < experts)
    raised = jnp.where(named, jnp.exp(logits), 0.0)
    share = raised / jnp.sum(raised, axis=1, keepdims=True)
    high = share.astype(jnp.bfloat16).astype(jnp.float32)
    side = high + pltpu.roll(share - high, experts, 1)
    out_ref[:, model:] = side.astype(out_ref.dtype)
    for mask, piece in enumerate(pieces):
        gain = piece[:, block + LANES :].astype(jnp.float32)
        gain = jnp.concatenate([gain[j : j + 1, :] for j in range(block // LANES)], axis=1)
        x = (piece[:, :block].astype(jnp.float32) - mean) * inv * gain
        at = pl.multiple_of(lax.bitwise_xor(place_ref[0], mask) * block, block)
        out_ref[:, pl.ds(at, block)] = x.astype(out_ref.dtype)


def norm_rows(place, blocks, experts):
    tokens, wide = blocks[0].shape
    model = (wide - 2 * LANES) * len(blocks)
    vmem = pl.BlockSpec(memory_space=pltpu.VMEM)
    return pl.pallas_call(
        functools.partial(norm_kernel, experts=experts),
        out_shape=jax.ShapeDtypeStruct((tokens, model + LANES), jnp.bfloat16),
        in_specs=[pl.BlockSpec(memory_space=pltpu.SMEM)] + [vmem] * len(blocks),
        out_specs=vmem,
        compiler_params=pltpu.CompilerParams(vmem_limit_bytes=4 * MIB),
        name="norm",
    )(place, *blocks)


def run_expert(place, near, far, gate_w, up_w, down_w, experts):
    model = gate_w.shape[2]
    rows = jnp.concatenate([near, far], axis=0)
    x, side = rows[:, :model], rows[:, model:].astype(jnp.float32)
    lane = jnp.arange(side.shape[1])[None, :]
    mine = (lane == place[1]) | (lane == place[1] + experts)
    share = jnp.sum(jnp.where(mine, side, 0.0), axis=1, keepdims=True)
    gate = lax.dot_general(x, gate_w[0], BY_ROW, preferred_element_type=jnp.float32)
    up = lax.dot_general(x, up_w[0], BY_ROW, preferred_element_type=jnp.float32)
    hidden = (jax.nn.silu(gate) * up).astype(jnp.bfloat16)
    out = jnp.dot(hidden, down_w[0], preferred_element_type=jnp.float32)
    return (out * share).astype(jnp.bfloat16)


def send(x, axis, mask):
    return lax.ppermute(x, axis, [(i, i ^ mask) for i in range(lax.axis_size(axis))])


def add(*terms):
    return sum(t.astype(jnp.float32) for t in terms)


def per_device(
    queries, new_kv, kv_cache, cache_len, residual, norm_gain, router, routes, gate_w, up_w, down_w
):
    sections, groups, tensors = (lax.axis_size(a) for a in ("section", "group", "tensor"))
    experts, block = router.shape
    tokens = queries.shape[0]
    place = lax.axis_index("tensor")
    where = jnp.stack([place, lax.axis_index("section") * tensors + place]).astype(jnp.int32)

    fresh = attend(cache_len, queries, new_kv, kv_cache, residual, routes, router, norm_gain)
    blocks = [fresh] + [send(fresh, "tensor", m) for m in range(1, tensors)]
    rows = norm_rows(where, blocks, experts)
    near = jnp.concatenate([rows] + [send(rows, "group", m) for m in range(1, groups)], axis=0)
    far = send(near, "section", 1)

    out = run_expert(where, near, far, gate_w, up_w, down_w, experts)
    half = out.shape[0] // 2
    both = add(out[:half], send(out[half:], "section", 1)).astype(jnp.bfloat16)
    both = both.reshape(groups, tokens, -1)
    got = add(both[0], *[send(both[m], "group", m) for m in range(1, groups)]).astype(jnp.bfloat16)
    parts = [lax.dynamic_slice_in_dim(got, (place ^ m) * block, block, axis=1) for m in range(tensors)]
    mixed = add(fresh[:, :block], parts[0], *[send(parts[m], "tensor", m) for m in range(1, tensors)])
    return mixed.astype(jnp.bfloat16)


def solution(mesh):
    rows = P(("section", "group"), "tensor")
    weights = P(("section", "tensor"), "group", None)
    in_specs = (
        rows,
        rows,
        P(("section", "group"), None, "tensor"),
        P(("section", "group")),
        rows,
        P("tensor"),
        P(None, "tensor"),
        P(("section", "group"), None),
        weights,
        weights,
        weights,
    )
    return jax.shard_map(per_device, mesh=mesh, in_specs=in_specs, out_specs=rows, check_vma=False)
```

```python
import functools

import jax
import jax.numpy as jnp
from jax import lax
from jax.experimental import pallas as pl
from jax.experimental.pallas import tpu as pltpu
from jax.sharding import PartitionSpec as P

HEAD_DIM = 128
NORM_EPS = 1e-05
LANES = 128
SLOT = 36
MASK_AT = 3 * SLOT
MIB = 1 << 20
CHUNKS = 6
BY_ROW = (((1,), (1,)), ((), ()))


def split_terms(value):
    high = value.astype(jnp.bfloat16).astype(jnp.float32)
    rest = value - high
    middle = rest.astype(jnp.bfloat16).astype(jnp.float32)
    return high, middle, rest - middle


def attention_kernel(
    len_ref,
    q_hbm,
    new_hbm,
    kv_hbm,
    res_hbm,
    routes_hbm,
    router_hbm,
    gain_hbm,
    out_ref,
    q_ref,
    new_ref,
    kv,
    res_ref,
    routes_ref,
    router_ref,
    gain_ref,
    scores,
    sems,
    *,
    chunks,
):
    slots = kv_hbm.shape[1]
    part = slots // chunks
    sources = [q_hbm, new_hbm] + [kv_hbm.at[0, pl.ds(c * part, part)] for c in range(chunks)]
    targets = [q_ref, new_ref] + [kv.at[pl.ds(c * part, part)] for c in range(chunks)]
    sources += [res_hbm, routes_hbm, router_hbm, gain_hbm]
    targets += [res_ref, routes_ref, router_ref, gain_ref]
    copies = [pltpu.make_async_copy(a, b, sems.at[i]) for i, (a, b) in enumerate(zip(sources, targets))]
    for copy in copies:
        copy.start()
    tokens, columns = q_ref.shape
    key_heads = new_ref.shape[1] // (2 * HEAD_DIM)
    grouped = columns // HEAD_DIM // key_heads
    rows = grouped * tokens
    scale = HEAD_DIM ** (-0.5)
    copies[0].wait()
    copies[1].wait()
    queries, selves = [], []
    for h in range(key_heads):
        first = h * grouped * HEAD_DIM
        q = jnp.concatenate(
            [
                q_ref[:, first + j * HEAD_DIM : first + (j + 1) * HEAD_DIM].astype(jnp.float32)
                for j in range(grouped)
            ],
            axis=0,
        )
        own_key = new_ref[:, 2 * h * HEAD_DIM : (2 * h + 1) * HEAD_DIM].astype(jnp.float32)
        own_key = jnp.concatenate([own_key] * grouped, axis=0)
        selves.append(jnp.sum(q * own_key, axis=1, keepdims=True) * scale)
        queries.append(q.astype(jnp.bfloat16))
    live = len_ref[0]
    for c in range(chunks):
        copies[2 + c].wait()
        for h in range(key_heads):
            keys = kv[c * part : (c + 1) * part, 2 * h * HEAD_DIM : (2 * h + 1) * HEAD_DIM]
            s = lax.dot_general(queries[h], keys, BY_ROW, preferred_element_type=jnp.float32)
            at = lax.broadcasted_iota(jnp.int32, (rows, part), 1) + c * part
            scores[h, :, c * part : (c + 1) * part] = jnp.where(at < live, s * scale, -jnp.inf)
    for copy in copies[2 + chunks :]:
        copy.wait()

    experts = router_ref.shape[0]
    routes = routes_ref[...]
    expert_at = lax.broadcasted_iota(jnp.int32, (LANES, tokens), 0) - MASK_AT
    named = jnp.zeros((LANES, tokens), jnp.float32)
    for k in range(routes.shape[0]):
        named = jnp.where(expert_at == routes[k : k + 1, :], 1.0, named)
    side = named.T

    streams = []
    for h in range(key_heads):
        s = scores[h]
        top = jnp.maximum(jnp.max(s, axis=1, keepdims=True), selves[h])
        weights = jnp.exp(s - top).astype(jnp.bfloat16)
        own = jnp.exp(selves[h] - top).astype(jnp.bfloat16).astype(jnp.float32)
        total = jnp.sum(weights.astype(jnp.float32), axis=1, keepdims=True) + own
        value_at = (2 * h + 1) * HEAD_DIM
        mixed = jnp.dot(weights, kv[:, value_at : value_at + HEAD_DIM], preferred_element_type=jnp.float32)
        own_value = new_ref[:, value_at : value_at + HEAD_DIM].astype(jnp.float32)
        mixed = (mixed + own * jnp.concatenate([own_value] * grouped, axis=0)) / total
        for j in range(grouped):
            at = (h * grouped + j) * HEAD_DIM
            got = res_ref[:, at : at + HEAD_DIM].astype(jnp.float32) + mixed[j * tokens : (j + 1) * tokens]
            got = got.astype(jnp.bfloat16)
            out_ref[:, at : at + HEAD_DIM] = got
            streams.append(got.astype(jnp.float32))

    lane = lax.broadcasted_iota(jnp.int32, (tokens, LANES), 1)
    sums = jnp.zeros((tokens, LANES), jnp.float32)

    def put(sums, at, pieces):
        total = pieces[0]
        for piece in pieces[1:]:
            total = total + piece
        return jnp.where(lane == at, jnp.sum(total, axis=1, keepdims=True), sums)

    blocks = range(len(streams))
    sums = put(sums, experts, streams)
    sums = put(sums, experts + 1, [x * x for x in streams])
    gain = gain_ref[...].astype(jnp.float32).reshape(1, -1)
    gains = [gain[:, b * HEAD_DIM : (b + 1) * HEAD_DIM] for b in blocks]
    scaled = [x * g for x, g in zip(streams, gains)]
    for e in range(experts):
        weights = [router_ref[e : e + 1, b * HEAD_DIM : (b + 1) * HEAD_DIM].astype(jnp.float32) for b in blocks]
        sums = put(sums, e, [x * w for x, w in zip(scaled, weights)])
        plain = [jnp.broadcast_to(g * w, (tokens, HEAD_DIM)) for g, w in zip(gains, weights)]
        sums = put(sums, experts + 2 + e, plain)
    for i, term in enumerate(split_terms(sums)):
        side = side + (pltpu.roll(term, i * SLOT, 1) if i else term)
    out_ref[:, columns : columns + LANES] = side.astype(out_ref.dtype)
    gain_rows = jnp.concatenate(
        gains + [jnp.zeros((1, LANES), jnp.float32)] * (tokens - len(gains)), axis=0
    )
    out_ref[:, columns + LANES :] = gain_rows.astype(out_ref.dtype)


def attend(cache_len, queries, new_kv, kv_cache, residual, routes, router, norm_gain):
    tokens, columns = queries.shape
    slots, width = kv_cache.shape[1:]
    key_heads = new_kv.shape[1] // (2 * HEAD_DIM)
    rows = columns // HEAD_DIM // key_heads * tokens
    chunks = 4
    operands = [queries, new_kv, kv_cache, residual, routes.T, router, norm_gain]
    operands = [pltpu.with_memory_space_constraint(x, pltpu.HBM) for x in operands]
    kept = [pltpu.VMEM(x.shape, x.dtype) for x in operands]
    kept[2] = pltpu.VMEM((slots, width), kv_cache.dtype)
    return pl.pallas_call(
        functools.partial(attention_kernel, chunks=chunks),
        out_shape=jax.ShapeDtypeStruct((tokens, columns + 2 * LANES), jnp.bfloat16),
        in_specs=[pl.BlockSpec(memory_space=pltpu.SMEM)]
        + [pl.BlockSpec(memory_space=pl.ANY)] * len(operands),
        out_specs=pl.BlockSpec(memory_space=pltpu.VMEM),
        scratch_shapes=kept
        + [
            pltpu.VMEM((key_heads, rows, slots), jnp.float32),
            pltpu.SemaphoreType.DMA((chunks + len(operands) - 1,)),
        ],
        compiler_params=pltpu.CompilerParams(vmem_limit_bytes=8 * MIB),
        cost_estimate=pl.CostEstimate(
            flops=4 * rows * slots * HEAD_DIM * key_heads,
            bytes_accessed=slots * width * 2,
            transcendentals=rows * slots * key_heads,
        ),
        name="attention",
    )(cache_len, *operands)


def norm_kernel(place_ref, _, *refs, experts):
    pieces, out_ref = refs[:-1], refs[-1]
    tokens, wide = pieces[0].shape
    block = wide - 2 * LANES
    model = len(pieces) * block
    total = jnp.zeros((tokens, LANES), jnp.float32)
    for piece in pieces:
        total = total + piece[:, block : block + LANES].astype(jnp.float32)
    sums = total + pltpu.roll(total, LANES - SLOT, 1) + pltpu.roll(total, LANES - 2 * SLOT, 1)
    mean = sums[:, experts : experts + 1] / model
    variance = sums[:, experts + 1 : experts + 2] / model - mean * mean
    inv = lax.rsqrt(variance + NORM_EPS)
    plain = pltpu.roll(sums, LANES - experts - 2, 1)
    logits = (sums - mean * plain) * inv
    lane = lax.broadcasted_iota(jnp.int32, (tokens, LANES), 1)
    named = (pltpu.roll(total, LANES - MASK_AT, 1) > 0) & (lane < experts)
    raised = jnp.where(named, jnp.exp(logits), 0.0)
    share = raised / jnp.sum(raised, axis=1, keepdims=True)
    high = share.astype(jnp.bfloat16).astype(jnp.float32)
    side = high + pltpu.roll(share - high, experts, 1)
    out_ref[:, model:] = side.astype(out_ref.dtype)
    for mask, piece in enumerate(pieces):
        gain = piece[:, block + LANES :].astype(jnp.float32)
        gain = jnp.concatenate([gain[j : j + 1, :] for j in range(block // LANES)], axis=1)
        x = (piece[:, :block].astype(jnp.float32) - mean) * inv * gain
        at = pl.multiple_of(lax.bitwise_xor(place_ref[0], mask) * block, block)
        out_ref[:, pl.ds(at, block)] = x.astype(out_ref.dtype)


def norm_rows(place, token, blocks, experts):
    tokens, wide = blocks[0].shape
    model = (wide - 2 * LANES) * len(blocks)
    vmem = pl.BlockSpec(memory_space=pltpu.VMEM)
    return pl.pallas_call(
        functools.partial(norm_kernel, experts=experts),
        out_shape=jax.ShapeDtypeStruct((tokens, model + LANES), jnp.bfloat16),
        in_specs=[pl.BlockSpec(memory_space=pltpu.SMEM)] + [vmem] * (1 + len(blocks)),
        out_specs=vmem,
        compiler_params=pltpu.CompilerParams(vmem_limit_bytes=4 * MIB),
        name="norm",
    )(place, token, *blocks)


def row_chunks(rows, most):
    count = max(c for c in range(1, most + 1) if rows % (16 * c) == 0 or c == 1)
    return [pl.ds(i * (rows // count), rows // count) for i in range(count)]


def load_kernel(_, source, out_ref, token_ref, sems):
    copies = [
        pltpu.make_async_copy(source.at[0, part], out_ref.at[part], sems.at[i])
        for i, part in enumerate(row_chunks(out_ref.shape[0], CHUNKS))
    ]
    for copy in copies:
        copy.start()
    token_ref[...] = jnp.zeros_like(token_ref)
    for copy in copies:
        copy.wait()


def load(after, weight):
    shape = weight.shape[1:]
    return pl.pallas_call(
        load_kernel,
        out_shape=(pltpu.VMEM(shape, weight.dtype), jax.ShapeDtypeStruct((8, LANES), jnp.float32)),
        in_specs=[pl.BlockSpec(memory_space=pl.ANY)] * 2,
        out_specs=(pl.BlockSpec(memory_space=pltpu.VMEM),) * 2,
        scratch_shapes=[pltpu.SemaphoreType.DMA((CHUNKS,))],
        compiler_params=pltpu.CompilerParams(vmem_limit_bytes=MIB),
        cost_estimate=pl.CostEstimate(flops=0, bytes_accessed=4 * shape[0] * shape[1], transcendentals=0),
        name="load",
    )(after, pltpu.with_memory_space_constraint(weight, pltpu.HBM))


def stack_kernel(_, *refs):
    pieces, out_ref = refs[:-1], refs[-1]
    rows = 2 * pieces[0].shape[0]
    for i in range(0, len(pieces), 2):
        pair = [piece[...].astype(jnp.float32) for piece in pieces[i : i + 2]]
        out_ref[i // 2 * rows : (i // 2 + 1) * rows] = jnp.concatenate(pair, axis=0).astype(out_ref.dtype)


def stack_rows(token, pieces):
    rows, wide = pieces[0].shape
    vmem = pl.BlockSpec(memory_space=pltpu.VMEM)
    return pl.pallas_call(
        stack_kernel,
        out_shape=jax.ShapeDtypeStruct((rows * len(pieces), wide), pieces[0].dtype),
        in_specs=[vmem] * (1 + len(pieces)),
        out_specs=vmem,
        compiler_params=pltpu.CompilerParams(vmem_limit_bytes=4 * MIB),
        name="stack",
    )(token, *pieces)


def expert_kernel(place_ref, near, far, gate, up, down_hbm, near_out, far_out, x, hidden, down, sems, *, experts):
    units, model = gate.shape
    half = near.shape[0]
    copies = [
        pltpu.make_async_copy(down_hbm.at[0, part], down.at[part], sems.at[i])
        for i, part in enumerate(row_chunks(units, CHUNKS))
    ]
    for copy in copies:
        copy.start()
    x[:half] = near[:, :model]
    x[half:] = far[:, :model]
    side = jnp.concatenate([near[:, model:], far[:, model:]], axis=0).astype(jnp.float32)
    lane = lax.broadcasted_iota(jnp.int32, side.shape, 1)
    expert = place_ref[1]
    mine = (lane == expert) | (lane == expert + experts)
    share = jnp.sum(jnp.where(mine, side, 0.0), axis=1, keepdims=True)
    for at in range(0, units, 256):
        part = slice(at, min(at + 256, units))
        a = lax.dot_general(x[...], gate[part], BY_ROW, preferred_element_type=jnp.float32)
        b = lax.dot_general(x[...], up[part], BY_ROW, preferred_element_type=jnp.float32)
        hidden[:, part] = (a / (1.0 + jnp.exp(-a)) * b).astype(hidden.dtype)
    for copy in copies:
        copy.wait()
    step = model // 6
    for at in range(0, model, step):
        part = slice(at, at + step)
        out = jnp.dot(hidden[...], down[:, part], preferred_element_type=jnp.float32) * share
        near_out[:, part] = out[:half].astype(near_out.dtype)
        far_out[:, part] = out[half:].astype(far_out.dtype)


def run_expert(place, near, far, gate, up, down_w, experts):
    units, model = gate.shape
    rows = 2 * near.shape[0]
    vmem = pl.BlockSpec(memory_space=pltpu.VMEM)
    shape = jax.ShapeDtypeStruct((near.shape[0], model), jnp.bfloat16)
    return pl.pallas_call(
        functools.partial(expert_kernel, experts=experts),
        out_shape=(shape, shape),
        in_specs=[pl.BlockSpec(memory_space=pltpu.SMEM)] + [vmem] * 4 + [pl.BlockSpec(memory_space=pl.ANY)],
        out_specs=(vmem, vmem),
        scratch_shapes=[
            pltpu.VMEM((rows, model), jnp.bfloat16),
            pltpu.VMEM((rows, units), jnp.bfloat16),
            pltpu.VMEM((units, model), down_w.dtype),
            pltpu.SemaphoreType.DMA((CHUNKS,)),
        ],
        compiler_params=pltpu.CompilerParams(vmem_limit_bytes=20 * MIB),
        cost_estimate=pl.CostEstimate(
            flops=6 * rows * units * model, bytes_accessed=6 * units * model, transcendentals=rows * units
        ),
        name="experts",
    )(place, near, far, gate, up, pltpu.with_memory_space_constraint(down_w, pltpu.HBM))


def send(x, axis, mask):
    return lax.ppermute(x, axis, [(i, i ^ mask) for i in range(lax.axis_size(axis))])


def add(*terms):
    return sum(t.astype(jnp.float32) for t in terms)


def per_device(
    queries, new_kv, kv_cache, cache_len, residual, norm_gain, router, routes, gate_w, up_w, down_w
):
    sections, groups, tensors = (lax.axis_size(a) for a in ("section", "group", "tensor"))
    experts, block = router.shape
    tokens = queries.shape[0]
    place = lax.axis_index("tensor")
    where = jnp.stack([place, lax.axis_index("section") * tensors + place]).astype(jnp.int32)

    fresh = attend(cache_len, queries, new_kv, kv_cache, residual, routes, router, norm_gain)
    blocks = [fresh] + [send(fresh, "tensor", m) for m in range(1, tensors)]
    gate, token = load(fresh, gate_w)
    rows = norm_rows(where, token, blocks, experts)
    arrived = [send(rows, "group", m) for m in range(1, groups)]
    up, token = load(rows, up_w)
    near = stack_rows(token, [rows] + arrived)
    far = send(near, "section", 1)

    kept, other = run_expert(where, near, far, gate, up, down_w, experts)
    both = add(kept, send(other, "section", 1)).astype(jnp.bfloat16)
    both = both.reshape(groups, tokens, -1)
    got = add(both[0], *[send(both[m], "group", m) for m in range(1, groups)]).astype(jnp.bfloat16)
    parts = [lax.dynamic_slice_in_dim(got, (place ^ m) * block, block, axis=1) for m in range(tensors)]
    mixed = add(fresh[:, :block], parts[0], *[send(parts[m], "tensor", m) for m in range(1, tensors)])
    return mixed.astype(jnp.bfloat16)


def solution(mesh):
    rows = P(("section", "group"), "tensor")
    weights = P(("section", "tensor"), "group", None)
    in_specs = (
        rows,
        rows,
        P(("section", "group"), None, "tensor"),
        P(("section", "group")),
        rows,
        P("tensor"),
        P(None, "tensor"),
        P(("section", "group"), None),
        weights,
        weights,
        weights,
    )
    return jax.shard_map(per_device, mesh=mesh, in_specs=in_specs, out_specs=rows, check_vma=False)
```

```python
import functools

import jax
import jax.numpy as jnp
from jax import lax
from jax.experimental import pallas as pl
from jax.experimental.pallas import tpu as pltpu
from jax.sharding import PartitionSpec as P

HEAD_DIM = 128
NORM_EPS = 1e-05
LANES = 128
SLOT = 36
MASK_AT = 3 * SLOT
MIB = 1 << 20
CHUNKS = 4
UNITS = 256
BY_ROW = (((1,), (1,)), ((), ()))


def split_terms(value):
    high = value.astype(jnp.bfloat16).astype(jnp.float32)
    rest = value - high
    middle = rest.astype(jnp.bfloat16).astype(jnp.float32)
    return high, middle, rest - middle


def attention_kernel(
    len_ref,
    q_hbm,
    new_hbm,
    kv_hbm,
    res_hbm,
    routes_hbm,
    router_hbm,
    gain_hbm,
    out_ref,
    q_ref,
    new_ref,
    kv,
    res_ref,
    routes_ref,
    router_ref,
    gain_ref,
    scores,
    sems,
    *,
    chunks,
):
    slots = kv_hbm.shape[1]
    part = slots // chunks
    sources = [q_hbm, new_hbm] + [kv_hbm.at[0, pl.ds(c * part, part)] for c in range(chunks)]
    targets = [q_ref, new_ref] + [kv.at[pl.ds(c * part, part)] for c in range(chunks)]
    sources += [res_hbm, routes_hbm, router_hbm, gain_hbm]
    targets += [res_ref, routes_ref, router_ref, gain_ref]
    copies = [pltpu.make_async_copy(a, b, sems.at[i]) for i, (a, b) in enumerate(zip(sources, targets))]
    for copy in copies:
        copy.start()
    tokens, columns = q_ref.shape
    key_heads = new_ref.shape[1] // (2 * HEAD_DIM)
    grouped = columns // HEAD_DIM // key_heads
    rows = grouped * tokens
    scale = HEAD_DIM ** (-0.5)
    copies[0].wait()
    copies[1].wait()
    queries, selves = [], []
    for h in range(key_heads):
        first = h * grouped * HEAD_DIM
        q = jnp.concatenate(
            [
                q_ref[:, first + j * HEAD_DIM : first + (j + 1) * HEAD_DIM].astype(jnp.float32)
                for j in range(grouped)
            ],
            axis=0,
        )
        own_key = new_ref[:, 2 * h * HEAD_DIM : (2 * h + 1) * HEAD_DIM].astype(jnp.float32)
        own_key = jnp.concatenate([own_key] * grouped, axis=0)
        selves.append(jnp.sum(q * own_key, axis=1, keepdims=True) * scale)
        queries.append(q.astype(jnp.bfloat16))
    live = len_ref[0]
    for c in range(chunks):
        copies[2 + c].wait()
        for h in range(key_heads):
            keys = kv[c * part : (c + 1) * part, 2 * h * HEAD_DIM : (2 * h + 1) * HEAD_DIM]
            s = lax.dot_general(queries[h], keys, BY_ROW, preferred_element_type=jnp.float32)
            at = lax.broadcasted_iota(jnp.int32, (rows, part), 1) + c * part
            scores[h, :, c * part : (c + 1) * part] = jnp.where(at < live, s * scale, -jnp.inf)
    for copy in copies[2 + chunks :]:
        copy.wait()

    experts = router_ref.shape[0]
    routes = routes_ref[...]
    expert_at = lax.broadcasted_iota(jnp.int32, (LANES, tokens), 0) - MASK_AT
    named = jnp.zeros((LANES, tokens), jnp.float32)
    for k in range(routes.shape[0]):
        named = jnp.where(expert_at == routes[k : k + 1, :], 1.0, named)
    side = named.T

    streams = []
    for h in range(key_heads):
        s = scores[h]
        top = jnp.maximum(jnp.max(s, axis=1, keepdims=True), selves[h])
        weights = jnp.exp(s - top).astype(jnp.bfloat16)
        own = jnp.exp(selves[h] - top).astype(jnp.bfloat16).astype(jnp.float32)
        total = jnp.sum(weights.astype(jnp.float32), axis=1, keepdims=True) + own
        value_at = (2 * h + 1) * HEAD_DIM
        mixed = jnp.dot(weights, kv[:, value_at : value_at + HEAD_DIM], preferred_element_type=jnp.float32)
        own_value = new_ref[:, value_at : value_at + HEAD_DIM].astype(jnp.float32)
        mixed = (mixed + own * jnp.concatenate([own_value] * grouped, axis=0)) / total
        for j in range(grouped):
            at = (h * grouped + j) * HEAD_DIM
            got = res_ref[:, at : at + HEAD_DIM].astype(jnp.float32) + mixed[j * tokens : (j + 1) * tokens]
            got = got.astype(jnp.bfloat16)
            out_ref[:, at : at + HEAD_DIM] = got
            streams.append(got.astype(jnp.float32))

    lane = lax.broadcasted_iota(jnp.int32, (tokens, LANES), 1)
    sums = jnp.zeros((tokens, LANES), jnp.float32)

    def put(sums, at, pieces):
        total = pieces[0]
        for piece in pieces[1:]:
            total = total + piece
        return jnp.where(lane == at, jnp.sum(total, axis=1, keepdims=True), sums)

    blocks = range(len(streams))
    sums = put(sums, experts, streams)
    sums = put(sums, experts + 1, [x * x for x in streams])
    gain = gain_ref[...].astype(jnp.float32).reshape(1, -1)
    gains = [gain[:, b * HEAD_DIM : (b + 1) * HEAD_DIM] for b in blocks]
    scaled = [x * g for x, g in zip(streams, gains)]
    for e in range(experts):
        weights = [router_ref[e : e + 1, b * HEAD_DIM : (b + 1) * HEAD_DIM].astype(jnp.float32) for b in blocks]
        sums = put(sums, e, [x * w for x, w in zip(scaled, weights)])
        plain = [jnp.broadcast_to(g * w, (tokens, HEAD_DIM)) for g, w in zip(gains, weights)]
        sums = put(sums, experts + 2 + e, plain)
    for i, term in enumerate(split_terms(sums)):
        side = side + (pltpu.roll(term, i * SLOT, 1) if i else term)
    out_ref[:, columns : columns + LANES] = side.astype(out_ref.dtype)
    gain_rows = jnp.concatenate(
        gains + [jnp.zeros((1, LANES), jnp.float32)] * (tokens - len(gains)), axis=0
    )
    out_ref[:, columns + LANES :] = gain_rows.astype(out_ref.dtype)


def attend(cache_len, queries, new_kv, kv_cache, residual, routes, router, norm_gain):
    tokens, columns = queries.shape
    slots, width = kv_cache.shape[1:]
    key_heads = new_kv.shape[1] // (2 * HEAD_DIM)
    rows = columns // HEAD_DIM // key_heads * tokens
    chunks = 4
    operands = [queries, new_kv, kv_cache, residual, routes.T, router, norm_gain]
    operands = [pltpu.with_memory_space_constraint(x, pltpu.HBM) for x in operands]
    kept = [pltpu.VMEM(x.shape, x.dtype) for x in operands]
    kept[2] = pltpu.VMEM((slots, width), kv_cache.dtype)
    return pl.pallas_call(
        functools.partial(attention_kernel, chunks=chunks),
        out_shape=jax.ShapeDtypeStruct((tokens, columns + 2 * LANES), jnp.bfloat16),
        in_specs=[pl.BlockSpec(memory_space=pltpu.SMEM)]
        + [pl.BlockSpec(memory_space=pl.ANY)] * len(operands),
        out_specs=pl.BlockSpec(memory_space=pltpu.VMEM),
        scratch_shapes=kept
        + [
            pltpu.VMEM((key_heads, rows, slots), jnp.float32),
            pltpu.SemaphoreType.DMA((chunks + len(operands) - 1,)),
        ],
        compiler_params=pltpu.CompilerParams(vmem_limit_bytes=8 * MIB),
        cost_estimate=pl.CostEstimate(
            flops=4 * rows * slots * HEAD_DIM * key_heads,
            bytes_accessed=slots * width * 2,
            transcendentals=rows * slots * key_heads,
        ),
        name="attention",
    )(cache_len, *operands)


def unit_parts(units):
    first = max(UNITS, units * 3 // 4 // UNITS * UNITS)
    if units <= 2 * UNITS:
        first = units // 32 * 16
    return pl.ds(0, first), pl.ds(first, units - first)


def start_load(source, target, part, sems):
    count = max(c for c in range(1, CHUNKS + 1) if part.size % (16 * c) == 0 or c == 1)
    step = part.size // count
    copies = [
        pltpu.make_async_copy(
            source.at[0, pl.ds(part.start + i * step, step)], target.at[pl.ds(i * step, step)], sems.at[i]
        )
        for i in range(count)
    ]
    for copy in copies:
        copy.start()
    return copies


def load_kernel(_, source, out_ref, token_ref, sems, *, part):
    copies = start_load(source, out_ref, part, sems)
    token_ref[...] = jnp.zeros_like(token_ref)
    for copy in copies:
        copy.wait()


def load(after, weight, part):
    shape = (part.size, weight.shape[2])
    return pl.pallas_call(
        functools.partial(load_kernel, part=part),
        out_shape=(pltpu.VMEM(shape, weight.dtype), jax.ShapeDtypeStruct((8, LANES), jnp.float32)),
        in_specs=[pl.BlockSpec(memory_space=pl.ANY)] * 2,
        out_specs=(pl.BlockSpec(memory_space=pltpu.VMEM),) * 2,
        scratch_shapes=[pltpu.SemaphoreType.DMA((CHUNKS,))],
        compiler_params=pltpu.CompilerParams(vmem_limit_bytes=MIB),
        cost_estimate=pl.CostEstimate(flops=0, bytes_accessed=4 * shape[0] * shape[1], transcendentals=0),
        name="load",
    )(after, pltpu.with_memory_space_constraint(weight, pltpu.HBM))


def norm_kernel(place_ref, _, source, *refs, experts, part):
    pieces, (out_ref, rest_ref, sems) = refs[:-3], refs[-3:]
    copies = start_load(source, rest_ref, part, sems)
    tokens, wide = pieces[0].shape
    block = wide - 2 * LANES
    model = len(pieces) * block
    total = jnp.zeros((tokens, LANES), jnp.float32)
    for piece in pieces:
        total = total + piece[:, block : block + LANES].astype(jnp.float32)
    sums = total + pltpu.roll(total, LANES - SLOT, 1) + pltpu.roll(total, LANES - 2 * SLOT, 1)
    mean = sums[:, experts : experts + 1] / model
    variance = sums[:, experts + 1 : experts + 2] / model - mean * mean
    inv = lax.rsqrt(variance + NORM_EPS)
    plain = pltpu.roll(sums, LANES - experts - 2, 1)
    logits = (sums - mean * plain) * inv
    lane = lax.broadcasted_iota(jnp.int32, (tokens, LANES), 1)
    named = (pltpu.roll(total, LANES - MASK_AT, 1) > 0) & (lane < experts)
    raised = jnp.where(named, jnp.exp(logits), 0.0)
    share = raised / jnp.sum(raised, axis=1, keepdims=True)
    high = share.astype(jnp.bfloat16).astype(jnp.float32)
    side = high + pltpu.roll(share - high, experts, 1)
    out_ref[:, model:] = side.astype(out_ref.dtype)
    for mask, piece in enumerate(reversed(pieces)):
        gain = piece[:, block + LANES :].astype(jnp.float32)
        gain = jnp.concatenate([gain[j : j + 1, :] for j in range(block // LANES)], axis=1)
        x = (piece[:, :block].astype(jnp.float32) - mean) * inv * gain
        at = pl.multiple_of(lax.bitwise_xor(place_ref[0], mask) * block, block)
        out_ref[:, pl.ds(at, block)] = x.astype(out_ref.dtype)
    for copy in copies:
        copy.wait()


def norm_rows(place, token, weight, part, blocks, experts):
    tokens, wide = blocks[0].shape
    model = (wide - 2 * LANES) * len(blocks)
    vmem = pl.BlockSpec(memory_space=pltpu.VMEM)
    return pl.pallas_call(
        functools.partial(norm_kernel, experts=experts, part=part),
        out_shape=(
            jax.ShapeDtypeStruct((tokens, model + LANES), jnp.bfloat16),
            pltpu.VMEM((part.size, weight.shape[2]), weight.dtype),
        ),
        in_specs=[pl.BlockSpec(memory_space=pltpu.SMEM), vmem, pl.BlockSpec(memory_space=pl.ANY)]
        + [vmem] * len(blocks),
        out_specs=(vmem, vmem),
        scratch_shapes=[pltpu.SemaphoreType.DMA((CHUNKS,))],
        compiler_params=pltpu.CompilerParams(vmem_limit_bytes=4 * MIB),
        name="norm",
    )(place, token, pltpu.with_memory_space_constraint(weight, pltpu.HBM), *blocks)


def stack_kernel(_, *refs):
    pieces, out_ref = refs[:-1][::-1], refs[-1]
    rows = 2 * pieces[0].shape[0]
    for i in range(0, len(pieces), 2):
        pair = [piece[...].astype(jnp.float32) for piece in pieces[i : i + 2]]
        out_ref[i // 2 * rows : (i // 2 + 1) * rows] = jnp.concatenate(pair, axis=0).astype(out_ref.dtype)


def stack_rows(token, pieces):
    rows, wide = pieces[0].shape
    vmem = pl.BlockSpec(memory_space=pltpu.VMEM)
    return pl.pallas_call(
        stack_kernel,
        out_shape=jax.ShapeDtypeStruct((rows * len(pieces), wide), pieces[0].dtype),
        in_specs=[vmem] * (1 + len(pieces)),
        out_specs=vmem,
        compiler_params=pltpu.CompilerParams(vmem_limit_bytes=4 * MIB),
        name="stack",
    )(token, *pieces)


def hidden_kernel(place_ref, near, far, gate_a, gate_b, up_a, up_b, _, hidden, x, *, experts):
    half = near.shape[0]
    model = gate_a.shape[1]
    x[:half] = near[:, :model]
    x[half:] = far[:, :model]
    side = jnp.concatenate([near[:, model:], far[:, model:]], axis=0).astype(jnp.float32)
    lane = lax.broadcasted_iota(jnp.int32, side.shape, 1)
    expert = place_ref[1]
    mine = (lane == expert) | (lane == expert + experts)
    share = jnp.sum(jnp.where(mine, side, 0.0), axis=1, keepdims=True)
    first = 0
    for gate, up in ((gate_a, up_a), (gate_b, up_b)):
        units = gate.shape[0]
        for at in range(0, units, UNITS):
            part = slice(at, min(at + UNITS, units))
            a = lax.dot_general(x[...], gate[part], BY_ROW, preferred_element_type=jnp.float32)
            b = lax.dot_general(x[...], up[part], BY_ROW, preferred_element_type=jnp.float32)
            out = a / (1.0 + jnp.exp(-a)) * b * share
            hidden[:, first + part.start : first + part.stop] = out.astype(hidden.dtype)
        first += units


def run_hidden(place, near, far, weights, token, experts):
    units = weights[0].shape[0] + weights[1].shape[0]
    model = weights[0].shape[1]
    rows = 2 * near.shape[0]
    vmem = pl.BlockSpec(memory_space=pltpu.VMEM)
    return pl.pallas_call(
        functools.partial(hidden_kernel, experts=experts),
        out_shape=jax.ShapeDtypeStruct((rows, units), jnp.bfloat16),
        in_specs=[pl.BlockSpec(memory_space=pltpu.SMEM)] + [vmem] * 7,
        out_specs=vmem,
        scratch_shapes=[pltpu.VMEM((rows, model), jnp.bfloat16)],
        compiler_params=pltpu.CompilerParams(vmem_limit_bytes=6 * MIB),
        cost_estimate=pl.CostEstimate(
            flops=4 * rows * units * model, bytes_accessed=4 * units * model, transcendentals=rows * units
        ),
        name="hidden",
    )(place, near, far, *weights, token)


def send(x, axis, mask):
    return lax.ppermute(x, axis, [(i, i ^ mask) for i in range(lax.axis_size(axis))])


def exchange(parts, axis):
    return [send(parts[m], axis, m) for m in reversed(range(1, lax.axis_size(axis)))]


def add(*terms):
    return sum(t.astype(jnp.float32) for t in terms)


def per_device(
    queries, new_kv, kv_cache, cache_len, residual, norm_gain, router, routes, gate_w, up_w, down_w
):
    sections, groups, tensors = (lax.axis_size(a) for a in ("section", "group", "tensor"))
    experts, block = router.shape
    tokens = queries.shape[0]
    place = lax.axis_index("tensor")
    where = jnp.stack([place, lax.axis_index("section") * tensors + place]).astype(jnp.int32)

    early, late = unit_parts(gate_w.shape[1])

    fresh = attend(cache_len, queries, new_kv, kv_cache, residual, routes, router, norm_gain)
    blocks = exchange([fresh] * tensors, "tensor") + [fresh]
    gate_a, token = load(fresh, gate_w, early)
    rows, gate_b = norm_rows(where, token, gate_w, late, blocks, experts)
    ranks = exchange([rows] * groups, "group") + [rows]
    up_a, token = load(rows, up_w, early)
    near = stack_rows(token, ranks)
    far = send(near, "section", 1)
    up_b, token = load(near, up_w, late)

    hidden = run_hidden(where, near, far, (gate_a, gate_b, up_a, up_b), token, experts)
    out = jnp.dot(hidden, down_w[0], preferred_element_type=jnp.float32).astype(jnp.bfloat16)
    half = out.shape[0] // 2
    both = add(out[:half], send(out[half:], "section", 1)).astype(jnp.bfloat16)
    both = both.reshape(groups, tokens, -1)
    got = add(*exchange(both, "group"), both[0]).astype(jnp.bfloat16)
    parts = [lax.dynamic_slice_in_dim(got, (place ^ m) * block, block, axis=1) for m in range(tensors)]
    mixed = add(*exchange(parts, "tensor"), parts[0], fresh[:, :block])
    return mixed.astype(jnp.bfloat16)


def solution(mesh):
    rows = P(("section", "group"), "tensor")
    weights = P(("section", "tensor"), "group", None)
    in_specs = (
        rows,
        rows,
        P(("section", "group"), None, "tensor"),
        P(("section", "group")),
        rows,
        P("tensor"),
        P(None, "tensor"),
        P(("section", "group"), None),
        weights,
        weights,
        weights,
    )
    return jax.shard_map(per_device, mesh=mesh, in_specs=in_specs, out_specs=rows, check_vma=False)
```

```python
import functools

import jax
import jax.numpy as jnp
from jax import lax
from jax.experimental import pallas as pl
from jax.experimental.pallas import tpu as pltpu
from jax.sharding import PartitionSpec as P

HEAD_DIM = 128
NORM_EPS = 1e-05
LANES = 128
SLOT = 36
MASK_AT = 3 * SLOT
MIB = 1 << 20
CHUNKS = 4
UNITS = 256
BY_ROW = (((1,), (1,)), ((), ()))


def split_terms(value):
    high = value.astype(jnp.bfloat16).astype(jnp.float32)
    rest = value - high
    middle = rest.astype(jnp.bfloat16).astype(jnp.float32)
    return high, middle, rest - middle


def unit_parts(units):
    first = max(UNITS, units * 3 // 4 // UNITS * UNITS)
    if units <= 2 * UNITS:
        first = units // 32 * 16
    return pl.ds(0, first), pl.ds(first, units - first)


def start_load(source, target, part, sems):
    count = max(c for c in range(1, CHUNKS + 1) if part.size % (16 * c) == 0 or c == 1)
    step = part.size // count
    copies = [
        pltpu.make_async_copy(
            source.at[0, pl.ds(part.start + i * step, step)], target.at[pl.ds(i * step, step)], sems.at[i]
        )
        for i in range(count)
    ]
    for copy in copies:
        copy.start()
    return copies


def attention_kernel(
    len_ref,
    q_hbm,
    new_hbm,
    kv_hbm,
    res_hbm,
    routes_hbm,
    router_hbm,
    gain_hbm,
    weight_hbm,
    out_ref,
    weight_ref,
    q_ref,
    new_ref,
    kv,
    res_ref,
    routes_ref,
    router_ref,
    gain_ref,
    scores,
    sems,
    weight_sems,
    *,
    chunks,
    rest,
):
    slots = kv_hbm.shape[1]
    part = slots // chunks
    sources = [q_hbm, new_hbm] + [kv_hbm.at[0, pl.ds(c * part, part)] for c in range(chunks)]
    targets = [q_ref, new_ref] + [kv.at[pl.ds(c * part, part)] for c in range(chunks)]
    sources += [res_hbm, routes_hbm, router_hbm, gain_hbm]
    targets += [res_ref, routes_ref, router_ref, gain_ref]
    copies = [pltpu.make_async_copy(a, b, sems.at[i]) for i, (a, b) in enumerate(zip(sources, targets))]
    for copy in copies:
        copy.start()
    loads = start_load(weight_hbm, weight_ref, rest, weight_sems)
    tokens, columns = q_ref.shape
    key_heads = new_ref.shape[1] // (2 * HEAD_DIM)
    grouped = columns // HEAD_DIM // key_heads
    rows = grouped * tokens
    scale = HEAD_DIM ** (-0.5)
    copies[0].wait()
    copies[1].wait()
    queries, selves = [], []
    for h in range(key_heads):
        first = h * grouped * HEAD_DIM
        q = jnp.concatenate(
            [
                q_ref[:, first + j * HEAD_DIM : first + (j + 1) * HEAD_DIM].astype(jnp.float32)
                for j in range(grouped)
            ],
            axis=0,
        )
        own_key = new_ref[:, 2 * h * HEAD_DIM : (2 * h + 1) * HEAD_DIM].astype(jnp.float32)
        own_key = jnp.concatenate([own_key] * grouped, axis=0)
        selves.append(jnp.sum(q * own_key, axis=1, keepdims=True) * scale)
        queries.append(q.astype(jnp.bfloat16))
    live = len_ref[0]
    for c in range(chunks):
        copies[2 + c].wait()
        for h in range(key_heads):
            keys = kv[c * part : (c + 1) * part, 2 * h * HEAD_DIM : (2 * h + 1) * HEAD_DIM]
            s = lax.dot_general(queries[h], keys, BY_ROW, preferred_element_type=jnp.float32)
            at = lax.broadcasted_iota(jnp.int32, (rows, part), 1) + c * part
            scores[h, :, c * part : (c + 1) * part] = jnp.where(at < live, s * scale, -jnp.inf)
    for copy in copies[2 + chunks :]:
        copy.wait()

    experts = router_ref.shape[0]
    routes = routes_ref[...]
    expert_at = lax.broadcasted_iota(jnp.int32, (LANES, tokens), 0) - MASK_AT
    named = jnp.zeros((LANES, tokens), jnp.float32)
    for k in range(routes.shape[0]):
        named = jnp.where(expert_at == routes[k : k + 1, :], 1.0, named)
    side = named.T

    streams = []
    for h in range(key_heads):
        s = scores[h]
        top = jnp.maximum(jnp.max(s, axis=1, keepdims=True), selves[h])
        weights = jnp.exp(s - top).astype(jnp.bfloat16)
        own = jnp.exp(selves[h] - top).astype(jnp.bfloat16).astype(jnp.float32)
        total = jnp.sum(weights.astype(jnp.float32), axis=1, keepdims=True) + own
        value_at = (2 * h + 1) * HEAD_DIM
        mixed = jnp.dot(weights, kv[:, value_at : value_at + HEAD_DIM], preferred_element_type=jnp.float32)
        own_value = new_ref[:, value_at : value_at + HEAD_DIM].astype(jnp.float32)
        mixed = (mixed + own * jnp.concatenate([own_value] * grouped, axis=0)) / total
        for j in range(grouped):
            at = (h * grouped + j) * HEAD_DIM
            got = res_ref[:, at : at + HEAD_DIM].astype(jnp.float32) + mixed[j * tokens : (j + 1) * tokens]
            got = got.astype(jnp.bfloat16)
            out_ref[:, at : at + HEAD_DIM] = got
            streams.append(got.astype(jnp.float32))

    lane = lax.broadcasted_iota(jnp.int32, (tokens, LANES), 1)
    sums = jnp.zeros((tokens, LANES), jnp.float32)

    def put(sums, at, pieces):
        total = pieces[0]
        for piece in pieces[1:]:
            total = total + piece
        return jnp.where(lane == at, jnp.sum(total, axis=1, keepdims=True), sums)

    blocks = range(len(streams))
    sums = put(sums, experts, streams)
    sums = put(sums, experts + 1, [x * x for x in streams])
    gain = gain_ref[...].astype(jnp.float32).reshape(1, -1)
    gains = [gain[:, b * HEAD_DIM : (b + 1) * HEAD_DIM] for b in blocks]
    scaled = [x * g for x, g in zip(streams, gains)]
    for e in range(experts):
        weights = [router_ref[e : e + 1, b * HEAD_DIM : (b + 1) * HEAD_DIM].astype(jnp.float32) for b in blocks]
        sums = put(sums, e, [x * w for x, w in zip(scaled, weights)])
        plain = [jnp.broadcast_to(g * w, (tokens, HEAD_DIM)) for g, w in zip(gains, weights)]
        sums = put(sums, experts + 2 + e, plain)
    for i, term in enumerate(split_terms(sums)):
        side = side + (pltpu.roll(term, i * SLOT, 1) if i else term)
    out_ref[:, columns : columns + LANES] = side.astype(out_ref.dtype)
    gain_rows = jnp.concatenate(
        gains + [jnp.zeros((1, LANES), jnp.float32)] * (tokens - len(gains)), axis=0
    )
    out_ref[:, columns + LANES :] = gain_rows.astype(out_ref.dtype)
    for copy in loads:
        copy.wait()


def attend(cache_len, queries, new_kv, kv_cache, residual, routes, router, norm_gain, weight, rest):
    tokens, columns = queries.shape
    slots, width = kv_cache.shape[1:]
    key_heads = new_kv.shape[1] // (2 * HEAD_DIM)
    rows = columns // HEAD_DIM // key_heads * tokens
    chunks = 4
    operands = [queries, new_kv, kv_cache, residual, routes.T, router, norm_gain, weight]
    operands = [pltpu.with_memory_space_constraint(x, pltpu.HBM) for x in operands]
    kept = [pltpu.VMEM(x.shape, x.dtype) for x in operands[:-1]]
    kept[2] = pltpu.VMEM((slots, width), kv_cache.dtype)
    return pl.pallas_call(
        functools.partial(attention_kernel, chunks=chunks, rest=rest),
        out_shape=(
            jax.ShapeDtypeStruct((tokens, columns + 2 * LANES), jnp.bfloat16),
            pltpu.VMEM((rest.size, weight.shape[2]), weight.dtype),
        ),
        in_specs=[pl.BlockSpec(memory_space=pltpu.SMEM)]
        + [pl.BlockSpec(memory_space=pl.ANY)] * len(operands),
        out_specs=(pl.BlockSpec(memory_space=pltpu.VMEM),) * 2,
        scratch_shapes=kept
        + [
            pltpu.VMEM((key_heads, rows, slots), jnp.float32),
            pltpu.SemaphoreType.DMA((chunks + len(operands) - 2,)),
            pltpu.SemaphoreType.DMA((CHUNKS,)),
        ],
        compiler_params=pltpu.CompilerParams(vmem_limit_bytes=8 * MIB),
        cost_estimate=pl.CostEstimate(
            flops=4 * rows * slots * HEAD_DIM * key_heads,
            bytes_accessed=slots * width * 2,
            transcendentals=rows * slots * key_heads,
        ),
        name="attention",
    )(cache_len, *operands)


def load_kernel(_, source, out_ref, token_ref, sems, *, part):
    copies = start_load(source, out_ref, part, sems)
    token_ref[...] = jnp.zeros_like(token_ref)
    for copy in copies:
        copy.wait()


def load(after, weight, part):
    shape = (part.size, weight.shape[2])
    return pl.pallas_call(
        functools.partial(load_kernel, part=part),
        out_shape=(pltpu.VMEM(shape, weight.dtype), jax.ShapeDtypeStruct((8, LANES), jnp.float32)),
        in_specs=[pl.BlockSpec(memory_space=pl.ANY)] * 2,
        out_specs=(pl.BlockSpec(memory_space=pltpu.VMEM),) * 2,
        scratch_shapes=[pltpu.SemaphoreType.DMA((CHUNKS,))],
        compiler_params=pltpu.CompilerParams(vmem_limit_bytes=MIB),
        cost_estimate=pl.CostEstimate(flops=0, bytes_accessed=4 * shape[0] * shape[1], transcendentals=0),
        name="load",
    )(after, pltpu.with_memory_space_constraint(weight, pltpu.HBM))


def norm_kernel(place_ref, _, *refs, experts):
    pieces, out_ref = refs[:-1], refs[-1]
    tokens, wide = pieces[0].shape
    block = wide - 2 * LANES
    model = len(pieces) * block
    total = jnp.zeros((tokens, LANES), jnp.float32)
    for piece in pieces:
        total = total + piece[:, block : block + LANES].astype(jnp.float32)
    sums = total + pltpu.roll(total, LANES - SLOT, 1) + pltpu.roll(total, LANES - 2 * SLOT, 1)
    mean = sums[:, experts : experts + 1] / model
    variance = sums[:, experts + 1 : experts + 2] / model - mean * mean
    inv = lax.rsqrt(variance + NORM_EPS)
    plain = pltpu.roll(sums, LANES - experts - 2, 1)
    logits = (sums - mean * plain) * inv
    lane = lax.broadcasted_iota(jnp.int32, (tokens, LANES), 1)
    named = (pltpu.roll(total, LANES - MASK_AT, 1) > 0) & (lane < experts)
    raised = jnp.where(named, jnp.exp(logits), 0.0)
    share = raised / jnp.sum(raised, axis=1, keepdims=True)
    high = share.astype(jnp.bfloat16).astype(jnp.float32)
    side = high + pltpu.roll(share - high, experts, 1)
    out_ref[:, model:] = side.astype(out_ref.dtype)
    for mask, piece in enumerate(reversed(pieces)):
        gain = piece[:, block + LANES :].astype(jnp.float32)
        gain = jnp.concatenate([gain[j : j + 1, :] for j in range(block // LANES)], axis=1)
        x = (piece[:, :block].astype(jnp.float32) - mean) * inv * gain
        at = pl.multiple_of(lax.bitwise_xor(place_ref[0], mask) * block, block)
        out_ref[:, pl.ds(at, block)] = x.astype(out_ref.dtype)


def norm_rows(place, token, blocks, experts):
    tokens, wide = blocks[0].shape
    model = (wide - 2 * LANES) * len(blocks)
    vmem = pl.BlockSpec(memory_space=pltpu.VMEM)
    return pl.pallas_call(
        functools.partial(norm_kernel, experts=experts),
        out_shape=jax.ShapeDtypeStruct((tokens, model + LANES), jnp.bfloat16),
        in_specs=[pl.BlockSpec(memory_space=pltpu.SMEM)] + [vmem] * (1 + len(blocks)),
        out_specs=vmem,
        compiler_params=pltpu.CompilerParams(vmem_limit_bytes=4 * MIB),
        name="norm",
    )(place, token, *blocks)


def stack_kernel(_, *refs):
    pieces, out_ref = refs[:-1][::-1], refs[-1]
    rows = 2 * pieces[0].shape[0]
    for i in range(0, len(pieces), 2):
        pair = [piece[...].astype(jnp.float32) for piece in pieces[i : i + 2]]
        out_ref[i // 2 * rows : (i // 2 + 1) * rows] = jnp.concatenate(pair, axis=0).astype(out_ref.dtype)


def stack_rows(token, pieces):
    rows, wide = pieces[0].shape
    vmem = pl.BlockSpec(memory_space=pltpu.VMEM)
    return pl.pallas_call(
        stack_kernel,
        out_shape=jax.ShapeDtypeStruct((rows * len(pieces), wide), pieces[0].dtype),
        in_specs=[vmem] * (1 + len(pieces)),
        out_specs=vmem,
        compiler_params=pltpu.CompilerParams(vmem_limit_bytes=4 * MIB),
        name="stack",
    )(token, *pieces)


def hidden_kernel(place_ref, near, far, gate_a, gate_b, up_a, up_hbm, hidden, x, up_b, sems, *, experts, rest):
    loads = start_load(up_hbm, up_b, rest, sems)
    model = gate_a.shape[1]
    step = 2 * LANES
    for at in range(0, model, step):
        both = [ref[:, at : at + step].astype(jnp.float32) for ref in (near, far)]
        x[at : at + step] = jnp.concatenate(both, axis=0).T.astype(x.dtype)
    side = jnp.concatenate([ref[:, model:].astype(jnp.float32) for ref in (near, far)], axis=0).T
    at = lax.broadcasted_iota(jnp.int32, side.shape, 0)
    expert = place_ref[1]
    mine = (at == expert) | (at == expert + experts)
    share = jnp.sum(jnp.where(mine, side, 0.0), axis=0, keepdims=True)
    first = 0
    for gate, up in ((gate_a, up_a), (gate_b, up_b)):
        if first:
            for copy in loads:
                copy.wait()
        units = gate.shape[0]
        for at in range(0, units, UNITS):
            part = slice(at, min(at + UNITS, units))
            a = jnp.dot(gate[part], x[...], preferred_element_type=jnp.float32)
            b = jnp.dot(up[part], x[...], preferred_element_type=jnp.float32)
            out = a / (1.0 + jnp.exp(-a)) * b * share
            hidden[:, first + part.start : first + part.stop] = out.T.astype(hidden.dtype)
        first += units


def run_hidden(place, near, far, gate_a, gate_b, up_a, up_w, rest, experts):
    units, model = up_w.shape[1:]
    rows = 2 * near.shape[0]
    vmem = pl.BlockSpec(memory_space=pltpu.VMEM)
    return pl.pallas_call(
        functools.partial(hidden_kernel, experts=experts, rest=rest),
        out_shape=jax.ShapeDtypeStruct((rows, units), jnp.bfloat16),
        in_specs=[pl.BlockSpec(memory_space=pltpu.SMEM)] + [vmem] * 5 + [pl.BlockSpec(memory_space=pl.ANY)],
        out_specs=vmem,
        scratch_shapes=[
            pltpu.VMEM((model, rows), jnp.bfloat16),
            pltpu.VMEM((rest.size, model), up_w.dtype),
            pltpu.SemaphoreType.DMA((CHUNKS,)),
        ],
        compiler_params=pltpu.CompilerParams(vmem_limit_bytes=(8 if rows <= 64 else 24) * MIB),
        cost_estimate=pl.CostEstimate(
            flops=4 * rows * units * model, bytes_accessed=4 * units * model, transcendentals=rows * units
        ),
        name="hidden",
    )(place, near, far, gate_a, gate_b, up_a, pltpu.with_memory_space_constraint(up_w, pltpu.HBM))


def send(x, axis, mask):
    return lax.ppermute(x, axis, [(i, i ^ mask) for i in range(lax.axis_size(axis))])


def exchange(parts, axis):
    return [send(parts[m], axis, m) for m in reversed(range(1, lax.axis_size(axis)))]


def add(*terms):
    return sum(t.astype(jnp.float32) for t in terms)


def per_device(
    queries, new_kv, kv_cache, cache_len, residual, norm_gain, router, routes, gate_w, up_w, down_w
):
    sections, groups, tensors = (lax.axis_size(a) for a in ("section", "group", "tensor"))
    experts, block = router.shape
    tokens = queries.shape[0]
    place = lax.axis_index("tensor")
    where = jnp.stack([place, lax.axis_index("section") * tensors + place]).astype(jnp.int32)

    early, late = unit_parts(gate_w.shape[1])

    fresh, gate_b = attend(
        cache_len, queries, new_kv, kv_cache, residual, routes, router, norm_gain, gate_w, late
    )
    blocks = exchange([fresh] * tensors, "tensor") + [fresh]
    gate_a, token = load(fresh, gate_w, early)
    rows = norm_rows(where, token, blocks, experts)
    ranks = exchange([rows] * groups, "group") + [rows]
    up_a, token = load(rows, up_w, early)
    near = stack_rows(token, ranks)
    far = send(near, "section", 1)

    hidden = run_hidden(where, near, far, gate_a, gate_b, up_a, up_w, late, experts)
    out = jnp.dot(hidden, down_w[0], preferred_element_type=jnp.float32).astype(jnp.bfloat16)
    half = out.shape[0] // 2
    both = add(out[:half], send(out[half:], "section", 1)).astype(jnp.bfloat16)
    both = both.reshape(groups, tokens, -1)
    got = add(*exchange(both, "group"), both[0]).astype(jnp.bfloat16)
    parts = [lax.dynamic_slice_in_dim(got, (place ^ m) * block, block, axis=1) for m in range(tensors)]
    mixed = add(*exchange(parts, "tensor"), parts[0], fresh[:, :block])
    return mixed.astype(jnp.bfloat16)


def solution(mesh):
    rows = P(("section", "group"), "tensor")
    weights = P(("section", "tensor"), "group", None)
    in_specs = (
        rows,
        rows,
        P(("section", "group"), None, "tensor"),
        P(("section", "group")),
        rows,
        P("tensor"),
        P(None, "tensor"),
        P(("section", "group"), None),
        weights,
        weights,
        weights,
    )
    return jax.shard_map(per_device, mesh=mesh, in_specs=in_specs, out_specs=rows, check_vma=False)
```

```python
import functools

import jax
import jax.numpy as jnp
from jax import lax
from jax.experimental import pallas as pl
from jax.experimental.pallas import tpu as pltpu
from jax.sharding import PartitionSpec as P

HEAD_DIM = 128
NORM_EPS = 1e-05
LANES = 128
SLOT = 36
MASK_AT = 3 * SLOT
MIB = 1 << 20
CHUNKS = 4
UNITS = 256
BY_ROW = (((1,), (1,)), ((), ()))


def split_terms(value):
    high = value.astype(jnp.bfloat16).astype(jnp.float32)
    rest = value - high
    middle = rest.astype(jnp.bfloat16).astype(jnp.float32)
    return high, middle, rest - middle


def unit_parts(units):
    ends = [0, 4 * UNITS, 5 * UNITS, units]
    if units <= ends[2]:
        step = units // 64 * 16
        ends = [0, 2 * step, 3 * step, units]
    return [pl.ds(a, b - a) for a, b in zip(ends, ends[1:])]


def start_load(source, target, part, sems):
    count = max(c for c in range(1, CHUNKS + 1) if part.size % (16 * c) == 0 or c == 1)
    step = part.size // count
    copies = [
        pltpu.make_async_copy(
            source.at[0, pl.ds(part.start + i * step, step)], target.at[pl.ds(i * step, step)], sems.at[i]
        )
        for i in range(count)
    ]
    for copy in copies:
        copy.start()
    return copies


def attention_kernel(
    len_ref,
    q_hbm,
    new_hbm,
    kv_hbm,
    res_hbm,
    routes_hbm,
    router_hbm,
    gain_hbm,
    weight_hbm,
    out_ref,
    weight_ref,
    q_ref,
    new_ref,
    kv,
    res_ref,
    routes_ref,
    router_ref,
    gain_ref,
    scores,
    sems,
    weight_sems,
    *,
    chunks,
    rest,
):
    slots = kv_hbm.shape[1]
    part = slots // chunks
    sources = [q_hbm, new_hbm, res_hbm, routes_hbm, router_hbm, gain_hbm]
    targets = [q_ref, new_ref, res_ref, routes_ref, router_ref, gain_ref]
    small = len(sources)
    sources += [kv_hbm.at[0, pl.ds(c * part, part)] for c in range(chunks)]
    targets += [kv.at[pl.ds(c * part, part)] for c in range(chunks)]
    copies = [pltpu.make_async_copy(a, b, sems.at[i]) for i, (a, b) in enumerate(zip(sources, targets))]
    for copy in copies:
        copy.start()
    loads = start_load(weight_hbm, weight_ref, rest, weight_sems)
    tokens, columns = q_ref.shape
    blocks = range(columns // HEAD_DIM)
    key_heads = new_ref.shape[1] // (2 * HEAD_DIM)
    grouped = columns // HEAD_DIM // key_heads
    rows = grouped * tokens
    scale = HEAD_DIM ** (-0.5)
    copies[0].wait()
    copies[1].wait()
    queries, selves = [], []
    for h in range(key_heads):
        first = h * grouped * HEAD_DIM
        q = jnp.concatenate(
            [
                q_ref[:, first + j * HEAD_DIM : first + (j + 1) * HEAD_DIM].astype(jnp.float32)
                for j in range(grouped)
            ],
            axis=0,
        )
        own_key = new_ref[:, 2 * h * HEAD_DIM : (2 * h + 1) * HEAD_DIM].astype(jnp.float32)
        own_key = jnp.concatenate([own_key] * grouped, axis=0)
        selves.append(jnp.sum(q * own_key, axis=1, keepdims=True) * scale)
        queries.append(q.astype(jnp.bfloat16))
    for copy in copies[2:small]:
        copy.wait()

    experts = router_ref.shape[0]
    routes = routes_ref[...]
    expert_at = lax.broadcasted_iota(jnp.int32, (LANES, tokens), 0) - MASK_AT
    named = jnp.zeros((LANES, tokens), jnp.float32)
    for k in range(routes.shape[0]):
        named = jnp.where(expert_at == routes[k : k + 1, :], 1.0, named)
    side = named.T

    lane = lax.broadcasted_iota(jnp.int32, (tokens, LANES), 1)
    sums = jnp.zeros((tokens, LANES), jnp.float32)

    def put(sums, at, pieces):
        total = pieces[0]
        for piece in pieces[1:]:
            total = total + piece
        return jnp.where(lane == at, jnp.sum(total, axis=1, keepdims=True), sums)

    gain = gain_ref[...].astype(jnp.float32).reshape(1, -1)
    gains = [gain[:, b * HEAD_DIM : (b + 1) * HEAD_DIM] for b in blocks]
    scaled = []
    for e in range(experts):
        weights = [router_ref[e : e + 1, b * HEAD_DIM : (b + 1) * HEAD_DIM].astype(jnp.float32) for b in blocks]
        scaled.append([jnp.broadcast_to(g * w, (tokens, HEAD_DIM)) for g, w in zip(gains, weights)])
        sums = put(sums, experts + 2 + e, scaled[e])

    live = len_ref[0]
    for c in range(chunks):
        copies[small + c].wait()
        for h in range(key_heads):
            keys = kv[c * part : (c + 1) * part, 2 * h * HEAD_DIM : (2 * h + 1) * HEAD_DIM]
            s = lax.dot_general(queries[h], keys, BY_ROW, preferred_element_type=jnp.float32)
            at = lax.broadcasted_iota(jnp.int32, (rows, part), 1) + c * part
            scores[h, :, c * part : (c + 1) * part] = jnp.where(at < live, s * scale, -jnp.inf)
    streams = []
    for h in range(key_heads):
        s = scores[h]
        top = jnp.maximum(jnp.max(s, axis=1, keepdims=True), selves[h])
        weights = jnp.exp(s - top).astype(jnp.bfloat16)
        own = jnp.exp(selves[h] - top).astype(jnp.bfloat16).astype(jnp.float32)
        total = jnp.sum(weights.astype(jnp.float32), axis=1, keepdims=True) + own
        value_at = (2 * h + 1) * HEAD_DIM
        mixed = jnp.dot(weights, kv[:, value_at : value_at + HEAD_DIM], preferred_element_type=jnp.float32)
        own_value = new_ref[:, value_at : value_at + HEAD_DIM].astype(jnp.float32)
        mixed = (mixed + own * jnp.concatenate([own_value] * grouped, axis=0)) / total
        for j in range(grouped):
            at = (h * grouped + j) * HEAD_DIM
            got = res_ref[:, at : at + HEAD_DIM].astype(jnp.float32) + mixed[j * tokens : (j + 1) * tokens]
            got = got.astype(jnp.bfloat16)
            out_ref[:, at : at + HEAD_DIM] = got
            streams.append(got.astype(jnp.float32))

    sums = put(sums, experts, streams)
    sums = put(sums, experts + 1, [x * x for x in streams])
    for e in range(experts):
        sums = put(sums, e, [x * w for x, w in zip(streams, scaled[e])])
    for i, term in enumerate(split_terms(sums)):
        side = side + (pltpu.roll(term, i * SLOT, 1) if i else term)
    out_ref[:, columns : columns + LANES] = side.astype(out_ref.dtype)
    gain_rows = jnp.concatenate(
        gains + [jnp.zeros((1, LANES), jnp.float32)] * (tokens - len(gains)), axis=0
    )
    out_ref[:, columns + LANES :] = gain_rows.astype(out_ref.dtype)
    for copy in loads:
        copy.wait()


def attend(cache_len, queries, new_kv, kv_cache, residual, routes, router, norm_gain, weight, rest):
    tokens, columns = queries.shape
    slots, width = kv_cache.shape[1:]
    key_heads = new_kv.shape[1] // (2 * HEAD_DIM)
    rows = columns // HEAD_DIM // key_heads * tokens
    chunks = 4
    operands = [queries, new_kv, kv_cache, residual, routes.T, router, norm_gain, weight]
    operands = [pltpu.with_memory_space_constraint(x, pltpu.HBM) for x in operands]
    kept = [pltpu.VMEM(x.shape, x.dtype) for x in operands[:-1]]
    kept[2] = pltpu.VMEM((slots, width), kv_cache.dtype)
    return pl.pallas_call(
        functools.partial(attention_kernel, chunks=chunks, rest=rest),
        out_shape=(
            jax.ShapeDtypeStruct((tokens, columns + 2 * LANES), jnp.bfloat16),
            pltpu.VMEM((rest.size, weight.shape[2]), weight.dtype),
        ),
        in_specs=[pl.BlockSpec(memory_space=pltpu.SMEM)]
        + [pl.BlockSpec(memory_space=pl.ANY)] * len(operands),
        out_specs=(pl.BlockSpec(memory_space=pltpu.VMEM),) * 2,
        scratch_shapes=kept
        + [
            pltpu.VMEM((key_heads, rows, slots), jnp.float32),
            pltpu.SemaphoreType.DMA((chunks + len(operands) - 2,)),
            pltpu.SemaphoreType.DMA((CHUNKS,)),
        ],
        compiler_params=pltpu.CompilerParams(vmem_limit_bytes=8 * MIB),
        cost_estimate=pl.CostEstimate(
            flops=4 * rows * slots * HEAD_DIM * key_heads,
            bytes_accessed=slots * width * 2,
            transcendentals=rows * slots * key_heads,
        ),
        name="attention",
    )(cache_len, *operands)


def load_kernel(_, source, out_ref, token_ref, sems, *, part):
    copies = start_load(source, out_ref, part, sems)
    token_ref[...] = jnp.zeros_like(token_ref)
    for copy in copies:
        copy.wait()


def load(after, weight, part):
    shape = (part.size, weight.shape[2])
    return pl.pallas_call(
        functools.partial(load_kernel, part=part),
        out_shape=(pltpu.VMEM(shape, weight.dtype), jax.ShapeDtypeStruct((8, LANES), jnp.float32)),
        in_specs=[pl.BlockSpec(memory_space=pl.ANY)] * 2,
        out_specs=(pl.BlockSpec(memory_space=pltpu.VMEM),) * 2,
        scratch_shapes=[pltpu.SemaphoreType.DMA((CHUNKS,))],
        compiler_params=pltpu.CompilerParams(vmem_limit_bytes=MIB),
        cost_estimate=pl.CostEstimate(flops=0, bytes_accessed=4 * shape[0] * shape[1], transcendentals=0),
        name="load",
    )(after, pltpu.with_memory_space_constraint(weight, pltpu.HBM))


def norm_kernel(place_ref, _, *refs, experts):
    pieces, out_ref = refs[:-1], refs[-1]
    tokens, wide = pieces[0].shape
    block = wide - 2 * LANES
    model = len(pieces) * block
    total = jnp.zeros((tokens, LANES), jnp.float32)
    for piece in pieces:
        total = total + piece[:, block : block + LANES].astype(jnp.float32)
    sums = total + pltpu.roll(total, LANES - SLOT, 1) + pltpu.roll(total, LANES - 2 * SLOT, 1)
    mean = sums[:, experts : experts + 1] / model
    variance = sums[:, experts + 1 : experts + 2] / model - mean * mean
    inv = lax.rsqrt(variance + NORM_EPS)
    plain = pltpu.roll(sums, LANES - experts - 2, 1)
    logits = (sums - mean * plain) * inv
    lane = lax.broadcasted_iota(jnp.int32, (tokens, LANES), 1)
    named = (pltpu.roll(total, LANES - MASK_AT, 1) > 0) & (lane < experts)
    raised = jnp.where(named, jnp.exp(logits), 0.0)
    share = raised / jnp.sum(raised, axis=1, keepdims=True)
    high = share.astype(jnp.bfloat16).astype(jnp.float32)
    side = high + pltpu.roll(share - high, experts, 1)
    out_ref[:, model:] = side.astype(out_ref.dtype)
    for mask, piece in enumerate(reversed(pieces)):
        gain = piece[:, block + LANES :].astype(jnp.float32)
        gain = jnp.concatenate([gain[j : j + 1, :] for j in range(block // LANES)], axis=1)
        x = (piece[:, :block].astype(jnp.float32) - mean) * inv * gain
        at = pl.multiple_of(lax.bitwise_xor(place_ref[0], mask) * block, block)
        out_ref[:, pl.ds(at, block)] = x.astype(out_ref.dtype)


def norm_rows(place, token, blocks, experts):
    tokens, wide = blocks[0].shape
    model = (wide - 2 * LANES) * len(blocks)
    vmem = pl.BlockSpec(memory_space=pltpu.VMEM)
    return pl.pallas_call(
        functools.partial(norm_kernel, experts=experts),
        out_shape=jax.ShapeDtypeStruct((tokens, model + LANES), jnp.bfloat16),
        in_specs=[pl.BlockSpec(memory_space=pltpu.SMEM)] + [vmem] * (1 + len(blocks)),
        out_specs=vmem,
        compiler_params=pltpu.CompilerParams(vmem_limit_bytes=4 * MIB),
        name="norm",
    )(place, token, *blocks)


def stack_kernel(_, *refs):
    pieces, out_ref = refs[:-1][::-1], refs[-1]
    rows = 2 * pieces[0].shape[0]
    for i in range(0, len(pieces), 2):
        pair = [piece[...].astype(jnp.float32) for piece in pieces[i : i + 2]]
        out_ref[i // 2 * rows : (i // 2 + 1) * rows] = jnp.concatenate(pair, axis=0).astype(out_ref.dtype)


def stack_rows(token, pieces):
    rows, wide = pieces[0].shape
    vmem = pl.BlockSpec(memory_space=pltpu.VMEM)
    return pl.pallas_call(
        stack_kernel,
        out_shape=jax.ShapeDtypeStruct((rows * len(pieces), wide), pieces[0].dtype),
        in_specs=[vmem] * (1 + len(pieces)),
        out_specs=vmem,
        compiler_params=pltpu.CompilerParams(vmem_limit_bytes=4 * MIB),
        name="stack",
    )(token, *pieces)


def hidden_kernel(
    place_ref, near, far, gate_a, gate_c, up_a, gate_hbm, up_hbm, hidden, x, gate_b, up_b, up_c, sems, *, experts, parts
):
    loads = [
        start_load(source, target, part, sems.at[i])
        for i, (source, target, part) in enumerate(
            ((up_hbm, up_c, parts[2]), (gate_hbm, gate_b, parts[1]), (up_hbm, up_b, parts[1]))
        )
    ]
    model = gate_a.shape[1]
    step = 2 * LANES
    for at in range(0, model, step):
        both = [ref[:, at : at + step].astype(jnp.float32) for ref in (near, far)]
        x[at : at + step] = jnp.concatenate(both, axis=0).T.astype(x.dtype)
    side = jnp.concatenate([ref[:, model:].astype(jnp.float32) for ref in (near, far)], axis=0).T
    at = lax.broadcasted_iota(jnp.int32, side.shape, 0)
    expert = place_ref[1]
    mine = (at == expert) | (at == expert + experts)
    share = jnp.sum(jnp.where(mine, side, 0.0), axis=0, keepdims=True)
    work = (
        (parts[0], gate_a, up_a, []),
        (parts[2], gate_c, up_c, loads[0]),
        (parts[1], gate_b, up_b, loads[1] + loads[2]),
    )
    for part, gate, up, copies in work:
        for copy in copies:
            copy.wait()
        for at in range(0, part.size, UNITS):
            end = min(at + UNITS, part.size)
            a = jnp.dot(gate[at:end], x[...], preferred_element_type=jnp.float32)
            b = jnp.dot(up[at:end], x[...], preferred_element_type=jnp.float32)
            out = a / (1.0 + jnp.exp(-a)) * b * share
            hidden[:, part.start + at : part.start + end] = out.T.astype(hidden.dtype)


def run_hidden(place, near, far, gate_a, gate_c, up_a, gate_w, up_w, parts, experts):
    units, model = up_w.shape[1:]
    rows = 2 * near.shape[0]
    vmem = pl.BlockSpec(memory_space=pltpu.VMEM)
    return pl.pallas_call(
        functools.partial(hidden_kernel, experts=experts, parts=parts),
        out_shape=jax.ShapeDtypeStruct((rows, units), jnp.bfloat16),
        in_specs=[pl.BlockSpec(memory_space=pltpu.SMEM)]
        + [vmem] * 5
        + [pl.BlockSpec(memory_space=pl.ANY)] * 2,
        out_specs=vmem,
        scratch_shapes=[
            pltpu.VMEM((model, rows), jnp.bfloat16),
            pltpu.VMEM((parts[1].size, model), gate_w.dtype),
            pltpu.VMEM((parts[1].size, model), up_w.dtype),
            pltpu.VMEM((parts[2].size, model), up_w.dtype),
            pltpu.SemaphoreType.DMA((3, CHUNKS)),
        ],
        compiler_params=pltpu.CompilerParams(vmem_limit_bytes=(12 if rows <= 64 else 24) * MIB),
        cost_estimate=pl.CostEstimate(
            flops=4 * rows * units * model, bytes_accessed=4 * units * model, transcendentals=rows * units
        ),
        name="hidden",
    )(place, near, far, gate_a, gate_c, up_a, *[pltpu.with_memory_space_constraint(w, pltpu.HBM) for w in (gate_w, up_w)])


def send(x, axis, mask):
    return lax.ppermute(x, axis, [(i, i ^ mask) for i in range(lax.axis_size(axis))])


def exchange(parts, axis):
    return [send(parts[m], axis, m) for m in reversed(range(1, lax.axis_size(axis)))]


def add(*terms):
    return sum(t.astype(jnp.float32) for t in terms)


def per_device(
    queries, new_kv, kv_cache, cache_len, residual, norm_gain, router, routes, gate_w, up_w, down_w
):
    sections, groups, tensors = (lax.axis_size(a) for a in ("section", "group", "tensor"))
    experts, block = router.shape
    tokens = queries.shape[0]
    place = lax.axis_index("tensor")
    where = jnp.stack([place, lax.axis_index("section") * tensors + place]).astype(jnp.int32)

    parts = unit_parts(gate_w.shape[1])

    fresh, gate_c = attend(
        cache_len, queries, new_kv, kv_cache, residual, routes, router, norm_gain, gate_w, parts[2]
    )
    blocks = exchange([fresh] * tensors, "tensor") + [fresh]
    gate_a, token = load(fresh, gate_w, parts[0])
    rows = norm_rows(where, token, blocks, experts)
    ranks = exchange([rows] * groups, "group") + [rows]
    up_a, token = load(rows, up_w, parts[0])
    near = stack_rows(token, ranks)
    far = send(near, "section", 1)

    hidden = run_hidden(where, near, far, gate_a, gate_c, up_a, gate_w, up_w, parts, experts)
    out = jnp.dot(hidden, down_w[0], preferred_element_type=jnp.float32).astype(jnp.bfloat16)
    half = out.shape[0] // 2
    both = add(out[:half], send(out[half:], "section", 1)).astype(jnp.bfloat16)
    both = both.reshape(groups, tokens, -1)
    got = add(*exchange(both, "group"), both[0]).astype(jnp.bfloat16)
    pieces = [lax.dynamic_slice_in_dim(got, (place ^ m) * block, block, axis=1) for m in range(tensors)]
    mixed = add(*exchange(pieces, "tensor"), pieces[0], fresh[:, :block])
    return mixed.astype(jnp.bfloat16)


def solution(mesh):
    rows = P(("section", "group"), "tensor")
    weights = P(("section", "tensor"), "group", None)
    in_specs = (
        rows,
        rows,
        P(("section", "group"), None, "tensor"),
        P(("section", "group")),
        rows,
        P("tensor"),
        P(None, "tensor"),
        P(("section", "group"), None),
        weights,
        weights,
        weights,
    )
    return jax.shard_map(per_device, mesh=mesh, in_specs=in_specs, out_specs=rows, check_vma=False)
```

```python
import functools

import jax
import jax.numpy as jnp
from jax import lax
from jax.experimental import pallas as pl
from jax.experimental.pallas import tpu as pltpu
from jax.sharding import PartitionSpec as P

HEAD_DIM = 128
NORM_EPS = 1e-05
LANES = 128
SLOT = 36
MASK_AT = 3 * SLOT
MIB = 1 << 20
CHUNKS = 4
UNITS = 256
BY_ROW = (((1,), (1,)), ((), ()))


def split_terms(value):
    high = value.astype(jnp.bfloat16).astype(jnp.float32)
    rest = value - high
    middle = rest.astype(jnp.bfloat16).astype(jnp.float32)
    return high, middle, rest - middle


def cut_units(units):
    if units <= 7 * UNITS // 2:
        return units // 32 * 16, units // 32 * 16
    return units * 3 // 4 // UNITS * UNITS, units - UNITS


def unit_parts(units, cut):
    return pl.ds(0, cut), pl.ds(cut, units - cut)


def start_load(source, target, part, sems):
    count = max(c for c in range(1, CHUNKS + 1) if part.size % (16 * c) == 0 or c == 1)
    step = part.size // count
    copies = [
        pltpu.make_async_copy(
            source.at[0, pl.ds(part.start + i * step, step)], target.at[pl.ds(i * step, step)], sems.at[i]
        )
        for i in range(count)
    ]
    for copy in copies:
        copy.start()
    return copies


def attention_kernel(
    len_ref,
    q_hbm,
    new_hbm,
    kv_hbm,
    res_hbm,
    routes_hbm,
    router_hbm,
    gain_hbm,
    weight_hbm,
    out_ref,
    weight_ref,
    q_ref,
    new_ref,
    kv,
    res_ref,
    routes_ref,
    router_ref,
    gain_ref,
    scores,
    sems,
    weight_sems,
    *,
    chunks,
    rest,
):
    slots = kv_hbm.shape[1]
    part = slots // chunks
    sources = [q_hbm, new_hbm] + [kv_hbm.at[0, pl.ds(c * part, part)] for c in range(chunks)]
    targets = [q_ref, new_ref] + [kv.at[pl.ds(c * part, part)] for c in range(chunks)]
    sources += [res_hbm, routes_hbm, router_hbm, gain_hbm]
    targets += [res_ref, routes_ref, router_ref, gain_ref]
    copies = [pltpu.make_async_copy(a, b, sems.at[i]) for i, (a, b) in enumerate(zip(sources, targets))]
    for copy in copies:
        copy.start()
    loads = start_load(weight_hbm, weight_ref, rest, weight_sems)
    tokens, columns = q_ref.shape
    key_heads = new_ref.shape[1] // (2 * HEAD_DIM)
    grouped = columns // HEAD_DIM // key_heads
    rows = grouped * tokens
    scale = HEAD_DIM ** (-0.5)
    copies[0].wait()
    copies[1].wait()
    queries, selves = [], []
    for h in range(key_heads):
        first = h * grouped * HEAD_DIM
        q = jnp.concatenate(
            [
                q_ref[:, first + j * HEAD_DIM : first + (j + 1) * HEAD_DIM].astype(jnp.float32)
                for j in range(grouped)
            ],
            axis=0,
        )
        own_key = new_ref[:, 2 * h * HEAD_DIM : (2 * h + 1) * HEAD_DIM].astype(jnp.float32)
        own_key = jnp.concatenate([own_key] * grouped, axis=0)
        selves.append(jnp.sum(q * own_key, axis=1, keepdims=True) * scale)
        queries.append(q.astype(jnp.bfloat16))
    live = len_ref[0]
    for c in range(chunks):
        copies[2 + c].wait()
        for h in range(key_heads):
            keys = kv[c * part : (c + 1) * part, 2 * h * HEAD_DIM : (2 * h + 1) * HEAD_DIM]
            s = lax.dot_general(queries[h], keys, BY_ROW, preferred_element_type=jnp.float32)
            at = lax.broadcasted_iota(jnp.int32, (rows, part), 1) + c * part
            scores[h, :, c * part : (c + 1) * part] = jnp.where(at < live, s * scale, -jnp.inf)
    for copy in copies[2 + chunks :]:
        copy.wait()

    experts = router_ref.shape[0]
    routes = routes_ref[...]
    expert_at = lax.broadcasted_iota(jnp.int32, (LANES, tokens), 0) - MASK_AT
    named = jnp.zeros((LANES, tokens), jnp.float32)
    for k in range(routes.shape[0]):
        named = jnp.where(expert_at == routes[k : k + 1, :], 1.0, named)
    side = named.T

    streams = []
    for h in range(key_heads):
        s = scores[h]
        top = jnp.maximum(jnp.max(s, axis=1, keepdims=True), selves[h])
        weights = jnp.exp(s - top).astype(jnp.bfloat16)
        own = jnp.exp(selves[h] - top).astype(jnp.bfloat16).astype(jnp.float32)
        total = jnp.sum(weights.astype(jnp.float32), axis=1, keepdims=True) + own
        value_at = (2 * h + 1) * HEAD_DIM
        mixed = jnp.dot(weights, kv[:, value_at : value_at + HEAD_DIM], preferred_element_type=jnp.float32)
        own_value = new_ref[:, value_at : value_at + HEAD_DIM].astype(jnp.float32)
        mixed = (mixed + own * jnp.concatenate([own_value] * grouped, axis=0)) / total
        for j in range(grouped):
            at = (h * grouped + j) * HEAD_DIM
            got = res_ref[:, at : at + HEAD_DIM].astype(jnp.float32) + mixed[j * tokens : (j + 1) * tokens]
            got = got.astype(jnp.bfloat16)
            out_ref[:, at : at + HEAD_DIM] = got
            streams.append(got.astype(jnp.float32))

    lane = lax.broadcasted_iota(jnp.int32, (tokens, LANES), 1)
    sums = jnp.zeros((tokens, LANES), jnp.float32)

    def put(sums, at, pieces):
        total = pieces[0]
        for piece in pieces[1:]:
            total = total + piece
        return jnp.where(lane == at, jnp.sum(total, axis=1, keepdims=True), sums)

    blocks = range(len(streams))
    sums = put(sums, experts, streams)
    sums = put(sums, experts + 1, [x * x for x in streams])
    gain = gain_ref[...].astype(jnp.float32).reshape(1, -1)
    gains = [gain[:, b * HEAD_DIM : (b + 1) * HEAD_DIM] for b in blocks]
    scaled = [x * g for x, g in zip(streams, gains)]
    for e in range(experts):
        weights = [router_ref[e : e + 1, b * HEAD_DIM : (b + 1) * HEAD_DIM].astype(jnp.float32) for b in blocks]
        sums = put(sums, e, [x * w for x, w in zip(scaled, weights)])
        plain = [jnp.broadcast_to(g * w, (tokens, HEAD_DIM)) for g, w in zip(gains, weights)]
        sums = put(sums, experts + 2 + e, plain)
    for i, term in enumerate(split_terms(sums)):
        side = side + (pltpu.roll(term, i * SLOT, 1) if i else term)
    out_ref[:, columns : columns + LANES] = side.astype(out_ref.dtype)
    gain_rows = jnp.concatenate(
        gains + [jnp.zeros((1, LANES), jnp.float32)] * (tokens - len(gains)), axis=0
    )
    out_ref[:, columns + LANES :] = gain_rows.astype(out_ref.dtype)
    for copy in loads:
        copy.wait()


def attend(cache_len, queries, new_kv, kv_cache, residual, routes, router, norm_gain, weight, rest):
    tokens, columns = queries.shape
    slots, width = kv_cache.shape[1:]
    key_heads = new_kv.shape[1] // (2 * HEAD_DIM)
    rows = columns // HEAD_DIM // key_heads * tokens
    chunks = 4
    operands = [queries, new_kv, kv_cache, residual, routes.T, router, norm_gain, weight]
    operands = [pltpu.with_memory_space_constraint(x, pltpu.HBM) for x in operands]
    kept = [pltpu.VMEM(x.shape, x.dtype) for x in operands[:-1]]
    kept[2] = pltpu.VMEM((slots, width), kv_cache.dtype)
    return pl.pallas_call(
        functools.partial(attention_kernel, chunks=chunks, rest=rest),
        out_shape=(
            jax.ShapeDtypeStruct((tokens, columns + 2 * LANES), jnp.bfloat16),
            pltpu.VMEM((rest.size, weight.shape[2]), weight.dtype),
        ),
        in_specs=[pl.BlockSpec(memory_space=pltpu.SMEM)]
        + [pl.BlockSpec(memory_space=pl.ANY)] * len(operands),
        out_specs=(pl.BlockSpec(memory_space=pltpu.VMEM),) * 2,
        scratch_shapes=kept
        + [
            pltpu.VMEM((key_heads, rows, slots), jnp.float32),
            pltpu.SemaphoreType.DMA((chunks + len(operands) - 2,)),
            pltpu.SemaphoreType.DMA((CHUNKS,)),
        ],
        compiler_params=pltpu.CompilerParams(vmem_limit_bytes=8 * MIB),
        cost_estimate=pl.CostEstimate(
            flops=4 * rows * slots * HEAD_DIM * key_heads,
            bytes_accessed=slots * width * 2,
            transcendentals=rows * slots * key_heads,
        ),
        name="attention",
    )(cache_len, *operands)


def load_kernel(_, source, out_ref, token_ref, sems, *, part):
    copies = start_load(source, out_ref, part, sems)
    token_ref[...] = jnp.zeros_like(token_ref)
    for copy in copies:
        copy.wait()


def load(after, weight, part):
    shape = (part.size, weight.shape[2])
    return pl.pallas_call(
        functools.partial(load_kernel, part=part),
        out_shape=(pltpu.VMEM(shape, weight.dtype), jax.ShapeDtypeStruct((8, LANES), jnp.float32)),
        in_specs=[pl.BlockSpec(memory_space=pl.ANY)] * 2,
        out_specs=(pl.BlockSpec(memory_space=pltpu.VMEM),) * 2,
        scratch_shapes=[pltpu.SemaphoreType.DMA((CHUNKS,))],
        compiler_params=pltpu.CompilerParams(vmem_limit_bytes=MIB),
        cost_estimate=pl.CostEstimate(flops=0, bytes_accessed=4 * shape[0] * shape[1], transcendentals=0),
        name="load",
    )(after, pltpu.with_memory_space_constraint(weight, pltpu.HBM))


def norm_kernel(place_ref, _, *refs, experts):
    pieces, out_ref = refs[:-1], refs[-1]
    tokens, wide = pieces[0].shape
    block = wide - 2 * LANES
    model = len(pieces) * block
    total = jnp.zeros((tokens, LANES), jnp.float32)
    for piece in pieces:
        total = total + piece[:, block : block + LANES].astype(jnp.float32)
    sums = total + pltpu.roll(total, LANES - SLOT, 1) + pltpu.roll(total, LANES - 2 * SLOT, 1)
    mean = sums[:, experts : experts + 1] / model
    variance = sums[:, experts + 1 : experts + 2] / model - mean * mean
    inv = lax.rsqrt(variance + NORM_EPS)
    plain = pltpu.roll(sums, LANES - experts - 2, 1)
    logits = (sums - mean * plain) * inv
    lane = lax.broadcasted_iota(jnp.int32, (tokens, LANES), 1)
    named = (pltpu.roll(total, LANES - MASK_AT, 1) > 0) & (lane < experts)
    raised = jnp.where(named, jnp.exp(logits), 0.0)
    share = raised / jnp.sum(raised, axis=1, keepdims=True)
    high = share.astype(jnp.bfloat16).astype(jnp.float32)
    side = high + pltpu.roll(share - high, experts, 1)
    out_ref[:, model:] = side.astype(out_ref.dtype)
    for mask, piece in enumerate(reversed(pieces)):
        gain = piece[:, block + LANES :].astype(jnp.float32)
        gain = jnp.concatenate([gain[j : j + 1, :] for j in range(block // LANES)], axis=1)
        x = (piece[:, :block].astype(jnp.float32) - mean) * inv * gain
        at = pl.multiple_of(lax.bitwise_xor(place_ref[0], mask) * block, block)
        out_ref[:, pl.ds(at, block)] = x.astype(out_ref.dtype)


def norm_rows(place, token, blocks, experts):
    tokens, wide = blocks[0].shape
    model = (wide - 2 * LANES) * len(blocks)
    vmem = pl.BlockSpec(memory_space=pltpu.VMEM)
    return pl.pallas_call(
        functools.partial(norm_kernel, experts=experts),
        out_shape=jax.ShapeDtypeStruct((tokens, model + LANES), jnp.bfloat16),
        in_specs=[pl.BlockSpec(memory_space=pltpu.SMEM)] + [vmem] * (1 + len(blocks)),
        out_specs=vmem,
        compiler_params=pltpu.CompilerParams(vmem_limit_bytes=4 * MIB),
        name="norm",
    )(place, token, *blocks)


def stack_kernel(_, *refs):
    pieces, out_ref = refs[:-1][::-1], refs[-1]
    rows = 2 * pieces[0].shape[0]
    for i in range(0, len(pieces), 2):
        pair = [piece[...].astype(jnp.float32) for piece in pieces[i : i + 2]]
        out_ref[i // 2 * rows : (i // 2 + 1) * rows] = jnp.concatenate(pair, axis=0).astype(out_ref.dtype)


def stack_rows(token, pieces):
    rows, wide = pieces[0].shape
    vmem = pl.BlockSpec(memory_space=pltpu.VMEM)
    return pl.pallas_call(
        stack_kernel,
        out_shape=jax.ShapeDtypeStruct((rows * len(pieces), wide), pieces[0].dtype),
        in_specs=[vmem] * (1 + len(pieces)),
        out_specs=vmem,
        compiler_params=pltpu.CompilerParams(vmem_limit_bytes=4 * MIB),
        name="stack",
    )(token, *pieces)


def hidden_kernel(place_ref, near, far, gate_a, gate_b, up_a, up_b, _, hidden, x, *, experts):
    half = near.shape[0]
    model = gate_a.shape[1]
    x[:half] = near[:, :model]
    x[half:] = far[:, :model]
    side = jnp.concatenate([ref[:, model:].astype(jnp.float32) for ref in (near, far)], axis=0).T
    at = lax.broadcasted_iota(jnp.int32, side.shape, 0)
    expert = place_ref[1]
    mine = (at == expert) | (at == expert + experts)
    share = jnp.sum(jnp.where(mine, side, 0.0), axis=0, keepdims=True)
    units = gate_a.shape[0] + gate_b.shape[0]
    cuts = sorted({0, gate_a.shape[0], up_a.shape[0], units})

    def times(first, second, start, stop):
        cut = first.shape[0]
        block = first[start:stop] if stop <= cut else second[start - cut : stop - cut]
        return lax.dot_general(block, x[...], BY_ROW, preferred_element_type=jnp.float32)

    for low, high in zip(cuts, cuts[1:]):
        for start in range(low, high, UNITS):
            stop = min(start + UNITS, high)
            a = times(gate_a, gate_b, start, stop)
            b = times(up_a, up_b, start, stop)
            out = a / (1.0 + jnp.exp(-a)) * b * share
            hidden[:, start:stop] = out.T.astype(hidden.dtype)


def run_hidden(place, near, far, weights, token, experts):
    units = weights[0].shape[0] + weights[1].shape[0]
    model = weights[0].shape[1]
    rows = 2 * near.shape[0]
    vmem = pl.BlockSpec(memory_space=pltpu.VMEM)
    return pl.pallas_call(
        functools.partial(hidden_kernel, experts=experts),
        out_shape=jax.ShapeDtypeStruct((rows, units), jnp.bfloat16),
        in_specs=[pl.BlockSpec(memory_space=pltpu.SMEM)] + [vmem] * 7,
        out_specs=vmem,
        scratch_shapes=[pltpu.VMEM((rows, model), jnp.bfloat16)],
        compiler_params=pltpu.CompilerParams(vmem_limit_bytes=(6 if rows <= 64 else 24) * MIB),
        cost_estimate=pl.CostEstimate(
            flops=4 * rows * units * model, bytes_accessed=4 * units * model, transcendentals=rows * units
        ),
        name="hidden",
    )(place, near, far, *weights, token)


def send(x, axis, mask):
    return lax.ppermute(x, axis, [(i, i ^ mask) for i in range(lax.axis_size(axis))])


def exchange(parts, axis):
    return [send(parts[m], axis, m) for m in reversed(range(1, lax.axis_size(axis)))]


def add(*terms):
    return sum(t.astype(jnp.float32) for t in terms)


def per_device(
    queries, new_kv, kv_cache, cache_len, residual, norm_gain, router, routes, gate_w, up_w, down_w
):
    sections, groups, tensors = (lax.axis_size(a) for a in ("section", "group", "tensor"))
    experts, block = router.shape
    tokens = queries.shape[0]
    place = lax.axis_index("tensor")
    where = jnp.stack([place, lax.axis_index("section") * tensors + place]).astype(jnp.int32)

    units = gate_w.shape[1]
    gate_parts, up_parts = [unit_parts(units, cut) for cut in cut_units(units)]

    fresh, gate_b = attend(
        cache_len, queries, new_kv, kv_cache, residual, routes, router, norm_gain, gate_w, gate_parts[1]
    )
    blocks = exchange([fresh] * tensors, "tensor") + [fresh]
    gate_a, token = load(fresh, gate_w, gate_parts[0])
    rows = norm_rows(where, token, blocks, experts)
    ranks = exchange([rows] * groups, "group") + [rows]
    up_a, token = load(rows, up_w, up_parts[0])
    near = stack_rows(token, ranks)
    far = send(near, "section", 1)
    up_b, token = load(near, up_w, up_parts[1])

    hidden = run_hidden(where, near, far, (gate_a, gate_b, up_a, up_b), token, experts)
    out = jnp.dot(hidden, down_w[0], preferred_element_type=jnp.float32).astype(jnp.bfloat16)
    half = out.shape[0] // 2
    both = add(out[:half], send(out[half:], "section", 1)).astype(jnp.bfloat16)
    both = both.reshape(groups, tokens, -1)
    got = add(*exchange(both, "group"), both[0]).astype(jnp.bfloat16)
    parts = [lax.dynamic_slice_in_dim(got, (place ^ m) * block, block, axis=1) for m in range(tensors)]
    mixed = add(*exchange(parts, "tensor"), parts[0], fresh[:, :block])
    return mixed.astype(jnp.bfloat16)


def solution(mesh):
    rows = P(("section", "group"), "tensor")
    weights = P(("section", "tensor"), "group", None)
    in_specs = (
        rows,
        rows,
        P(("section", "group"), None, "tensor"),
        P(("section", "group")),
        rows,
        P("tensor"),
        P(None, "tensor"),
        P(("section", "group"), None),
        weights,
        weights,
        weights,
    )
    return jax.shard_map(per_device, mesh=mesh, in_specs=in_specs, out_specs=rows, check_vma=False)
```

```python
import functools

import jax
import jax.numpy as jnp
from jax import lax
from jax.experimental import pallas as pl
from jax.experimental.pallas import tpu as pltpu
from jax.sharding import PartitionSpec as P

HEAD_DIM = 128
NORM_EPS = 1e-05
LANES = 128
SLOT = 36
MASK_AT = 3 * SLOT
MIB = 1 << 20
CHUNKS = 4
UNITS = 256
STREAM = 640
BY_ROW = (((1,), (1,)), ((), ()))


def split_terms(value):
    high = value.astype(jnp.bfloat16).astype(jnp.float32)
    rest = value - high
    middle = rest.astype(jnp.bfloat16).astype(jnp.float32)
    return high, middle, rest - middle


def cut_units(units):
    if units <= 7 * UNITS // 2:
        return units // 32 * 16, units // 32 * 16
    return units * 3 // 4 // UNITS * UNITS, units - UNITS


def unit_parts(units, cut):
    return pl.ds(0, cut), pl.ds(cut, units - cut)


def start_load(source, target, part, sems):
    count = max(c for c in range(1, CHUNKS + 1) if part.size % (16 * c) == 0 or c == 1)
    step = part.size // count
    copies = [
        pltpu.make_async_copy(
            source.at[0, pl.ds(part.start + i * step, step)], target.at[pl.ds(i * step, step)], sems.at[i]
        )
        for i in range(count)
    ]
    for copy in copies:
        copy.start()
    return copies


def attention_kernel(
    len_ref,
    q_hbm,
    new_hbm,
    kv_hbm,
    res_hbm,
    routes_hbm,
    router_hbm,
    gain_hbm,
    weight_hbm,
    out_ref,
    weight_ref,
    q_ref,
    new_ref,
    kv,
    res_ref,
    routes_ref,
    router_ref,
    gain_ref,
    scores,
    sems,
    weight_sems,
    *,
    chunks,
    rest,
):
    slots = kv_hbm.shape[1]
    part = slots // chunks
    sources = [q_hbm, new_hbm] + [kv_hbm.at[0, pl.ds(c * part, part)] for c in range(chunks)]
    targets = [q_ref, new_ref] + [kv.at[pl.ds(c * part, part)] for c in range(chunks)]
    sources += [res_hbm, routes_hbm, router_hbm, gain_hbm]
    targets += [res_ref, routes_ref, router_ref, gain_ref]
    copies = [pltpu.make_async_copy(a, b, sems.at[i]) for i, (a, b) in enumerate(zip(sources, targets))]
    for copy in copies:
        copy.start()
    loads = start_load(weight_hbm, weight_ref, rest, weight_sems)
    tokens, columns = q_ref.shape
    key_heads = new_ref.shape[1] // (2 * HEAD_DIM)
    grouped = columns // HEAD_DIM // key_heads
    rows = grouped * tokens
    scale = HEAD_DIM ** (-0.5)
    copies[0].wait()
    copies[1].wait()
    queries, selves = [], []
    for h in range(key_heads):
        first = h * grouped * HEAD_DIM
        q = jnp.concatenate(
            [
                q_ref[:, first + j * HEAD_DIM : first + (j + 1) * HEAD_DIM].astype(jnp.float32)
                for j in range(grouped)
            ],
            axis=0,
        )
        own_key = new_ref[:, 2 * h * HEAD_DIM : (2 * h + 1) * HEAD_DIM].astype(jnp.float32)
        own_key = jnp.concatenate([own_key] * grouped, axis=0)
        selves.append(jnp.sum(q * own_key, axis=1, keepdims=True) * scale)
        queries.append(q.astype(jnp.bfloat16))
    live = len_ref[0]
    for c in range(chunks):
        copies[2 + c].wait()
        for h in range(key_heads):
            keys = kv[c * part : (c + 1) * part, 2 * h * HEAD_DIM : (2 * h + 1) * HEAD_DIM]
            s = lax.dot_general(queries[h], keys, BY_ROW, preferred_element_type=jnp.float32)
            at = lax.broadcasted_iota(jnp.int32, (rows, part), 1) + c * part
            scores[h, :, c * part : (c + 1) * part] = jnp.where(at < live, s * scale, -jnp.inf)
    for copy in copies[2 + chunks :]:
        copy.wait()

    experts = router_ref.shape[0]
    routes = routes_ref[...]
    expert_at = lax.broadcasted_iota(jnp.int32, (LANES, tokens), 0) - MASK_AT
    named = jnp.zeros((LANES, tokens), jnp.float32)
    for k in range(routes.shape[0]):
        named = jnp.where(expert_at == routes[k : k + 1, :], 1.0, named)
    side = named.T

    streams = []
    for h in range(key_heads):
        s = scores[h]
        top = jnp.maximum(jnp.max(s, axis=1, keepdims=True), selves[h])
        weights = jnp.exp(s - top).astype(jnp.bfloat16)
        own = jnp.exp(selves[h] - top).astype(jnp.bfloat16).astype(jnp.float32)
        total = jnp.sum(weights.astype(jnp.float32), axis=1, keepdims=True) + own
        value_at = (2 * h + 1) * HEAD_DIM
        mixed = jnp.dot(weights, kv[:, value_at : value_at + HEAD_DIM], preferred_element_type=jnp.float32)
        own_value = new_ref[:, value_at : value_at + HEAD_DIM].astype(jnp.float32)
        mixed = (mixed + own * jnp.concatenate([own_value] * grouped, axis=0)) / total
        for j in range(grouped):
            at = (h * grouped + j) * HEAD_DIM
            got = res_ref[:, at : at + HEAD_DIM].astype(jnp.float32) + mixed[j * tokens : (j + 1) * tokens]
            got = got.astype(jnp.bfloat16)
            out_ref[:, at : at + HEAD_DIM] = got
            streams.append(got.astype(jnp.float32))

    lane = lax.broadcasted_iota(jnp.int32, (tokens, LANES), 1)
    sums = jnp.zeros((tokens, LANES), jnp.float32)

    def put(sums, at, pieces):
        total = pieces[0]
        for piece in pieces[1:]:
            total = total + piece
        return jnp.where(lane == at, jnp.sum(total, axis=1, keepdims=True), sums)

    blocks = range(len(streams))
    sums = put(sums, experts, streams)
    sums = put(sums, experts + 1, [x * x for x in streams])
    gain = gain_ref[...].astype(jnp.float32).reshape(1, -1)
    gains = [gain[:, b * HEAD_DIM : (b + 1) * HEAD_DIM] for b in blocks]
    scaled = [x * g for x, g in zip(streams, gains)]
    for e in range(experts):
        weights = [router_ref[e : e + 1, b * HEAD_DIM : (b + 1) * HEAD_DIM].astype(jnp.float32) for b in blocks]
        sums = put(sums, e, [x * w for x, w in zip(scaled, weights)])
        plain = [jnp.broadcast_to(g * w, (tokens, HEAD_DIM)) for g, w in zip(gains, weights)]
        sums = put(sums, experts + 2 + e, plain)
    for i, term in enumerate(split_terms(sums)):
        side = side + (pltpu.roll(term, i * SLOT, 1) if i else term)
    out_ref[:, columns : columns + LANES] = side.astype(out_ref.dtype)
    gain_rows = jnp.concatenate(
        gains + [jnp.zeros((1, LANES), jnp.float32)] * (tokens - len(gains)), axis=0
    )
    out_ref[:, columns + LANES :] = gain_rows.astype(out_ref.dtype)
    for copy in loads:
        copy.wait()


def attend(cache_len, queries, new_kv, kv_cache, residual, routes, router, norm_gain, weight, rest):
    tokens, columns = queries.shape
    slots, width = kv_cache.shape[1:]
    key_heads = new_kv.shape[1] // (2 * HEAD_DIM)
    rows = columns // HEAD_DIM // key_heads * tokens
    chunks = 4
    operands = [queries, new_kv, kv_cache, residual, routes.T, router, norm_gain, weight]
    operands = [pltpu.with_memory_space_constraint(x, pltpu.HBM) for x in operands]
    kept = [pltpu.VMEM(x.shape, x.dtype) for x in operands[:-1]]
    kept[2] = pltpu.VMEM((slots, width), kv_cache.dtype)
    return pl.pallas_call(
        functools.partial(attention_kernel, chunks=chunks, rest=rest),
        out_shape=(
            jax.ShapeDtypeStruct((tokens, columns + 2 * LANES), jnp.bfloat16),
            pltpu.VMEM((rest.size, weight.shape[2]), weight.dtype),
        ),
        in_specs=[pl.BlockSpec(memory_space=pltpu.SMEM)]
        + [pl.BlockSpec(memory_space=pl.ANY)] * len(operands),
        out_specs=(pl.BlockSpec(memory_space=pltpu.VMEM),) * 2,
        scratch_shapes=kept
        + [
            pltpu.VMEM((key_heads, rows, slots), jnp.float32),
            pltpu.SemaphoreType.DMA((chunks + len(operands) - 2,)),
            pltpu.SemaphoreType.DMA((CHUNKS,)),
        ],
        compiler_params=pltpu.CompilerParams(vmem_limit_bytes=8 * MIB),
        cost_estimate=pl.CostEstimate(
            flops=4 * rows * slots * HEAD_DIM * key_heads,
            bytes_accessed=slots * width * 2,
            transcendentals=rows * slots * key_heads,
        ),
        name="attention",
    )(cache_len, *operands)


def load_kernel(_, source, out_ref, token_ref, sems, *, part):
    copies = start_load(source, out_ref, part, sems)
    token_ref[...] = jnp.zeros_like(token_ref)
    for copy in copies:
        copy.wait()


def load(after, weight, part):
    shape = (part.size, weight.shape[2])
    return pl.pallas_call(
        functools.partial(load_kernel, part=part),
        out_shape=(pltpu.VMEM(shape, weight.dtype), jax.ShapeDtypeStruct((8, LANES), jnp.float32)),
        in_specs=[pl.BlockSpec(memory_space=pl.ANY)] * 2,
        out_specs=(pl.BlockSpec(memory_space=pltpu.VMEM),) * 2,
        scratch_shapes=[pltpu.SemaphoreType.DMA((CHUNKS,))],
        compiler_params=pltpu.CompilerParams(vmem_limit_bytes=MIB),
        cost_estimate=pl.CostEstimate(flops=0, bytes_accessed=4 * shape[0] * shape[1], transcendentals=0),
        name="load",
    )(after, pltpu.with_memory_space_constraint(weight, pltpu.HBM))


def norm_kernel(place_ref, _, *refs, experts):
    pieces, out_ref = refs[:-1], refs[-1]
    tokens, wide = pieces[0].shape
    block = wide - 2 * LANES
    model = len(pieces) * block
    total = jnp.zeros((tokens, LANES), jnp.float32)
    for piece in pieces:
        total = total + piece[:, block : block + LANES].astype(jnp.float32)
    sums = total + pltpu.roll(total, LANES - SLOT, 1) + pltpu.roll(total, LANES - 2 * SLOT, 1)
    mean = sums[:, experts : experts + 1] / model
    variance = sums[:, experts + 1 : experts + 2] / model - mean * mean
    inv = lax.rsqrt(variance + NORM_EPS)
    plain = pltpu.roll(sums, LANES - experts - 2, 1)
    logits = (sums - mean * plain) * inv
    lane = lax.broadcasted_iota(jnp.int32, (tokens, LANES), 1)
    named = (pltpu.roll(total, LANES - MASK_AT, 1) > 0) & (lane < experts)
    raised = jnp.where(named, jnp.exp(logits), 0.0)
    share = raised / jnp.sum(raised, axis=1, keepdims=True)
    high = share.astype(jnp.bfloat16).astype(jnp.float32)
    side = high + pltpu.roll(share - high, experts, 1)
    out_ref[:, model:] = side.astype(out_ref.dtype)
    for mask, piece in zip(send_order(len(pieces)) + [0], pieces):
        gain = piece[:, block + LANES :].astype(jnp.float32)
        gain = jnp.concatenate([gain[j : j + 1, :] for j in range(block // LANES)], axis=1)
        x = (piece[:, :block].astype(jnp.float32) - mean) * inv * gain
        at = pl.multiple_of(lax.bitwise_xor(place_ref[0], mask) * block, block)
        out_ref[:, pl.ds(at, block)] = x.astype(out_ref.dtype)


def norm_rows(place, token, blocks, experts):
    tokens, wide = blocks[0].shape
    model = (wide - 2 * LANES) * len(blocks)
    vmem = pl.BlockSpec(memory_space=pltpu.VMEM)
    return pl.pallas_call(
        functools.partial(norm_kernel, experts=experts),
        out_shape=jax.ShapeDtypeStruct((tokens, model + LANES), jnp.bfloat16),
        in_specs=[pl.BlockSpec(memory_space=pltpu.SMEM)] + [vmem] * (1 + len(blocks)),
        out_specs=vmem,
        compiler_params=pltpu.CompilerParams(vmem_limit_bytes=4 * MIB),
        name="norm",
    )(place, token, *blocks)


def stack_kernel(_, *refs):
    masks = send_order(len(refs) - 1) + [0]
    pieces, out_ref = [refs[masks.index(m)] for m in range(len(masks))], refs[-1]
    rows = 2 * pieces[0].shape[0]
    for i in range(0, len(pieces), 2):
        pair = [piece[...].astype(jnp.float32) for piece in pieces[i : i + 2]]
        out_ref[i // 2 * rows : (i // 2 + 1) * rows] = jnp.concatenate(pair, axis=0).astype(out_ref.dtype)


def stack_rows(token, pieces):
    rows, wide = pieces[0].shape
    vmem = pl.BlockSpec(memory_space=pltpu.VMEM)
    return pl.pallas_call(
        stack_kernel,
        out_shape=jax.ShapeDtypeStruct((rows * len(pieces), wide), pieces[0].dtype),
        in_specs=[vmem] * (1 + len(pieces)),
        out_specs=vmem,
        compiler_params=pltpu.CompilerParams(vmem_limit_bytes=4 * MIB),
        name="stack",
    )(token, *pieces)


def hidden_kernel(place_ref, near, far, gate_a, gate_b, up_a, up_b, _, hidden, x, *, experts):
    half = near.shape[0]
    model = gate_a.shape[1]
    x[:half] = near[:, :model]
    x[half:] = far[:, :model]
    side = jnp.concatenate([ref[:, model:].astype(jnp.float32) for ref in (near, far)], axis=0).T
    at = lax.broadcasted_iota(jnp.int32, side.shape, 0)
    expert = place_ref[1]
    mine = (at == expert) | (at == expert + experts)
    share = jnp.sum(jnp.where(mine, side, 0.0), axis=0, keepdims=True)
    units = gate_a.shape[0] + gate_b.shape[0]
    cuts = sorted({0, gate_a.shape[0], up_a.shape[0], units})

    def times(first, second, start, stop):
        cut = first.shape[0]
        block = first[start:stop] if stop <= cut else second[start - cut : stop - cut]
        return lax.dot_general(block, x[...], BY_ROW, preferred_element_type=jnp.float32)

    for low, high in zip(cuts, cuts[1:]):
        for start in range(low, high, STREAM):
            stop = min(start + STREAM, high)
            a = times(gate_a, gate_b, start, stop)
            b = times(up_a, up_b, start, stop)
            out = a / (1.0 + jnp.exp(-a)) * b * share
            hidden[:, start:stop] = out.T.astype(hidden.dtype)


def run_hidden(place, near, far, weights, token, experts):
    units = weights[0].shape[0] + weights[1].shape[0]
    model = weights[0].shape[1]
    rows = 2 * near.shape[0]
    vmem = pl.BlockSpec(memory_space=pltpu.VMEM)
    return pl.pallas_call(
        functools.partial(hidden_kernel, experts=experts),
        out_shape=jax.ShapeDtypeStruct((rows, units), jnp.bfloat16),
        in_specs=[pl.BlockSpec(memory_space=pltpu.SMEM)] + [vmem] * 7,
        out_specs=vmem,
        scratch_shapes=[pltpu.VMEM((rows, model), jnp.bfloat16)],
        compiler_params=pltpu.CompilerParams(vmem_limit_bytes=(6 if rows <= 64 else 24) * MIB),
        cost_estimate=pl.CostEstimate(
            flops=4 * rows * units * model, bytes_accessed=4 * units * model, transcendentals=rows * units
        ),
        name="hidden",
    )(place, near, far, *weights, token)


def send(x, axis, mask):
    return lax.ppermute(x, axis, [(i, i ^ mask) for i in range(lax.axis_size(axis))])


def send_order(size):
    order = list(range(size - 1, 0, -1))
    order[:2] = order[1::-1]
    return order


def exchange(parts, axis):
    return [send(parts[m], axis, m) for m in send_order(lax.axis_size(axis))]


def add(*terms):
    return sum(t.astype(jnp.float32) for t in terms)


def per_device(
    queries, new_kv, kv_cache, cache_len, residual, norm_gain, router, routes, gate_w, up_w, down_w
):
    sections, groups, tensors = (lax.axis_size(a) for a in ("section", "group", "tensor"))
    experts, block = router.shape
    tokens = queries.shape[0]
    place = lax.axis_index("tensor")
    where = jnp.stack([place, lax.axis_index("section") * tensors + place]).astype(jnp.int32)

    units = gate_w.shape[1]
    gate_parts, up_parts = [unit_parts(units, cut) for cut in cut_units(units)]

    fresh, gate_b = attend(
        cache_len, queries, new_kv, kv_cache, residual, routes, router, norm_gain, gate_w, gate_parts[1]
    )
    blocks = exchange([fresh] * tensors, "tensor") + [fresh]
    gate_a, token = load(fresh, gate_w, gate_parts[0])
    rows = norm_rows(where, token, blocks, experts)
    ranks = exchange([rows] * groups, "group") + [rows]
    up_a, token = load(rows, up_w, up_parts[0])
    near = stack_rows(token, ranks)
    far = send(near, "section", 1)
    up_b, token = load(near, up_w, up_parts[1])

    hidden = run_hidden(where, near, far, (gate_a, gate_b, up_a, up_b), token, experts)
    out = jnp.dot(hidden, down_w[0], preferred_element_type=jnp.float32).astype(jnp.bfloat16)
    half = out.shape[0] // 2
    both = add(out[:half], send(out[half:], "section", 1)).astype(jnp.bfloat16)
    both = both.reshape(groups, tokens, -1)
    got = add(*exchange(both, "group"), both[0]).astype(jnp.bfloat16)
    parts = [lax.dynamic_slice_in_dim(got, (place ^ m) * block, block, axis=1) for m in range(tensors)]
    mixed = add(*exchange(parts, "tensor"), parts[0], fresh[:, :block])
    return mixed.astype(jnp.bfloat16)


def solution(mesh):
    rows = P(("section", "group"), "tensor")
    weights = P(("section", "tensor"), "group", None)
    in_specs = (
        rows,
        rows,
        P(("section", "group"), None, "tensor"),
        P(("section", "group")),
        rows,
        P("tensor"),
        P(None, "tensor"),
        P(("section", "group"), None),
        weights,
        weights,
        weights,
    )
    return jax.shard_map(per_device, mesh=mesh, in_specs=in_specs, out_specs=rows, check_vma=False)
```

```python
import functools

import jax
import jax.numpy as jnp
from jax import lax
from jax.experimental import pallas as pl
from jax.experimental.pallas import tpu as pltpu
from jax.sharding import PartitionSpec as P

HEAD_DIM = 128
NORM_EPS = 1e-05
LANES = 128
SLOT = 36
MASK_AT = 3 * SLOT
MIB = 1 << 20
CHUNKS = 4
UNITS = 256
BY_ROW = (((1,), (1,)), ((), ()))


def split_terms(value):
    high = value.astype(jnp.bfloat16).astype(jnp.float32)
    rest = value - high
    middle = rest.astype(jnp.bfloat16).astype(jnp.float32)
    return high, middle, rest - middle


def cut_units(units):
    if units <= 7 * UNITS // 2:
        return units // 32 * 16, units // 32 * 16
    return units * 3 // 4 // UNITS * UNITS, units - UNITS


def unit_parts(units, cut):
    return pl.ds(0, cut), pl.ds(cut, units - cut)


def start_load(source, target, part, sems):
    count = max(c for c in range(1, CHUNKS + 1) if part.size % (16 * c) == 0 or c == 1)
    step = part.size // count
    copies = [
        pltpu.make_async_copy(
            source.at[0, pl.ds(part.start + i * step, step)], target.at[pl.ds(i * step, step)], sems.at[i]
        )
        for i in range(count)
    ]
    for copy in copies:
        copy.start()
    return copies


def attention_kernel(
    len_ref,
    q_hbm,
    new_hbm,
    kv_hbm,
    res_hbm,
    routes_hbm,
    router_hbm,
    gain_hbm,
    weight_hbm,
    out_ref,
    weight_ref,
    q_ref,
    new_ref,
    kv,
    res_ref,
    routes_ref,
    router_ref,
    gain_ref,
    scores,
    sems,
    weight_sems,
    *,
    chunks,
    rest,
):
    slots = kv_hbm.shape[1]
    part = slots // chunks
    sources = [q_hbm, new_hbm] + [kv_hbm.at[0, pl.ds(c * part, part)] for c in range(chunks)]
    targets = [q_ref, new_ref] + [kv.at[pl.ds(c * part, part)] for c in range(chunks)]
    sources += [res_hbm, routes_hbm, router_hbm, gain_hbm]
    targets += [res_ref, routes_ref, router_ref, gain_ref]
    copies = [pltpu.make_async_copy(a, b, sems.at[i]) for i, (a, b) in enumerate(zip(sources, targets))]
    for copy in copies:
        copy.start()
    loads = start_load(weight_hbm, weight_ref, rest, weight_sems)
    tokens, columns = q_ref.shape
    key_heads = new_ref.shape[1] // (2 * HEAD_DIM)
    grouped = columns // HEAD_DIM // key_heads
    rows = grouped * tokens
    scale = HEAD_DIM ** (-0.5)
    copies[0].wait()
    copies[1].wait()
    queries, selves = [], []
    for h in range(key_heads):
        first = h * grouped * HEAD_DIM
        q = jnp.concatenate(
            [
                q_ref[:, first + j * HEAD_DIM : first + (j + 1) * HEAD_DIM].astype(jnp.float32)
                for j in range(grouped)
            ],
            axis=0,
        )
        own_key = new_ref[:, 2 * h * HEAD_DIM : (2 * h + 1) * HEAD_DIM].astype(jnp.float32)
        own_key = jnp.concatenate([own_key] * grouped, axis=0)
        selves.append(jnp.sum(q * own_key, axis=1, keepdims=True) * scale)
        queries.append(q.astype(jnp.bfloat16))
    live = len_ref[0]
    for c in range(chunks):
        copies[2 + c].wait()
        for h in range(key_heads):
            keys = kv[c * part : (c + 1) * part, 2 * h * HEAD_DIM : (2 * h + 1) * HEAD_DIM]
            s = lax.dot_general(queries[h], keys, BY_ROW, preferred_element_type=jnp.float32)
            at = lax.broadcasted_iota(jnp.int32, (rows, part), 1) + c * part
            scores[h, :, c * part : (c + 1) * part] = jnp.where(at < live, s * scale, -jnp.inf)
    for copy in copies[2 + chunks :]:
        copy.wait()

    experts = router_ref.shape[0]
    routes = routes_ref[...]
    expert_at = lax.broadcasted_iota(jnp.int32, (LANES, tokens), 0) - MASK_AT
    named = jnp.zeros((LANES, tokens), jnp.float32)
    for k in range(routes.shape[0]):
        named = jnp.where(expert_at == routes[k : k + 1, :], 1.0, named)
    side = named.T

    streams = []
    for h in range(key_heads):
        s = scores[h]
        top = jnp.maximum(jnp.max(s, axis=1, keepdims=True), selves[h])
        weights = jnp.exp(s - top).astype(jnp.bfloat16)
        own = jnp.exp(selves[h] - top).astype(jnp.bfloat16).astype(jnp.float32)
        total = jnp.sum(weights.astype(jnp.float32), axis=1, keepdims=True) + own
        value_at = (2 * h + 1) * HEAD_DIM
        mixed = jnp.dot(weights, kv[:, value_at : value_at + HEAD_DIM], preferred_element_type=jnp.float32)
        own_value = new_ref[:, value_at : value_at + HEAD_DIM].astype(jnp.float32)
        mixed = (mixed + own * jnp.concatenate([own_value] * grouped, axis=0)) / total
        for j in range(grouped):
            at = (h * grouped + j) * HEAD_DIM
            got = res_ref[:, at : at + HEAD_DIM].astype(jnp.float32) + mixed[j * tokens : (j + 1) * tokens]
            got = got.astype(jnp.bfloat16)
            out_ref[:, at : at + HEAD_DIM] = got
            streams.append(got.astype(jnp.float32))

    lane = lax.broadcasted_iota(jnp.int32, (tokens, LANES), 1)
    sums = jnp.zeros((tokens, LANES), jnp.float32)

    def put(sums, at, pieces):
        total = pieces[0]
        for piece in pieces[1:]:
            total = total + piece
        return jnp.where(lane == at, jnp.sum(total, axis=1, keepdims=True), sums)

    blocks = range(len(streams))
    sums = put(sums, experts, streams)
    sums = put(sums, experts + 1, [x * x for x in streams])
    gain = gain_ref[...].astype(jnp.float32).reshape(1, -1)
    gains = [gain[:, b * HEAD_DIM : (b + 1) * HEAD_DIM] for b in blocks]
    scaled = [x * g for x, g in zip(streams, gains)]
    for e in range(experts):
        weights = [router_ref[e : e + 1, b * HEAD_DIM : (b + 1) * HEAD_DIM].astype(jnp.float32) for b in blocks]
        sums = put(sums, e, [x * w for x, w in zip(scaled, weights)])
        plain = [jnp.broadcast_to(g * w, (tokens, HEAD_DIM)) for g, w in zip(gains, weights)]
        sums = put(sums, experts + 2 + e, plain)
    for i, term in enumerate(split_terms(sums)):
        side = side + (pltpu.roll(term, i * SLOT, 1) if i else term)
    out_ref[:, columns : columns + LANES] = side.astype(out_ref.dtype)
    gain_rows = jnp.concatenate(
        gains + [jnp.zeros((1, LANES), jnp.float32)] * (tokens - len(gains)), axis=0
    )
    out_ref[:, columns + LANES :] = gain_rows.astype(out_ref.dtype)
    for copy in loads:
        copy.wait()


def attend(cache_len, queries, new_kv, kv_cache, residual, routes, router, norm_gain, weight, rest):
    tokens, columns = queries.shape
    slots, width = kv_cache.shape[1:]
    key_heads = new_kv.shape[1] // (2 * HEAD_DIM)
    rows = columns // HEAD_DIM // key_heads * tokens
    chunks = 4
    operands = [queries, new_kv, kv_cache, residual, routes.T, router, norm_gain, weight]
    operands = [pltpu.with_memory_space_constraint(x, pltpu.HBM) for x in operands]
    kept = [pltpu.VMEM(x.shape, x.dtype) for x in operands[:-1]]
    kept[2] = pltpu.VMEM((slots, width), kv_cache.dtype)
    return pl.pallas_call(
        functools.partial(attention_kernel, chunks=chunks, rest=rest),
        out_shape=(
            jax.ShapeDtypeStruct((tokens, columns + 2 * LANES), jnp.bfloat16),
            pltpu.VMEM((rest.size, weight.shape[2]), weight.dtype),
        ),
        in_specs=[pl.BlockSpec(memory_space=pltpu.SMEM)]
        + [pl.BlockSpec(memory_space=pl.ANY)] * len(operands),
        out_specs=(pl.BlockSpec(memory_space=pltpu.VMEM),) * 2,
        scratch_shapes=kept
        + [
            pltpu.VMEM((key_heads, rows, slots), jnp.float32),
            pltpu.SemaphoreType.DMA((chunks + len(operands) - 2,)),
            pltpu.SemaphoreType.DMA((CHUNKS,)),
        ],
        compiler_params=pltpu.CompilerParams(vmem_limit_bytes=8 * MIB),
        cost_estimate=pl.CostEstimate(
            flops=4 * rows * slots * HEAD_DIM * key_heads,
            bytes_accessed=slots * width * 2,
            transcendentals=rows * slots * key_heads,
        ),
        name="attention",
    )(cache_len, *operands)


def load_kernel(_, source, out_ref, token_ref, sems, *, part):
    copies = start_load(source, out_ref, part, sems)
    token_ref[...] = jnp.zeros_like(token_ref)
    for copy in copies:
        copy.wait()


def load(after, weight, part):
    shape = (part.size, weight.shape[2])
    return pl.pallas_call(
        functools.partial(load_kernel, part=part),
        out_shape=(pltpu.VMEM(shape, weight.dtype), jax.ShapeDtypeStruct((8, LANES), jnp.float32)),
        in_specs=[pl.BlockSpec(memory_space=pl.ANY)] * 2,
        out_specs=(pl.BlockSpec(memory_space=pltpu.VMEM),) * 2,
        scratch_shapes=[pltpu.SemaphoreType.DMA((CHUNKS,))],
        compiler_params=pltpu.CompilerParams(vmem_limit_bytes=MIB),
        cost_estimate=pl.CostEstimate(flops=0, bytes_accessed=4 * shape[0] * shape[1], transcendentals=0),
        name="load",
    )(after, pltpu.with_memory_space_constraint(weight, pltpu.HBM))


def norm_kernel(place_ref, _, *refs, experts):
    pieces, out_ref = refs[:-1], refs[-1]
    tokens, wide = pieces[0].shape
    block = wide - 2 * LANES
    model = len(pieces) * block
    total = jnp.zeros((tokens, LANES), jnp.float32)
    for piece in pieces:
        total = total + piece[:, block : block + LANES].astype(jnp.float32)
    sums = total + pltpu.roll(total, LANES - SLOT, 1) + pltpu.roll(total, LANES - 2 * SLOT, 1)
    mean = sums[:, experts : experts + 1] / model
    variance = sums[:, experts + 1 : experts + 2] / model - mean * mean
    inv = lax.rsqrt(variance + NORM_EPS)
    plain = pltpu.roll(sums, LANES - experts - 2, 1)
    logits = (sums - mean * plain) * inv
    lane = lax.broadcasted_iota(jnp.int32, (tokens, LANES), 1)
    named = (pltpu.roll(total, LANES - MASK_AT, 1) > 0) & (lane < experts)
    raised = jnp.where(named, jnp.exp(logits), 0.0)
    share = raised / jnp.sum(raised, axis=1, keepdims=True)
    high = share.astype(jnp.bfloat16).astype(jnp.float32)
    side = high + pltpu.roll(share - high, experts, 1)
    out_ref[:, model:] = side.astype(out_ref.dtype)
    for mask, piece in zip(send_order(len(pieces)) + [0], pieces):
        gain = piece[:, block + LANES :].astype(jnp.float32)
        gain = jnp.concatenate([gain[j : j + 1, :] for j in range(block // LANES)], axis=1)
        x = (piece[:, :block].astype(jnp.float32) - mean) * inv * gain
        at = pl.multiple_of(lax.bitwise_xor(place_ref[0], mask) * block, block)
        out_ref[:, pl.ds(at, block)] = x.astype(out_ref.dtype)


def norm_rows(place, token, blocks, experts):
    tokens, wide = blocks[0].shape
    model = (wide - 2 * LANES) * len(blocks)
    vmem = pl.BlockSpec(memory_space=pltpu.VMEM)
    return pl.pallas_call(
        functools.partial(norm_kernel, experts=experts),
        out_shape=jax.ShapeDtypeStruct((tokens, model + LANES), jnp.bfloat16),
        in_specs=[pl.BlockSpec(memory_space=pltpu.SMEM)] + [vmem] * (1 + len(blocks)),
        out_specs=vmem,
        compiler_params=pltpu.CompilerParams(vmem_limit_bytes=4 * MIB),
        name="norm",
    )(place, token, *blocks)


def stack_kernel(_, *refs):
    masks = send_order(len(refs) - 1) + [0]
    pieces, out_ref = [refs[masks.index(m)] for m in range(len(masks))], refs[-1]
    rows = 2 * pieces[0].shape[0]
    for i in range(0, len(pieces), 2):
        pair = [piece[...].astype(jnp.float32) for piece in pieces[i : i + 2]]
        out_ref[i // 2 * rows : (i // 2 + 1) * rows] = jnp.concatenate(pair, axis=0).astype(out_ref.dtype)


def stack_rows(token, pieces):
    rows, wide = pieces[0].shape
    vmem = pl.BlockSpec(memory_space=pltpu.VMEM)
    return pl.pallas_call(
        stack_kernel,
        out_shape=jax.ShapeDtypeStruct((rows * len(pieces), wide), pieces[0].dtype),
        in_specs=[vmem] * (1 + len(pieces)),
        out_specs=vmem,
        compiler_params=pltpu.CompilerParams(vmem_limit_bytes=4 * MIB),
        name="stack",
    )(token, *pieces)


def hidden_kernel(place_ref, near, far, gate_a, gate_b, up_a, up_b, _, hidden, x, *, experts):
    half = near.shape[0]
    model = gate_a.shape[1]
    x[:half] = near[:, :model]
    x[half:] = far[:, :model]
    side = jnp.concatenate([ref[:, model:].astype(jnp.float32) for ref in (near, far)], axis=0)
    lane = lax.broadcasted_iota(jnp.int32, side.shape, 1)
    expert = place_ref[1]
    mine = (lane == expert) | (lane == expert + experts)
    share = jnp.sum(jnp.where(mine, side, 0.0), axis=1, keepdims=True)
    units = gate_a.shape[0] + gate_b.shape[0]
    cuts = sorted({0, gate_a.shape[0], up_a.shape[0], units})

    def rows(first, second, start, stop):
        cut = first.shape[0]
        return first[start:stop] if stop <= cut else second[start - cut : stop - cut]

    for low, high in zip(cuts, cuts[1:]):
        for start in range(low, high, UNITS):
            stop = min(start + UNITS, high)
            gate, up = rows(gate_a, gate_b, start, stop), rows(up_a, up_b, start, stop)
            a = lax.dot_general(x[...], gate, BY_ROW, preferred_element_type=jnp.float32)
            b = lax.dot_general(up, x[...], BY_ROW, preferred_element_type=jnp.float32)
            out = a / (1.0 + jnp.exp(-a)) * share * b.T
            hidden[:, start:stop] = out.astype(hidden.dtype)


def run_hidden(place, near, far, weights, token, experts):
    units = weights[0].shape[0] + weights[1].shape[0]
    model = weights[0].shape[1]
    rows = 2 * near.shape[0]
    vmem = pl.BlockSpec(memory_space=pltpu.VMEM)
    return pl.pallas_call(
        functools.partial(hidden_kernel, experts=experts),
        out_shape=jax.ShapeDtypeStruct((rows, units), jnp.bfloat16),
        in_specs=[pl.BlockSpec(memory_space=pltpu.SMEM)] + [vmem] * 7,
        out_specs=vmem,
        scratch_shapes=[pltpu.VMEM((rows, model), jnp.bfloat16)],
        compiler_params=pltpu.CompilerParams(vmem_limit_bytes=(6 if rows <= 64 else 24) * MIB),
        cost_estimate=pl.CostEstimate(
            flops=4 * rows * units * model, bytes_accessed=4 * units * model, transcendentals=rows * units
        ),
        name="hidden",
    )(place, near, far, *weights, token)


def send(x, axis, mask):
    return lax.ppermute(x, axis, [(i, i ^ mask) for i in range(lax.axis_size(axis))])


def send_order(size):
    order = list(range(size - 1, 0, -1))
    order[:2] = order[1::-1]
    return order


def exchange(parts, axis):
    return [send(parts[m], axis, m) for m in send_order(lax.axis_size(axis))]


def add(*terms):
    return sum(t.astype(jnp.float32) for t in terms)


def per_device(
    queries, new_kv, kv_cache, cache_len, residual, norm_gain, router, routes, gate_w, up_w, down_w
):
    sections, groups, tensors = (lax.axis_size(a) for a in ("section", "group", "tensor"))
    experts, block = router.shape
    tokens = queries.shape[0]
    place = lax.axis_index("tensor")
    where = jnp.stack([place, lax.axis_index("section") * tensors + place]).astype(jnp.int32)

    units = gate_w.shape[1]
    gate_parts, up_parts = [unit_parts(units, cut) for cut in cut_units(units)]

    fresh, gate_b = attend(
        cache_len, queries, new_kv, kv_cache, residual, routes, router, norm_gain, gate_w, gate_parts[1]
    )
    blocks = exchange([fresh] * tensors, "tensor") + [fresh]
    gate_a, token = load(fresh, gate_w, gate_parts[0])
    rows = norm_rows(where, token, blocks, experts)
    ranks = exchange([rows] * groups, "group") + [rows]
    up_a, token = load(rows, up_w, up_parts[0])
    near = stack_rows(token, ranks)
    far = send(near, "section", 1)
    up_b, token = load(near, up_w, up_parts[1])

    hidden = run_hidden(where, near, far, (gate_a, gate_b, up_a, up_b), token, experts)
    out = jnp.dot(hidden, down_w[0], preferred_element_type=jnp.float32).astype(jnp.bfloat16)
    half = out.shape[0] // 2
    both = add(out[:half], send(out[half:], "section", 1)).astype(jnp.bfloat16)
    both = both.reshape(groups, tokens, -1)
    got = add(*exchange(both, "group"), both[0]).astype(jnp.bfloat16)
    parts = [lax.dynamic_slice_in_dim(got, (place ^ m) * block, block, axis=1) for m in range(tensors)]
    mixed = add(*exchange(parts, "tensor"), parts[0], fresh[:, :block])
    return mixed.astype(jnp.bfloat16)


def solution(mesh):
    rows = P(("section", "group"), "tensor")
    weights = P(("section", "tensor"), "group", None)
    in_specs = (
        rows,
        rows,
        P(("section", "group"), None, "tensor"),
        P(("section", "group")),
        rows,
        P("tensor"),
        P(None, "tensor"),
        P(("section", "group"), None),
        weights,
        weights,
        weights,
    )
    return jax.shard_map(per_device, mesh=mesh, in_specs=in_specs, out_specs=rows, check_vma=False)
```

```python
import functools

import jax
import jax.numpy as jnp
from jax import lax
from jax.experimental import pallas as pl
from jax.experimental.pallas import tpu as pltpu
from jax.sharding import PartitionSpec as P

HEAD_DIM = 128
NORM_EPS = 1e-05
LANES = 128
SLOT = 36
MASK_AT = 3 * SLOT
MIB = 1 << 20
CHUNKS = 16
UNITS = 256
BY_ROW = (((1,), (1,)), ((), ()))


def split_terms(value):
    high = value.astype(jnp.bfloat16).astype(jnp.float32)
    rest = value - high
    middle = rest.astype(jnp.bfloat16).astype(jnp.float32)
    return high, middle, rest - middle


def cut_units(units):
    if units <= 7 * UNITS // 2:
        return units // 32 * 16, units // 32 * 16
    return units * 3 // 4 // UNITS * UNITS, units - UNITS


def unit_parts(units, cut):
    return pl.ds(0, cut), pl.ds(cut, units - cut)


def start_load(source, target, part, sems):
    count = max(c for c in range(1, CHUNKS + 1) if part.size % (16 * c) == 0 or c == 1)
    step = part.size // count
    copies = [
        pltpu.make_async_copy(
            source.at[0, pl.ds(part.start + i * step, step)], target.at[pl.ds(i * step, step)], sems.at[i]
        )
        for i in range(count)
    ]
    for copy in copies:
        copy.start()
    return copies


def attention_kernel(
    len_ref,
    q_hbm,
    new_hbm,
    kv_hbm,
    res_hbm,
    routes_hbm,
    router_hbm,
    gain_hbm,
    weight_hbm,
    out_ref,
    weight_ref,
    q_ref,
    new_ref,
    kv,
    res_ref,
    routes_ref,
    router_ref,
    gain_ref,
    scores,
    sems,
    weight_sems,
    *,
    chunks,
    rest,
):
    slots = kv_hbm.shape[1]
    part = slots // chunks
    sources = [q_hbm, new_hbm] + [kv_hbm.at[0, pl.ds(c * part, part)] for c in range(chunks)]
    targets = [q_ref, new_ref] + [kv.at[pl.ds(c * part, part)] for c in range(chunks)]
    sources += [res_hbm, routes_hbm, router_hbm, gain_hbm]
    targets += [res_ref, routes_ref, router_ref, gain_ref]
    copies = [pltpu.make_async_copy(a, b, sems.at[i]) for i, (a, b) in enumerate(zip(sources, targets))]
    for copy in copies:
        copy.start()
    loads = start_load(weight_hbm, weight_ref, rest, weight_sems)
    tokens, columns = q_ref.shape
    key_heads = new_ref.shape[1] // (2 * HEAD_DIM)
    grouped = columns // HEAD_DIM // key_heads
    rows = grouped * tokens
    scale = HEAD_DIM ** (-0.5)
    copies[0].wait()
    copies[1].wait()
    queries, selves = [], []
    for h in range(key_heads):
        first = h * grouped * HEAD_DIM
        q = jnp.concatenate(
            [
                q_ref[:, first + j * HEAD_DIM : first + (j + 1) * HEAD_DIM].astype(jnp.float32)
                for j in range(grouped)
            ],
            axis=0,
        )
        own_key = new_ref[:, 2 * h * HEAD_DIM : (2 * h + 1) * HEAD_DIM].astype(jnp.float32)
        own_key = jnp.concatenate([own_key] * grouped, axis=0)
        selves.append(jnp.sum(q * own_key, axis=1, keepdims=True) * scale)
        queries.append(q.astype(jnp.bfloat16))
    live = len_ref[0]
    for c in range(chunks):
        copies[2 + c].wait()
        for h in range(key_heads):
            keys = kv[c * part : (c + 1) * part, 2 * h * HEAD_DIM : (2 * h + 1) * HEAD_DIM]
            s = lax.dot_general(queries[h], keys, BY_ROW, preferred_element_type=jnp.float32)
            at = lax.broadcasted_iota(jnp.int32, (rows, part), 1) + c * part
            scores[h, :, c * part : (c + 1) * part] = jnp.where(at < live, s * scale, -jnp.inf)
    for copy in copies[2 + chunks :]:
        copy.wait()

    experts = router_ref.shape[0]
    routes = routes_ref[...]
    expert_at = lax.broadcasted_iota(jnp.int32, (LANES, tokens), 0) - MASK_AT
    named = jnp.zeros((LANES, tokens), jnp.float32)
    for k in range(routes.shape[0]):
        named = jnp.where(expert_at == routes[k : k + 1, :], 1.0, named)
    side = named.T

    streams = []
    for h in range(key_heads):
        s = scores[h]
        top = jnp.maximum(jnp.max(s, axis=1, keepdims=True), selves[h])
        weights = jnp.exp(s - top).astype(jnp.bfloat16)
        own = jnp.exp(selves[h] - top).astype(jnp.bfloat16).astype(jnp.float32)
        total = jnp.sum(weights.astype(jnp.float32), axis=1, keepdims=True) + own
        value_at = (2 * h + 1) * HEAD_DIM
        mixed = jnp.dot(weights, kv[:, value_at : value_at + HEAD_DIM], preferred_element_type=jnp.float32)
        own_value = new_ref[:, value_at : value_at + HEAD_DIM].astype(jnp.float32)
        mixed = (mixed + own * jnp.concatenate([own_value] * grouped, axis=0)) / total
        for j in range(grouped):
            at = (h * grouped + j) * HEAD_DIM
            got = res_ref[:, at : at + HEAD_DIM].astype(jnp.float32) + mixed[j * tokens : (j + 1) * tokens]
            got = got.astype(jnp.bfloat16)
            out_ref[:, at : at + HEAD_DIM] = got
            streams.append(got.astype(jnp.float32))

    lane = lax.broadcasted_iota(jnp.int32, (tokens, LANES), 1)
    sums = jnp.zeros((tokens, LANES), jnp.float32)

    def put(sums, at, pieces):
        total = pieces[0]
        for piece in pieces[1:]:
            total = total + piece
        return jnp.where(lane == at, jnp.sum(total, axis=1, keepdims=True), sums)

    blocks = range(len(streams))
    sums = put(sums, experts, streams)
    sums = put(sums, experts + 1, [x * x for x in streams])
    gain = gain_ref[...].astype(jnp.float32).reshape(1, -1)
    gains = [gain[:, b * HEAD_DIM : (b + 1) * HEAD_DIM] for b in blocks]
    scaled = [x * g for x, g in zip(streams, gains)]
    for e in range(experts):
        weights = [router_ref[e : e + 1, b * HEAD_DIM : (b + 1) * HEAD_DIM].astype(jnp.float32) for b in blocks]
        sums = put(sums, e, [x * w for x, w in zip(scaled, weights)])
        plain = [jnp.broadcast_to(g * w, (tokens, HEAD_DIM)) for g, w in zip(gains, weights)]
        sums = put(sums, experts + 2 + e, plain)
    for i, term in enumerate(split_terms(sums)):
        side = side + (pltpu.roll(term, i * SLOT, 1) if i else term)
    out_ref[:, columns : columns + LANES] = side.astype(out_ref.dtype)
    gain_rows = jnp.concatenate(
        gains + [jnp.zeros((1, LANES), jnp.float32)] * (tokens - len(gains)), axis=0
    )
    out_ref[:, columns + LANES :] = gain_rows.astype(out_ref.dtype)
    for copy in loads:
        copy.wait()


def attend(cache_len, queries, new_kv, kv_cache, residual, routes, router, norm_gain, weight, rest):
    tokens, columns = queries.shape
    slots, width = kv_cache.shape[1:]
    key_heads = new_kv.shape[1] // (2 * HEAD_DIM)
    rows = columns // HEAD_DIM // key_heads * tokens
    chunks = 4
    operands = [queries, new_kv, kv_cache, residual, routes.T, router, norm_gain, weight]
    operands = [pltpu.with_memory_space_constraint(x, pltpu.HBM) for x in operands]
    kept = [pltpu.VMEM(x.shape, x.dtype) for x in operands[:-1]]
    kept[2] = pltpu.VMEM((slots, width), kv_cache.dtype)
    return pl.pallas_call(
        functools.partial(attention_kernel, chunks=chunks, rest=rest),
        out_shape=(
            jax.ShapeDtypeStruct((tokens, columns + 2 * LANES), jnp.bfloat16),
            pltpu.VMEM((rest.size, weight.shape[2]), weight.dtype),
        ),
        in_specs=[pl.BlockSpec(memory_space=pltpu.SMEM)]
        + [pl.BlockSpec(memory_space=pl.ANY)] * len(operands),
        out_specs=(pl.BlockSpec(memory_space=pltpu.VMEM),) * 2,
        scratch_shapes=kept
        + [
            pltpu.VMEM((key_heads, rows, slots), jnp.float32),
            pltpu.SemaphoreType.DMA((chunks + len(operands) - 2,)),
            pltpu.SemaphoreType.DMA((CHUNKS,)),
        ],
        compiler_params=pltpu.CompilerParams(vmem_limit_bytes=8 * MIB),
        cost_estimate=pl.CostEstimate(
            flops=4 * rows * slots * HEAD_DIM * key_heads,
            bytes_accessed=slots * width * 2,
            transcendentals=rows * slots * key_heads,
        ),
        name="attention",
    )(cache_len, *operands)


def load_kernel(_, source, out_ref, token_ref, sems, *, part):
    copies = start_load(source, out_ref, part, sems)
    token_ref[...] = jnp.zeros_like(token_ref)
    for copy in copies:
        copy.wait()


def load(after, weight, part):
    shape = (part.size, weight.shape[2])
    return pl.pallas_call(
        functools.partial(load_kernel, part=part),
        out_shape=(pltpu.VMEM(shape, weight.dtype), jax.ShapeDtypeStruct((8, LANES), jnp.float32)),
        in_specs=[pl.BlockSpec(memory_space=pl.ANY)] * 2,
        out_specs=(pl.BlockSpec(memory_space=pltpu.VMEM),) * 2,
        scratch_shapes=[pltpu.SemaphoreType.DMA((CHUNKS,))],
        compiler_params=pltpu.CompilerParams(vmem_limit_bytes=MIB),
        cost_estimate=pl.CostEstimate(flops=0, bytes_accessed=4 * shape[0] * shape[1], transcendentals=0),
        name="load",
    )(after, pltpu.with_memory_space_constraint(weight, pltpu.HBM))


def norm_kernel(place_ref, _, *refs, experts):
    pieces, out_ref = refs[:-1], refs[-1]
    tokens, wide = pieces[0].shape
    block = wide - 2 * LANES
    model = len(pieces) * block
    total = jnp.zeros((tokens, LANES), jnp.float32)
    for piece in pieces:
        total = total + piece[:, block : block + LANES].astype(jnp.float32)
    sums = total + pltpu.roll(total, LANES - SLOT, 1) + pltpu.roll(total, LANES - 2 * SLOT, 1)
    mean = sums[:, experts : experts + 1] / model
    variance = sums[:, experts + 1 : experts + 2] / model - mean * mean
    inv = lax.rsqrt(variance + NORM_EPS)
    plain = pltpu.roll(sums, LANES - experts - 2, 1)
    logits = (sums - mean * plain) * inv
    lane = lax.broadcasted_iota(jnp.int32, (tokens, LANES), 1)
    named = (pltpu.roll(total, LANES - MASK_AT, 1) > 0) & (lane < experts)
    raised = jnp.where(named, jnp.exp(logits), 0.0)
    share = raised / jnp.sum(raised, axis=1, keepdims=True)
    high = share.astype(jnp.bfloat16).astype(jnp.float32)
    side = high + pltpu.roll(share - high, experts, 1)
    out_ref[:, model:] = side.astype(out_ref.dtype)
    for mask, piece in zip(send_order(len(pieces)) + [0], pieces):
        gain = piece[:, block + LANES :].astype(jnp.float32)
        gain = jnp.concatenate([gain[j : j + 1, :] for j in range(block // LANES)], axis=1)
        x = (piece[:, :block].astype(jnp.float32) - mean) * inv * gain
        at = pl.multiple_of(lax.bitwise_xor(place_ref[0], mask) * block, block)
        out_ref[:, pl.ds(at, block)] = x.astype(out_ref.dtype)


def norm_rows(place, token, blocks, experts):
    tokens, wide = blocks[0].shape
    model = (wide - 2 * LANES) * len(blocks)
    vmem = pl.BlockSpec(memory_space=pltpu.VMEM)
    return pl.pallas_call(
        functools.partial(norm_kernel, experts=experts),
        out_shape=jax.ShapeDtypeStruct((tokens, model + LANES), jnp.bfloat16),
        in_specs=[pl.BlockSpec(memory_space=pltpu.SMEM)] + [vmem] * (1 + len(blocks)),
        out_specs=vmem,
        compiler_params=pltpu.CompilerParams(vmem_limit_bytes=4 * MIB),
        name="norm",
    )(place, token, *blocks)


def stack_kernel(_, *refs):
    masks = send_order(len(refs) - 1) + [0]
    pieces, out_ref = [refs[masks.index(m)] for m in range(len(masks))], refs[-1]
    rows = 2 * pieces[0].shape[0]
    for i in range(0, len(pieces), 2):
        pair = [piece[...].astype(jnp.float32) for piece in pieces[i : i + 2]]
        out_ref[i // 2 * rows : (i // 2 + 1) * rows] = jnp.concatenate(pair, axis=0).astype(out_ref.dtype)


def stack_rows(token, pieces):
    rows, wide = pieces[0].shape
    vmem = pl.BlockSpec(memory_space=pltpu.VMEM)
    return pl.pallas_call(
        stack_kernel,
        out_shape=jax.ShapeDtypeStruct((rows * len(pieces), wide), pieces[0].dtype),
        in_specs=[vmem] * (1 + len(pieces)),
        out_specs=vmem,
        compiler_params=pltpu.CompilerParams(vmem_limit_bytes=4 * MIB),
        name="stack",
    )(token, *pieces)


def hidden_kernel(place_ref, near, far, gate_a, gate_b, up_a, up_b, _, hidden, x, *, experts):
    half = near.shape[0]
    model = gate_a.shape[1]
    x[:half] = near[:, :model]
    x[half:] = far[:, :model]
    side = jnp.concatenate([ref[:, model:].astype(jnp.float32) for ref in (near, far)], axis=0)
    lane = lax.broadcasted_iota(jnp.int32, side.shape, 1)
    expert = place_ref[1]
    mine = (lane == expert) | (lane == expert + experts)
    share = jnp.sum(jnp.where(mine, side, 0.0), axis=1, keepdims=True)
    units = gate_a.shape[0] + gate_b.shape[0]
    cuts = sorted({0, gate_a.shape[0], up_a.shape[0], units})

    def rows(first, second, start, stop):
        cut = first.shape[0]
        return first[start:stop] if stop <= cut else second[start - cut : stop - cut]

    for low, high in zip(cuts, cuts[1:]):
        for start in range(low, high, UNITS):
            stop = min(start + UNITS, high)
            gate, up = rows(gate_a, gate_b, start, stop), rows(up_a, up_b, start, stop)
            a = lax.dot_general(x[...], gate, BY_ROW, preferred_element_type=jnp.float32)
            b = lax.dot_general(up, x[...], BY_ROW, preferred_element_type=jnp.float32)
            out = a / (1.0 + jnp.exp(-a)) * share * b.T
            hidden[:, start:stop] = out.astype(hidden.dtype)


def run_hidden(place, near, far, weights, token, experts):
    units = weights[0].shape[0] + weights[1].shape[0]
    model = weights[0].shape[1]
    rows = 2 * near.shape[0]
    vmem = pl.BlockSpec(memory_space=pltpu.VMEM)
    return pl.pallas_call(
        functools.partial(hidden_kernel, experts=experts),
        out_shape=jax.ShapeDtypeStruct((rows, units), jnp.bfloat16),
        in_specs=[pl.BlockSpec(memory_space=pltpu.SMEM)] + [vmem] * 7,
        out_specs=vmem,
        scratch_shapes=[pltpu.VMEM((rows, model), jnp.bfloat16)],
        compiler_params=pltpu.CompilerParams(vmem_limit_bytes=(6 if rows <= 64 else 24) * MIB),
        cost_estimate=pl.CostEstimate(
            flops=4 * rows * units * model, bytes_accessed=4 * units * model, transcendentals=rows * units
        ),
        name="hidden",
    )(place, near, far, *weights, token)


def send(x, axis, mask):
    return lax.ppermute(x, axis, [(i, i ^ mask) for i in range(lax.axis_size(axis))])


def send_order(size):
    order = list(range(size - 1, 0, -1))
    order[:2] = order[1::-1]
    return order


def exchange(parts, axis):
    return [send(parts[m], axis, m) for m in send_order(lax.axis_size(axis))]


def add(*terms):
    return sum(t.astype(jnp.float32) for t in terms)


def per_device(
    queries, new_kv, kv_cache, cache_len, residual, norm_gain, router, routes, gate_w, up_w, down_w
):
    sections, groups, tensors = (lax.axis_size(a) for a in ("section", "group", "tensor"))
    experts, block = router.shape
    tokens = queries.shape[0]
    place = lax.axis_index("tensor")
    where = jnp.stack([place, lax.axis_index("section") * tensors + place]).astype(jnp.int32)

    units = gate_w.shape[1]
    gate_parts, up_parts = [unit_parts(units, cut) for cut in cut_units(units)]

    fresh, gate_b = attend(
        cache_len, queries, new_kv, kv_cache, residual, routes, router, norm_gain, gate_w, gate_parts[1]
    )
    blocks = exchange([fresh] * tensors, "tensor") + [fresh]
    gate_a, token = load(fresh, gate_w, gate_parts[0])
    rows = norm_rows(where, token, blocks, experts)
    ranks = exchange([rows] * groups, "group") + [rows]
    up_a, token = load(rows, up_w, up_parts[0])
    near = stack_rows(token, ranks)
    far = send(near, "section", 1)
    up_b, token = load(near, up_w, up_parts[1])

    hidden = run_hidden(where, near, far, (gate_a, gate_b, up_a, up_b), token, experts)
    out = jnp.dot(hidden, down_w[0], preferred_element_type=jnp.float32).astype(jnp.bfloat16)
    half = out.shape[0] // 2
    both = add(out[:half], send(out[half:], "section", 1)).astype(jnp.bfloat16)
    both = both.reshape(groups, tokens, -1)
    others = [send(both[m], "group", m) for m in reversed(range(1, groups))]
    got = add(*others[1:], others[0], both[0]).astype(jnp.bfloat16)
    parts = [lax.dynamic_slice_in_dim(got, (place ^ m) * block, block, axis=1) for m in range(tensors)]
    mixed = add(*exchange(parts, "tensor"), parts[0], fresh[:, :block])
    return mixed.astype(jnp.bfloat16)


def solution(mesh):
    rows = P(("section", "group"), "tensor")
    weights = P(("section", "tensor"), "group", None)
    in_specs = (
        rows,
        rows,
        P(("section", "group"), None, "tensor"),
        P(("section", "group")),
        rows,
        P("tensor"),
        P(None, "tensor"),
        P(("section", "group"), None),
        weights,
        weights,
        weights,
    )
    return jax.shard_map(per_device, mesh=mesh, in_specs=in_specs, out_specs=rows, check_vma=False)
```

```python
import functools

import jax
import jax.numpy as jnp
from jax import lax
from jax.experimental import pallas as pl
from jax.experimental.pallas import tpu as pltpu
from jax.sharding import PartitionSpec as P

HEAD_DIM = 128
NORM_EPS = 1e-05
LANES = 128
SLOT = 36
MASK_AT = 3 * SLOT
MIB = 1 << 20
UNITS = 256
BY_ROW = (((1,), (1,)), ((), ()))


def split_terms(value):
    high = value.astype(jnp.bfloat16).astype(jnp.float32)
    rest = value - high
    middle = rest.astype(jnp.bfloat16).astype(jnp.float32)
    return high, middle, rest - middle


def cut_units(units):
    if units <= 7 * UNITS // 2:
        return units // 32 * 16, units // 32 * 16
    return units * 3 // 4 // UNITS * UNITS, units - UNITS


def unit_parts(units, cut):
    return pl.ds(0, cut), pl.ds(cut, units - cut)


def start_load(source, target, part, sem):
    copy = pltpu.make_async_copy(source.at[0, part], target, sem)
    copy.start()
    return copy


def attention_kernel(
    len_ref,
    q_hbm,
    new_hbm,
    kv_hbm,
    res_hbm,
    routes_hbm,
    router_hbm,
    gain_hbm,
    weight_hbm,
    out_ref,
    weight_ref,
    q_ref,
    new_ref,
    kv,
    res_ref,
    routes_ref,
    router_ref,
    gain_ref,
    scores,
    sems,
    weight_sem,
    *,
    chunks,
    rest,
):
    slots = kv_hbm.shape[1]
    part = slots // chunks
    sources = [q_hbm, new_hbm] + [kv_hbm.at[0, pl.ds(c * part, part)] for c in range(chunks)]
    targets = [q_ref, new_ref] + [kv.at[pl.ds(c * part, part)] for c in range(chunks)]
    sources += [res_hbm, routes_hbm, router_hbm, gain_hbm]
    targets += [res_ref, routes_ref, router_ref, gain_ref]
    copies = [pltpu.make_async_copy(a, b, sems.at[i]) for i, (a, b) in enumerate(zip(sources, targets))]
    for copy in copies:
        copy.start()
    load = start_load(weight_hbm, weight_ref, rest, weight_sem)
    tokens, columns = q_ref.shape
    key_heads = new_ref.shape[1] // (2 * HEAD_DIM)
    grouped = columns // HEAD_DIM // key_heads
    rows = grouped * tokens
    scale = HEAD_DIM ** (-0.5)
    copies[0].wait()
    copies[1].wait()
    queries, selves = [], []
    for h in range(key_heads):
        first = h * grouped * HEAD_DIM
        q = jnp.concatenate(
            [
                q_ref[:, first + j * HEAD_DIM : first + (j + 1) * HEAD_DIM].astype(jnp.float32)
                for j in range(grouped)
            ],
            axis=0,
        )
        own_key = new_ref[:, 2 * h * HEAD_DIM : (2 * h + 1) * HEAD_DIM].astype(jnp.float32)
        own_key = jnp.concatenate([own_key] * grouped, axis=0)
        selves.append(jnp.sum(q * own_key, axis=1, keepdims=True) * scale)
        queries.append(q.astype(jnp.bfloat16))
    live = len_ref[0]
    for c in range(chunks):
        copies[2 + c].wait()
        for h in range(key_heads):
            keys = kv[c * part : (c + 1) * part, 2 * h * HEAD_DIM : (2 * h + 1) * HEAD_DIM]
            s = lax.dot_general(queries[h], keys, BY_ROW, preferred_element_type=jnp.float32)
            at = lax.broadcasted_iota(jnp.int32, (rows, part), 1) + c * part
            scores[h, :, c * part : (c + 1) * part] = jnp.where(at < live, s * scale, -jnp.inf)
    for copy in copies[2 + chunks :]:
        copy.wait()

    experts = router_ref.shape[0]
    routes = routes_ref[...]
    expert_at = lax.broadcasted_iota(jnp.int32, (LANES, tokens), 0) - MASK_AT
    named = jnp.zeros((LANES, tokens), jnp.float32)
    for k in range(routes.shape[0]):
        named = jnp.where(expert_at == routes[k : k + 1, :], 1.0, named)
    side = named.T

    streams = []
    for h in range(key_heads):
        s = scores[h]
        top = jnp.maximum(jnp.max(s, axis=1, keepdims=True), selves[h])
        weights = jnp.exp(s - top).astype(jnp.bfloat16)
        own = jnp.exp(selves[h] - top).astype(jnp.bfloat16).astype(jnp.float32)
        total = jnp.sum(weights.astype(jnp.float32), axis=1, keepdims=True) + own
        value_at = (2 * h + 1) * HEAD_DIM
        mixed = jnp.dot(weights, kv[:, value_at : value_at + HEAD_DIM], preferred_element_type=jnp.float32)
        own_value = new_ref[:, value_at : value_at + HEAD_DIM].astype(jnp.float32)
        mixed = (mixed + own * jnp.concatenate([own_value] * grouped, axis=0)) / total
        for j in range(grouped):
            at = (h * grouped + j) * HEAD_DIM
            got = res_ref[:, at : at + HEAD_DIM].astype(jnp.float32) + mixed[j * tokens : (j + 1) * tokens]
            got = got.astype(jnp.bfloat16)
            out_ref[:, at : at + HEAD_DIM] = got
            streams.append(got.astype(jnp.float32))

    lane = lax.broadcasted_iota(jnp.int32, (tokens, LANES), 1)
    sums = jnp.zeros((tokens, LANES), jnp.float32)

    def put(sums, at, pieces):
        total = pieces[0]
        for piece in pieces[1:]:
            total = total + piece
        return jnp.where(lane == at, jnp.sum(total, axis=1, keepdims=True), sums)

    blocks = range(len(streams))
    sums = put(sums, experts, streams)
    sums = put(sums, experts + 1, [x * x for x in streams])
    gain = gain_ref[...].astype(jnp.float32).reshape(1, -1)
    gains = [gain[:, b * HEAD_DIM : (b + 1) * HEAD_DIM] for b in blocks]
    scaled = [x * g for x, g in zip(streams, gains)]
    for e in range(experts):
        weights = [router_ref[e : e + 1, b * HEAD_DIM : (b + 1) * HEAD_DIM].astype(jnp.float32) for b in blocks]
        sums = put(sums, e, [x * w for x, w in zip(scaled, weights)])
        plain = [jnp.broadcast_to(g * w, (tokens, HEAD_DIM)) for g, w in zip(gains, weights)]
        sums = put(sums, experts + 2 + e, plain)
    for i, term in enumerate(split_terms(sums)):
        side = side + (pltpu.roll(term, i * SLOT, 1) if i else term)
    out_ref[:, columns : columns + LANES] = side.astype(out_ref.dtype)
    gain_rows = jnp.concatenate(
        gains + [jnp.zeros((1, LANES), jnp.float32)] * (tokens - len(gains)), axis=0
    )
    out_ref[:, columns + LANES :] = gain_rows.astype(out_ref.dtype)
    load.wait()


def attend(cache_len, queries, new_kv, kv_cache, residual, routes, router, norm_gain, weight, rest):
    tokens, columns = queries.shape
    slots, width = kv_cache.shape[1:]
    key_heads = new_kv.shape[1] // (2 * HEAD_DIM)
    rows = columns // HEAD_DIM // key_heads * tokens
    chunks = 4
    operands = [queries, new_kv, kv_cache, residual, routes.T, router, norm_gain, weight]
    operands = [pltpu.with_memory_space_constraint(x, pltpu.HBM) for x in operands]
    kept = [pltpu.VMEM(x.shape, x.dtype) for x in operands[:-1]]
    kept[2] = pltpu.VMEM((slots, width), kv_cache.dtype)
    return pl.pallas_call(
        functools.partial(attention_kernel, chunks=chunks, rest=rest),
        out_shape=(
            jax.ShapeDtypeStruct((tokens, columns + 2 * LANES), jnp.bfloat16),
            pltpu.VMEM((rest.size, weight.shape[2]), weight.dtype),
        ),
        in_specs=[pl.BlockSpec(memory_space=pltpu.SMEM)]
        + [pl.BlockSpec(memory_space=pl.ANY)] * len(operands),
        out_specs=(pl.BlockSpec(memory_space=pltpu.VMEM),) * 2,
        scratch_shapes=kept
        + [
            pltpu.VMEM((key_heads, rows, slots), jnp.float32),
            pltpu.SemaphoreType.DMA((chunks + len(operands) - 2,)),
            pltpu.SemaphoreType.DMA,
        ],
        compiler_params=pltpu.CompilerParams(vmem_limit_bytes=8 * MIB),
        cost_estimate=pl.CostEstimate(
            flops=4 * rows * slots * HEAD_DIM * key_heads,
            bytes_accessed=slots * width * 2,
            transcendentals=rows * slots * key_heads,
        ),
        name="attention",
    )(cache_len, *operands)


def load_kernel(_, source, out_ref, token_ref, sem, *, part):
    copy = start_load(source, out_ref, part, sem)
    token_ref[...] = jnp.zeros_like(token_ref)
    copy.wait()


def load(after, weight, part):
    shape = (part.size, weight.shape[2])
    return pl.pallas_call(
        functools.partial(load_kernel, part=part),
        out_shape=(pltpu.VMEM(shape, weight.dtype), jax.ShapeDtypeStruct((8, LANES), jnp.float32)),
        in_specs=[pl.BlockSpec(memory_space=pl.ANY)] * 2,
        out_specs=(pl.BlockSpec(memory_space=pltpu.VMEM),) * 2,
        scratch_shapes=[pltpu.SemaphoreType.DMA],
        compiler_params=pltpu.CompilerParams(vmem_limit_bytes=MIB),
        cost_estimate=pl.CostEstimate(flops=0, bytes_accessed=4 * shape[0] * shape[1], transcendentals=0),
        name="load",
    )(after, pltpu.with_memory_space_constraint(weight, pltpu.HBM))


def norm_kernel(place_ref, _, *refs, experts):
    pieces, out_ref = refs[:-1], refs[-1]
    tokens, wide = pieces[0].shape
    block = wide - 2 * LANES
    model = len(pieces) * block
    total = jnp.zeros((tokens, LANES), jnp.float32)
    for piece in pieces:
        total = total + piece[:, block : block + LANES].astype(jnp.float32)
    sums = total + pltpu.roll(total, LANES - SLOT, 1) + pltpu.roll(total, LANES - 2 * SLOT, 1)
    mean = sums[:, experts : experts + 1] / model
    variance = sums[:, experts + 1 : experts + 2] / model - mean * mean
    inv = lax.rsqrt(variance + NORM_EPS)
    plain = pltpu.roll(sums, LANES - experts - 2, 1)
    logits = (sums - mean * plain) * inv
    lane = lax.broadcasted_iota(jnp.int32, (tokens, LANES), 1)
    named = (pltpu.roll(total, LANES - MASK_AT, 1) > 0) & (lane < experts)
    raised = jnp.where(named, jnp.exp(logits), 0.0)
    share = raised / jnp.sum(raised, axis=1, keepdims=True)
    high = share.astype(jnp.bfloat16).astype(jnp.float32)
    side = high + pltpu.roll(share - high, experts, 1)
    out_ref[:, model:] = side.astype(out_ref.dtype)
    for mask, piece in zip(send_order(len(pieces)) + [0], pieces):
        gain = piece[:, block + LANES :].astype(jnp.float32)
        gain = jnp.concatenate([gain[j : j + 1, :] for j in range(block // LANES)], axis=1)
        x = (piece[:, :block].astype(jnp.float32) - mean) * inv * gain
        at = pl.multiple_of(lax.bitwise_xor(place_ref[0], mask) * block, block)
        out_ref[:, pl.ds(at, block)] = x.astype(out_ref.dtype)


def norm_rows(place, token, blocks, experts):
    tokens, wide = blocks[0].shape
    model = (wide - 2 * LANES) * len(blocks)
    vmem = pl.BlockSpec(memory_space=pltpu.VMEM)
    return pl.pallas_call(
        functools.partial(norm_kernel, experts=experts),
        out_shape=jax.ShapeDtypeStruct((tokens, model + LANES), jnp.bfloat16),
        in_specs=[pl.BlockSpec(memory_space=pltpu.SMEM)] + [vmem] * (1 + len(blocks)),
        out_specs=vmem,
        compiler_params=pltpu.CompilerParams(vmem_limit_bytes=4 * MIB),
        name="norm",
    )(place, token, *blocks)


def stack_kernel(_, *refs):
    masks = send_order(len(refs) - 1) + [0]
    pieces, out_ref = [refs[masks.index(m)] for m in range(len(masks))], refs[-1]
    rows = 2 * pieces[0].shape[0]
    for i in range(0, len(pieces), 2):
        pair = [piece[...].astype(jnp.float32) for piece in pieces[i : i + 2]]
        out_ref[i // 2 * rows : (i // 2 + 1) * rows] = jnp.concatenate(pair, axis=0).astype(out_ref.dtype)


def stack_rows(token, pieces):
    rows, wide = pieces[0].shape
    vmem = pl.BlockSpec(memory_space=pltpu.VMEM)
    return pl.pallas_call(
        stack_kernel,
        out_shape=jax.ShapeDtypeStruct((rows * len(pieces), wide), pieces[0].dtype),
        in_specs=[vmem] * (1 + len(pieces)),
        out_specs=vmem,
        compiler_params=pltpu.CompilerParams(vmem_limit_bytes=4 * MIB),
        name="stack",
    )(token, *pieces)


def hidden_kernel(place_ref, near, far, gate_a, gate_b, up_a, up_b, _, hidden, x, *, experts):
    half = near.shape[0]
    model = gate_a.shape[1]
    x[:half] = near[:, :model]
    x[half:] = far[:, :model]
    side = jnp.concatenate([ref[:, model:].astype(jnp.float32) for ref in (near, far)], axis=0)
    lane = lax.broadcasted_iota(jnp.int32, side.shape, 1)
    expert = place_ref[1]
    mine = (lane == expert) | (lane == expert + experts)
    share = jnp.sum(jnp.where(mine, side, 0.0), axis=1, keepdims=True)
    units = gate_a.shape[0] + gate_b.shape[0]
    cuts = sorted({0, gate_a.shape[0], up_a.shape[0], units})

    def rows(first, second, start, stop):
        cut = first.shape[0]
        return first[start:stop] if stop <= cut else second[start - cut : stop - cut]

    for low, high in zip(cuts, cuts[1:]):
        for start in range(low, high, UNITS):
            stop = min(start + UNITS, high)
            gate, up = rows(gate_a, gate_b, start, stop), rows(up_a, up_b, start, stop)
            a = lax.dot_general(x[...], gate, BY_ROW, preferred_element_type=jnp.float32)
            b = lax.dot_general(up, x[...], BY_ROW, preferred_element_type=jnp.float32)
            out = a / (1.0 + jnp.exp(-a)) * share * b.T
            hidden[:, start:stop] = out.astype(hidden.dtype)


def run_hidden(place, near, far, weights, token, experts):
    units = weights[0].shape[0] + weights[1].shape[0]
    model = weights[0].shape[1]
    rows = 2 * near.shape[0]
    vmem = pl.BlockSpec(memory_space=pltpu.VMEM)
    return pl.pallas_call(
        functools.partial(hidden_kernel, experts=experts),
        out_shape=jax.ShapeDtypeStruct((rows, units), jnp.bfloat16),
        in_specs=[pl.BlockSpec(memory_space=pltpu.SMEM)] + [vmem] * 7,
        out_specs=vmem,
        scratch_shapes=[pltpu.VMEM((rows, model), jnp.bfloat16)],
        compiler_params=pltpu.CompilerParams(vmem_limit_bytes=(6 if rows <= 64 else 24) * MIB),
        cost_estimate=pl.CostEstimate(
            flops=4 * rows * units * model, bytes_accessed=4 * units * model, transcendentals=rows * units
        ),
        name="hidden",
    )(place, near, far, *weights, token)


def send(x, axis, mask):
    return lax.ppermute(x, axis, [(i, i ^ mask) for i in range(lax.axis_size(axis))])


def send_order(size):
    order = list(range(size - 1, 0, -1))
    order[:2] = order[1::-1]
    return order


def exchange(parts, axis):
    return [send(parts[m], axis, m) for m in send_order(lax.axis_size(axis))]


def add(*terms):
    return sum(t.astype(jnp.float32) for t in terms)


def per_device(
    queries, new_kv, kv_cache, cache_len, residual, norm_gain, router, routes, gate_w, up_w, down_w
):
    sections, groups, tensors = (lax.axis_size(a) for a in ("section", "group", "tensor"))
    experts, block = router.shape
    tokens = queries.shape[0]
    place = lax.axis_index("tensor")
    where = jnp.stack([place, lax.axis_index("section") * tensors + place]).astype(jnp.int32)

    units = gate_w.shape[1]
    gate_parts, up_parts = [unit_parts(units, cut) for cut in cut_units(units)]

    fresh, gate_b = attend(
        cache_len, queries, new_kv, kv_cache, residual, routes, router, norm_gain, gate_w, gate_parts[1]
    )
    blocks = exchange([fresh] * tensors, "tensor") + [fresh]
    gate_a, token = load(fresh, gate_w, gate_parts[0])
    rows = norm_rows(where, token, blocks, experts)
    ranks = exchange([rows] * groups, "group") + [rows]
    up_a, token = load(rows, up_w, up_parts[0])
    near = stack_rows(token, ranks)
    far = send(near, "section", 1)
    up_b, token = load(near, up_w, up_parts[1])

    hidden = run_hidden(where, near, far, (gate_a, gate_b, up_a, up_b), token, experts)
    out = jnp.dot(hidden, down_w[0], preferred_element_type=jnp.float32).astype(jnp.bfloat16)
    half = out.shape[0] // 2
    both = add(out[:half], send(out[half:], "section", 1)).astype(jnp.bfloat16)
    both = both.reshape(groups, tokens, -1)
    others = [send(both[m], "group", m) for m in reversed(range(1, groups))]
    got = add(*others[1:], others[0], both[0]).astype(jnp.bfloat16)
    parts = [lax.dynamic_slice_in_dim(got, (place ^ m) * block, block, axis=1) for m in range(tensors)]
    mixed = add(*exchange(parts, "tensor"), parts[0], fresh[:, :block])
    return mixed.astype(jnp.bfloat16)


def solution(mesh):
    rows = P(("section", "group"), "tensor")
    weights = P(("section", "tensor"), "group", None)
    in_specs = (
        rows,
        rows,
        P(("section", "group"), None, "tensor"),
        P(("section", "group")),
        rows,
        P("tensor"),
        P(None, "tensor"),
        P(("section", "group"), None),
        weights,
        weights,
        weights,
    )
    return jax.shard_map(per_device, mesh=mesh, in_specs=in_specs, out_specs=rows, check_vma=False)
```

```python
import functools

import jax
import jax.numpy as jnp
from jax import lax
from jax.experimental import pallas as pl
from jax.experimental.pallas import tpu as pltpu
from jax.sharding import PartitionSpec as P

HEAD_DIM = 128
NORM_EPS = 1e-05
LANES = 128
SLOT = 36
MASK_AT = 3 * SLOT
MIB = 1 << 20
UNITS = 256
BY_ROW = (((1,), (1,)), ((), ()))


def split_terms(value):
    high = value.astype(jnp.bfloat16).astype(jnp.float32)
    rest = value - high
    middle = rest.astype(jnp.bfloat16).astype(jnp.float32)
    return high, middle, rest - middle


def unit_parts(units):
    cut = units * 3 // 4 // UNITS * UNITS or units // 32 * 16
    return pl.ds(0, cut), pl.ds(cut, units - cut)


def start_load(source, target, part, sem):
    copy = pltpu.make_async_copy(source.at[0, part], target, sem)
    copy.start()
    return copy


def attention_kernel(
    len_ref,
    q_hbm,
    new_hbm,
    kv_hbm,
    res_hbm,
    routes_hbm,
    router_hbm,
    gain_hbm,
    weight_hbm,
    out_ref,
    weight_ref,
    q_ref,
    new_ref,
    kv,
    res_ref,
    routes_ref,
    router_ref,
    gain_ref,
    scores,
    sems,
    weight_sem,
    *,
    chunks,
    rest,
):
    slots = kv_hbm.shape[1]
    part = slots // chunks
    sources = [q_hbm, new_hbm] + [kv_hbm.at[0, pl.ds(c * part, part)] for c in range(chunks)]
    targets = [q_ref, new_ref] + [kv.at[pl.ds(c * part, part)] for c in range(chunks)]
    sources += [res_hbm, routes_hbm, router_hbm, gain_hbm]
    targets += [res_ref, routes_ref, router_ref, gain_ref]
    copies = [pltpu.make_async_copy(a, b, sems.at[i]) for i, (a, b) in enumerate(zip(sources, targets))]
    for copy in copies:
        copy.start()
    load = start_load(weight_hbm, weight_ref, rest, weight_sem)
    tokens, columns = q_ref.shape
    key_heads = new_ref.shape[1] // (2 * HEAD_DIM)
    grouped = columns // HEAD_DIM // key_heads
    rows = grouped * tokens
    scale = HEAD_DIM ** (-0.5)
    copies[0].wait()
    copies[1].wait()
    queries, selves = [], []
    for h in range(key_heads):
        first = h * grouped * HEAD_DIM
        q = jnp.concatenate(
            [
                q_ref[:, first + j * HEAD_DIM : first + (j + 1) * HEAD_DIM].astype(jnp.float32)
                for j in range(grouped)
            ],
            axis=0,
        )
        own_key = new_ref[:, 2 * h * HEAD_DIM : (2 * h + 1) * HEAD_DIM].astype(jnp.float32)
        own_key = jnp.concatenate([own_key] * grouped, axis=0)
        selves.append(jnp.sum(q * own_key, axis=1, keepdims=True) * scale)
        queries.append(q.astype(jnp.bfloat16))
    live = len_ref[0]
    for c in range(chunks):
        copies[2 + c].wait()
        for h in range(key_heads):
            keys = kv[c * part : (c + 1) * part, 2 * h * HEAD_DIM : (2 * h + 1) * HEAD_DIM]
            s = lax.dot_general(queries[h], keys, BY_ROW, preferred_element_type=jnp.float32)
            at = lax.broadcasted_iota(jnp.int32, (rows, part), 1) + c * part
            scores[h, :, c * part : (c + 1) * part] = jnp.where(at < live, s * scale, -jnp.inf)
    for copy in copies[2 + chunks :]:
        copy.wait()

    experts = router_ref.shape[0]
    routes = routes_ref[...]
    expert_at = lax.broadcasted_iota(jnp.int32, (LANES, tokens), 0) - MASK_AT
    named = jnp.zeros((LANES, tokens), jnp.float32)
    for k in range(routes.shape[0]):
        named = jnp.where(expert_at == routes[k : k + 1, :], 1.0, named)
    side = named.T

    streams = []
    for h in range(key_heads):
        s = scores[h]
        top = jnp.maximum(jnp.max(s, axis=1, keepdims=True), selves[h])
        weights = jnp.exp(s - top).astype(jnp.bfloat16)
        own = jnp.exp(selves[h] - top).astype(jnp.bfloat16).astype(jnp.float32)
        total = jnp.sum(weights.astype(jnp.float32), axis=1, keepdims=True) + own
        value_at = (2 * h + 1) * HEAD_DIM
        mixed = jnp.dot(weights, kv[:, value_at : value_at + HEAD_DIM], preferred_element_type=jnp.float32)
        own_value = new_ref[:, value_at : value_at + HEAD_DIM].astype(jnp.float32)
        mixed = (mixed + own * jnp.concatenate([own_value] * grouped, axis=0)) / total
        for j in range(grouped):
            at = (h * grouped + j) * HEAD_DIM
            got = res_ref[:, at : at + HEAD_DIM].astype(jnp.float32) + mixed[j * tokens : (j + 1) * tokens]
            got = got.astype(jnp.bfloat16)
            out_ref[:, at : at + HEAD_DIM] = got
            streams.append(got.astype(jnp.float32))

    lane = lax.broadcasted_iota(jnp.int32, (tokens, LANES), 1)
    sums = jnp.zeros((tokens, LANES), jnp.float32)

    def put(sums, at, pieces):
        total = pieces[0]
        for piece in pieces[1:]:
            total = total + piece
        return jnp.where(lane == at, jnp.sum(total, axis=1, keepdims=True), sums)

    blocks = range(len(streams))
    sums = put(sums, experts, streams)
    sums = put(sums, experts + 1, [x * x for x in streams])
    gain = gain_ref[...].astype(jnp.float32).reshape(1, -1)
    gains = [gain[:, b * HEAD_DIM : (b + 1) * HEAD_DIM] for b in blocks]
    scaled = [x * g for x, g in zip(streams, gains)]
    for e in range(experts):
        weights = [router_ref[e : e + 1, b * HEAD_DIM : (b + 1) * HEAD_DIM].astype(jnp.float32) for b in blocks]
        sums = put(sums, e, [x * w for x, w in zip(scaled, weights)])
        plain = [jnp.broadcast_to(g * w, (tokens, HEAD_DIM)) for g, w in zip(gains, weights)]
        sums = put(sums, experts + 2 + e, plain)
    for i, term in enumerate(split_terms(sums)):
        side = side + (pltpu.roll(term, i * SLOT, 1) if i else term)
    out_ref[:, columns : columns + LANES] = side.astype(out_ref.dtype)
    gain_rows = jnp.concatenate(
        gains + [jnp.zeros((1, LANES), jnp.float32)] * (tokens - len(gains)), axis=0
    )
    out_ref[:, columns + LANES :] = gain_rows.astype(out_ref.dtype)
    load.wait()


def attend(cache_len, queries, new_kv, kv_cache, residual, routes, router, norm_gain, weight, rest):
    tokens, columns = queries.shape
    slots, width = kv_cache.shape[1:]
    key_heads = new_kv.shape[1] // (2 * HEAD_DIM)
    rows = columns // HEAD_DIM // key_heads * tokens
    chunks = 4
    operands = [queries, new_kv, kv_cache, residual, routes.T, router, norm_gain, weight]
    operands = [pltpu.with_memory_space_constraint(x, pltpu.HBM) for x in operands]
    kept = [pltpu.VMEM(x.shape, x.dtype) for x in operands[:-1]]
    kept[2] = pltpu.VMEM((slots, width), kv_cache.dtype)
    return pl.pallas_call(
        functools.partial(attention_kernel, chunks=chunks, rest=rest),
        out_shape=(
            jax.ShapeDtypeStruct((tokens, columns + 2 * LANES), jnp.bfloat16),
            pltpu.VMEM((rest.size, weight.shape[2]), weight.dtype),
        ),
        in_specs=[pl.BlockSpec(memory_space=pltpu.SMEM)]
        + [pl.BlockSpec(memory_space=pl.ANY)] * len(operands),
        out_specs=(pl.BlockSpec(memory_space=pltpu.VMEM),) * 2,
        scratch_shapes=kept
        + [
            pltpu.VMEM((key_heads, rows, slots), jnp.float32),
            pltpu.SemaphoreType.DMA((chunks + len(operands) - 2,)),
            pltpu.SemaphoreType.DMA,
        ],
        compiler_params=pltpu.CompilerParams(vmem_limit_bytes=8 * MIB),
        cost_estimate=pl.CostEstimate(
            flops=4 * rows * slots * HEAD_DIM * key_heads,
            bytes_accessed=slots * width * 2,
            transcendentals=rows * slots * key_heads,
        ),
        name="attention",
    )(cache_len, *operands)


def load_kernel(_, source, out_ref, token_ref, sem, *, part):
    copy = start_load(source, out_ref, part, sem)
    token_ref[...] = jnp.zeros_like(token_ref)
    copy.wait()


def load(after, weight, part):
    shape = (part.size, weight.shape[2])
    return pl.pallas_call(
        functools.partial(load_kernel, part=part),
        out_shape=(pltpu.VMEM(shape, weight.dtype), jax.ShapeDtypeStruct((8, LANES), jnp.float32)),
        in_specs=[pl.BlockSpec(memory_space=pl.ANY)] * 2,
        out_specs=(pl.BlockSpec(memory_space=pltpu.VMEM),) * 2,
        scratch_shapes=[pltpu.SemaphoreType.DMA],
        compiler_params=pltpu.CompilerParams(vmem_limit_bytes=MIB),
        cost_estimate=pl.CostEstimate(flops=0, bytes_accessed=4 * shape[0] * shape[1], transcendentals=0),
        name="load",
    )(after, pltpu.with_memory_space_constraint(weight, pltpu.HBM))


def norm_kernel(place_ref, _, *refs, experts):
    pieces, out_ref = refs[:-1], refs[-1]
    tokens, wide = pieces[0].shape
    block = wide - 2 * LANES
    model = len(pieces) * block
    total = jnp.zeros((tokens, LANES), jnp.float32)
    for piece in pieces:
        total = total + piece[:, block : block + LANES].astype(jnp.float32)
    sums = total + pltpu.roll(total, LANES - SLOT, 1) + pltpu.roll(total, LANES - 2 * SLOT, 1)
    mean = sums[:, experts : experts + 1] / model
    variance = sums[:, experts + 1 : experts + 2] / model - mean * mean
    inv = lax.rsqrt(variance + NORM_EPS)
    plain = pltpu.roll(sums, LANES - experts - 2, 1)
    logits = (sums - mean * plain) * inv
    lane = lax.broadcasted_iota(jnp.int32, (tokens, LANES), 1)
    named = (pltpu.roll(total, LANES - MASK_AT, 1) > 0) & (lane < experts)
    raised = jnp.where(named, jnp.exp(logits), 0.0)
    share = raised / jnp.sum(raised, axis=1, keepdims=True)
    high = share.astype(jnp.bfloat16).astype(jnp.float32)
    side = high + pltpu.roll(share - high, experts, 1)
    out_ref[:, model:] = side.astype(out_ref.dtype)
    for mask, piece in zip(send_order(len(pieces)) + [0], pieces):
        gain = piece[:, block + LANES :].astype(jnp.float32)
        gain = jnp.concatenate([gain[j : j + 1, :] for j in range(block // LANES)], axis=1)
        x = (piece[:, :block].astype(jnp.float32) - mean) * inv * gain
        at = pl.multiple_of(lax.bitwise_xor(place_ref[0], mask) * block, block)
        out_ref[:, pl.ds(at, block)] = x.astype(out_ref.dtype)


def norm_rows(place, token, blocks, experts):
    tokens, wide = blocks[0].shape
    model = (wide - 2 * LANES) * len(blocks)
    vmem = pl.BlockSpec(memory_space=pltpu.VMEM)
    return pl.pallas_call(
        functools.partial(norm_kernel, experts=experts),
        out_shape=jax.ShapeDtypeStruct((tokens, model + LANES), jnp.bfloat16),
        in_specs=[pl.BlockSpec(memory_space=pltpu.SMEM)] + [vmem] * (1 + len(blocks)),
        out_specs=vmem,
        compiler_params=pltpu.CompilerParams(vmem_limit_bytes=4 * MIB),
        name="norm",
    )(place, token, *blocks)


def stack_kernel(*refs):
    masks = send_order(len(refs) - 1) + [0]
    pieces, out_ref = [refs[masks.index(m)] for m in range(len(masks))], refs[-1]
    rows = 2 * pieces[0].shape[0]
    for i in range(0, len(pieces), 2):
        pair = [piece[...].astype(jnp.float32) for piece in pieces[i : i + 2]]
        out_ref[i // 2 * rows : (i // 2 + 1) * rows] = jnp.concatenate(pair, axis=0).astype(out_ref.dtype)


def stack_rows(pieces):
    rows, wide = pieces[0].shape
    vmem = pl.BlockSpec(memory_space=pltpu.VMEM)
    return pl.pallas_call(
        stack_kernel,
        out_shape=jax.ShapeDtypeStruct((rows * len(pieces), wide), pieces[0].dtype),
        in_specs=[vmem] * len(pieces),
        out_specs=vmem,
        compiler_params=pltpu.CompilerParams(vmem_limit_bytes=4 * MIB),
        name="stack",
    )(*pieces)


def hidden_kernel(place_ref, near, far, gate_a, gate_b, up, hidden, x, *, experts):
    half = near.shape[0]
    model = gate_a.shape[1]
    x[:half] = near[:, :model]
    x[half:] = far[:, :model]
    side = jnp.concatenate([ref[:, model:].astype(jnp.float32) for ref in (near, far)], axis=0)
    lane = lax.broadcasted_iota(jnp.int32, side.shape, 1)
    expert = place_ref[1]
    mine = (lane == expert) | (lane == expert + experts)
    share = jnp.sum(jnp.where(mine, side, 0.0), axis=1, keepdims=True)
    first = 0
    for gate in (gate_a, gate_b):
        units = gate.shape[0]
        for start in range(0, units, UNITS):
            stop = min(start + UNITS, units)
            a = lax.dot_general(x[...], gate[start:stop], BY_ROW, preferred_element_type=jnp.float32)
            b = lax.dot_general(
                up[first + start : first + stop], x[...], BY_ROW, preferred_element_type=jnp.float32
            )
            out = a / (1.0 + jnp.exp(-a)) * share * b.T
            hidden[:, first + start : first + stop] = out.astype(hidden.dtype)
        first += units


def run_hidden(place, near, far, weights, experts):
    units = weights[0].shape[0] + weights[1].shape[0]
    model = weights[0].shape[1]
    rows = 2 * near.shape[0]
    vmem = pl.BlockSpec(memory_space=pltpu.VMEM)
    return pl.pallas_call(
        functools.partial(hidden_kernel, experts=experts),
        out_shape=jax.ShapeDtypeStruct((rows, units), jnp.bfloat16),
        in_specs=[pl.BlockSpec(memory_space=pltpu.SMEM)] + [vmem] * 5,
        out_specs=vmem,
        scratch_shapes=[pltpu.VMEM((rows, model), jnp.bfloat16)],
        compiler_params=pltpu.CompilerParams(vmem_limit_bytes=(18 if rows <= 64 else 24) * MIB),
        cost_estimate=pl.CostEstimate(
            flops=4 * rows * units * model, bytes_accessed=4 * units * model, transcendentals=rows * units
        ),
        name="hidden",
    )(place, near, far, *weights)


def send(x, axis, mask):
    return lax.ppermute(x, axis, [(i, i ^ mask) for i in range(lax.axis_size(axis))])


def send_order(size):
    order = list(range(size - 1, 0, -1))
    order[:2] = order[1::-1]
    return order


def exchange(parts, axis):
    return [send(parts[m], axis, m) for m in send_order(lax.axis_size(axis))]


def add(*terms):
    return sum(t.astype(jnp.float32) for t in terms)


def per_device(
    queries, new_kv, kv_cache, cache_len, residual, norm_gain, router, routes, gate_w, up_w, down_w
):
    sections, groups, tensors = (lax.axis_size(a) for a in ("section", "group", "tensor"))
    experts, block = router.shape
    tokens = queries.shape[0]
    place = lax.axis_index("tensor")
    where = jnp.stack([place, lax.axis_index("section") * tensors + place]).astype(jnp.int32)

    gate_parts = unit_parts(gate_w.shape[1])

    fresh, gate_b = attend(
        cache_len, queries, new_kv, kv_cache, residual, routes, router, norm_gain, gate_w, gate_parts[1]
    )
    blocks = exchange([fresh] * tensors, "tensor") + [fresh]
    gate_a, token = load(fresh, gate_w, gate_parts[0])
    rows = norm_rows(where, token, blocks, experts)
    ranks = exchange([rows] * groups, "group") + [rows]
    near = stack_rows(ranks)
    far = send(near, "section", 1)

    hidden = run_hidden(where, near, far, (gate_a, gate_b, up_w[0]), experts)
    out = jnp.dot(hidden, down_w[0], preferred_element_type=jnp.float32).astype(jnp.bfloat16)
    half = out.shape[0] // 2
    both = add(out[:half], send(out[half:], "section", 1)).astype(jnp.bfloat16)
    both = both.reshape(groups, tokens, -1)
    others = [send(both[m], "group", m) for m in reversed(range(1, groups))]
    got = add(*others[1:], others[0], both[0]).astype(jnp.bfloat16)
    parts = [lax.dynamic_slice_in_dim(got, (place ^ m) * block, block, axis=1) for m in range(tensors)]
    mixed = add(*exchange(parts, "tensor"), parts[0], fresh[:, :block])
    return mixed.astype(jnp.bfloat16)


def solution(mesh):
    rows = P(("section", "group"), "tensor")
    weights = P(("section", "tensor"), "group", None)
    in_specs = (
        rows,
        rows,
        P(("section", "group"), None, "tensor"),
        P(("section", "group")),
        rows,
        P("tensor"),
        P(None, "tensor"),
        P(("section", "group"), None),
        weights,
        weights,
        weights,
    )
    return jax.shard_map(per_device, mesh=mesh, in_specs=in_specs, out_specs=rows, check_vma=False)
```

```python
import functools

import jax
import jax.numpy as jnp
from jax import lax
from jax.experimental import pallas as pl
from jax.experimental.pallas import tpu as pltpu
from jax.sharding import PartitionSpec as P

HEAD_DIM = 128
NORM_EPS = 1e-05
LANES = 128
SLOT = 36
MASK_AT = 3 * SLOT
MIB = 1 << 20
UNITS = 256
BY_ROW = (((1,), (1,)), ((), ()))


def split_terms(value):
    high = value.astype(jnp.bfloat16).astype(jnp.float32)
    rest = value - high
    middle = rest.astype(jnp.bfloat16).astype(jnp.float32)
    return high, middle, rest - middle


def unit_parts(units):
    cut = units * 3 // 4 // UNITS * UNITS or units // 32 * 16
    return pl.ds(0, cut), pl.ds(cut, units - cut)


def start_load(source, target, part, sem):
    copy = pltpu.make_async_copy(source.at[0, part], target, sem)
    copy.start()
    return copy


def attention_kernel(
    len_ref,
    q_hbm,
    new_hbm,
    kv_hbm,
    res_hbm,
    routes_hbm,
    router_hbm,
    gain_hbm,
    gate_hbm,
    up_hbm,
    out_ref,
    gate_ref,
    up_ref,
    q_ref,
    new_ref,
    kv,
    res_ref,
    routes_ref,
    router_ref,
    gain_ref,
    scores,
    sems,
    weight_sems,
    *,
    chunks,
    rest,
):
    slots = kv_hbm.shape[1]
    part = slots // chunks
    sources = [q_hbm, new_hbm] + [kv_hbm.at[0, pl.ds(c * part, part)] for c in range(chunks)]
    targets = [q_ref, new_ref] + [kv.at[pl.ds(c * part, part)] for c in range(chunks)]
    sources += [res_hbm, routes_hbm, router_hbm, gain_hbm]
    targets += [res_ref, routes_ref, router_ref, gain_ref]
    copies = [pltpu.make_async_copy(a, b, sems.at[i]) for i, (a, b) in enumerate(zip(sources, targets))]
    for copy in copies:
        copy.start()
    loads = [
        start_load(gate_hbm, gate_ref, rest, weight_sems.at[0]),
        start_load(up_hbm, up_ref, rest, weight_sems.at[1]),
    ]
    tokens, columns = q_ref.shape
    key_heads = new_ref.shape[1] // (2 * HEAD_DIM)
    grouped = columns // HEAD_DIM // key_heads
    rows = grouped * tokens
    scale = HEAD_DIM ** (-0.5)
    copies[0].wait()
    copies[1].wait()
    queries, selves = [], []
    for h in range(key_heads):
        first = h * grouped * HEAD_DIM
        q = jnp.concatenate(
            [
                q_ref[:, first + j * HEAD_DIM : first + (j + 1) * HEAD_DIM].astype(jnp.float32)
                for j in range(grouped)
            ],
            axis=0,
        )
        own_key = new_ref[:, 2 * h * HEAD_DIM : (2 * h + 1) * HEAD_DIM].astype(jnp.float32)
        own_key = jnp.concatenate([own_key] * grouped, axis=0)
        selves.append(jnp.sum(q * own_key, axis=1, keepdims=True) * scale)
        queries.append(q.astype(jnp.bfloat16))
    live = len_ref[0]
    for c in range(chunks):
        copies[2 + c].wait()
        for h in range(key_heads):
            keys = kv[c * part : (c + 1) * part, 2 * h * HEAD_DIM : (2 * h + 1) * HEAD_DIM]
            s = lax.dot_general(queries[h], keys, BY_ROW, preferred_element_type=jnp.float32)
            at = lax.broadcasted_iota(jnp.int32, (rows, part), 1) + c * part
            scores[h, :, c * part : (c + 1) * part] = jnp.where(at < live, s * scale, -jnp.inf)
    for copy in copies[2 + chunks :]:
        copy.wait()

    experts = router_ref.shape[0]
    routes = routes_ref[...]
    expert_at = lax.broadcasted_iota(jnp.int32, (LANES, tokens), 0) - MASK_AT
    named = jnp.zeros((LANES, tokens), jnp.float32)
    for k in range(routes.shape[0]):
        named = jnp.where(expert_at == routes[k : k + 1, :], 1.0, named)
    side = named.T

    streams = []
    for h in range(key_heads):
        s = scores[h]
        top = jnp.maximum(jnp.max(s, axis=1, keepdims=True), selves[h])
        weights = jnp.exp(s - top).astype(jnp.bfloat16)
        own = jnp.exp(selves[h] - top).astype(jnp.bfloat16).astype(jnp.float32)
        total = jnp.sum(weights.astype(jnp.float32), axis=1, keepdims=True) + own
        value_at = (2 * h + 1) * HEAD_DIM
        mixed = jnp.dot(weights, kv[:, value_at : value_at + HEAD_DIM], preferred_element_type=jnp.float32)
        own_value = new_ref[:, value_at : value_at + HEAD_DIM].astype(jnp.float32)
        mixed = (mixed + own * jnp.concatenate([own_value] * grouped, axis=0)) / total
        for j in range(grouped):
            at = (h * grouped + j) * HEAD_DIM
            got = res_ref[:, at : at + HEAD_DIM].astype(jnp.float32) + mixed[j * tokens : (j + 1) * tokens]
            got = got.astype(jnp.bfloat16)
            out_ref[:, at : at + HEAD_DIM] = got
            streams.append(got.astype(jnp.float32))

    lane = lax.broadcasted_iota(jnp.int32, (tokens, LANES), 1)
    sums = jnp.zeros((tokens, LANES), jnp.float32)

    def put(sums, at, pieces):
        total = pieces[0]
        for piece in pieces[1:]:
            total = total + piece
        return jnp.where(lane == at, jnp.sum(total, axis=1, keepdims=True), sums)

    blocks = range(len(streams))
    sums = put(sums, experts, streams)
    sums = put(sums, experts + 1, [x * x for x in streams])
    gain = gain_ref[...].astype(jnp.float32).reshape(1, -1)
    gains = [gain[:, b * HEAD_DIM : (b + 1) * HEAD_DIM] for b in blocks]
    scaled = [x * g for x, g in zip(streams, gains)]
    for e in range(experts):
        weights = [router_ref[e : e + 1, b * HEAD_DIM : (b + 1) * HEAD_DIM].astype(jnp.float32) for b in blocks]
        sums = put(sums, e, [x * w for x, w in zip(scaled, weights)])
        plain = [jnp.broadcast_to(g * w, (tokens, HEAD_DIM)) for g, w in zip(gains, weights)]
        sums = put(sums, experts + 2 + e, plain)
    for i, term in enumerate(split_terms(sums)):
        side = side + (pltpu.roll(term, i * SLOT, 1) if i else term)
    out_ref[:, columns : columns + LANES] = side.astype(out_ref.dtype)
    gain_rows = jnp.concatenate(
        gains + [jnp.zeros((1, LANES), jnp.float32)] * (tokens - len(gains)), axis=0
    )
    out_ref[:, columns + LANES :] = gain_rows.astype(out_ref.dtype)
    for copy in loads:
        copy.wait()


def attend(cache_len, queries, new_kv, kv_cache, residual, routes, router, norm_gain, gate_w, up_w, rest):
    tokens, columns = queries.shape
    slots, width = kv_cache.shape[1:]
    key_heads = new_kv.shape[1] // (2 * HEAD_DIM)
    rows = columns // HEAD_DIM // key_heads * tokens
    chunks = 4
    operands = [queries, new_kv, kv_cache, residual, routes.T, router, norm_gain, gate_w, up_w]
    operands = [pltpu.with_memory_space_constraint(x, pltpu.HBM) for x in operands]
    kept = [pltpu.VMEM(x.shape, x.dtype) for x in operands[:-2]]
    kept[2] = pltpu.VMEM((slots, width), kv_cache.dtype)
    return pl.pallas_call(
        functools.partial(attention_kernel, chunks=chunks, rest=rest),
        out_shape=(
            jax.ShapeDtypeStruct((tokens, columns + 2 * LANES), jnp.bfloat16),
            *[pltpu.VMEM((rest.size, w.shape[2]), w.dtype) for w in (gate_w, up_w)],
        ),
        in_specs=[pl.BlockSpec(memory_space=pltpu.SMEM)]
        + [pl.BlockSpec(memory_space=pl.ANY)] * len(operands),
        out_specs=(pl.BlockSpec(memory_space=pltpu.VMEM),) * 3,
        scratch_shapes=kept
        + [
            pltpu.VMEM((key_heads, rows, slots), jnp.float32),
            pltpu.SemaphoreType.DMA((chunks + len(operands) - 3,)),
            pltpu.SemaphoreType.DMA((2,)),
        ],
        compiler_params=pltpu.CompilerParams(vmem_limit_bytes=8 * MIB),
        cost_estimate=pl.CostEstimate(
            flops=4 * rows * slots * HEAD_DIM * key_heads,
            bytes_accessed=slots * width * 2,
            transcendentals=rows * slots * key_heads,
        ),
        name="attention",
    )(cache_len, *operands)


def load_kernel(_, source, out_ref, token_ref, sem, *, part):
    copy = start_load(source, out_ref, part, sem)
    token_ref[...] = jnp.zeros_like(token_ref)
    copy.wait()


def load(after, weight, part):
    shape = (part.size, weight.shape[2])
    return pl.pallas_call(
        functools.partial(load_kernel, part=part),
        out_shape=(pltpu.VMEM(shape, weight.dtype), jax.ShapeDtypeStruct((8, LANES), jnp.float32)),
        in_specs=[pl.BlockSpec(memory_space=pl.ANY)] * 2,
        out_specs=(pl.BlockSpec(memory_space=pltpu.VMEM),) * 2,
        scratch_shapes=[pltpu.SemaphoreType.DMA],
        compiler_params=pltpu.CompilerParams(vmem_limit_bytes=MIB),
        cost_estimate=pl.CostEstimate(flops=0, bytes_accessed=4 * shape[0] * shape[1], transcendentals=0),
        name="load",
    )(after, pltpu.with_memory_space_constraint(weight, pltpu.HBM))


def norm_kernel(place_ref, _, *refs, experts):
    pieces, out_ref = refs[:-1], refs[-1]
    tokens, wide = pieces[0].shape
    block = wide - 2 * LANES
    model = len(pieces) * block
    total = jnp.zeros((tokens, LANES), jnp.float32)
    for piece in pieces:
        total = total + piece[:, block : block + LANES].astype(jnp.float32)
    sums = total + pltpu.roll(total, LANES - SLOT, 1) + pltpu.roll(total, LANES - 2 * SLOT, 1)
    mean = sums[:, experts : experts + 1] / model
    variance = sums[:, experts + 1 : experts + 2] / model - mean * mean
    inv = lax.rsqrt(variance + NORM_EPS)
    plain = pltpu.roll(sums, LANES - experts - 2, 1)
    logits = (sums - mean * plain) * inv
    lane = lax.broadcasted_iota(jnp.int32, (tokens, LANES), 1)
    named = (pltpu.roll(total, LANES - MASK_AT, 1) > 0) & (lane < experts)
    raised = jnp.where(named, jnp.exp(logits), 0.0)
    share = raised / jnp.sum(raised, axis=1, keepdims=True)
    high = share.astype(jnp.bfloat16).astype(jnp.float32)
    side = high + pltpu.roll(share - high, experts, 1)
    out_ref[:, model:] = side.astype(out_ref.dtype)
    for mask, piece in zip(send_order(len(pieces)) + [0], pieces):
        gain = piece[:, block + LANES :].astype(jnp.float32)
        gain = jnp.concatenate([gain[j : j + 1, :] for j in range(block // LANES)], axis=1)
        x = (piece[:, :block].astype(jnp.float32) - mean) * inv * gain
        at = pl.multiple_of(lax.bitwise_xor(place_ref[0], mask) * block, block)
        out_ref[:, pl.ds(at, block)] = x.astype(out_ref.dtype)


def norm_rows(place, token, blocks, experts):
    tokens, wide = blocks[0].shape
    model = (wide - 2 * LANES) * len(blocks)
    vmem = pl.BlockSpec(memory_space=pltpu.VMEM)
    return pl.pallas_call(
        functools.partial(norm_kernel, experts=experts),
        out_shape=jax.ShapeDtypeStruct((tokens, model + LANES), jnp.bfloat16),
        in_specs=[pl.BlockSpec(memory_space=pltpu.SMEM)] + [vmem] * (1 + len(blocks)),
        out_specs=vmem,
        compiler_params=pltpu.CompilerParams(vmem_limit_bytes=4 * MIB),
        name="norm",
    )(place, token, *blocks)


def stack_kernel(_, *refs):
    masks = send_order(len(refs) - 1) + [0]
    pieces, out_ref = [refs[masks.index(m)] for m in range(len(masks))], refs[-1]
    rows = 2 * pieces[0].shape[0]
    for i in range(0, len(pieces), 2):
        pair = [piece[...].astype(jnp.float32) for piece in pieces[i : i + 2]]
        out_ref[i // 2 * rows : (i // 2 + 1) * rows] = jnp.concatenate(pair, axis=0).astype(out_ref.dtype)


def stack_rows(token, pieces):
    rows, wide = pieces[0].shape
    vmem = pl.BlockSpec(memory_space=pltpu.VMEM)
    return pl.pallas_call(
        stack_kernel,
        out_shape=jax.ShapeDtypeStruct((rows * len(pieces), wide), pieces[0].dtype),
        in_specs=[vmem] * (1 + len(pieces)),
        out_specs=vmem,
        compiler_params=pltpu.CompilerParams(vmem_limit_bytes=4 * MIB),
        name="stack",
    )(token, *pieces)


def hidden_kernel(place_ref, near, far, gate_a, gate_b, up_a, up_b, hidden, x, *, experts):
    half = near.shape[0]
    model = gate_a.shape[1]
    x[:half] = near[:, :model]
    x[half:] = far[:, :model]
    side = jnp.concatenate([ref[:, model:].astype(jnp.float32) for ref in (near, far)], axis=0)
    lane = lax.broadcasted_iota(jnp.int32, side.shape, 1)
    expert = place_ref[1]
    mine = (lane == expert) | (lane == expert + experts)
    share = jnp.sum(jnp.where(mine, side, 0.0), axis=1, keepdims=True)
    units = gate_a.shape[0] + gate_b.shape[0]
    cuts = sorted({0, gate_a.shape[0], up_a.shape[0], units})

    def rows(first, second, start, stop):
        cut = first.shape[0]
        return first[start:stop] if stop <= cut else second[start - cut : stop - cut]

    for low, high in zip(cuts, cuts[1:]):
        for start in range(low, high, UNITS):
            stop = min(start + UNITS, high)
            gate, up = rows(gate_a, gate_b, start, stop), rows(up_a, up_b, start, stop)
            a = lax.dot_general(x[...], gate, BY_ROW, preferred_element_type=jnp.float32)
            b = lax.dot_general(up, x[...], BY_ROW, preferred_element_type=jnp.float32)
            out = a / (1.0 + jnp.exp(-a)) * share * b.T
            hidden[:, start:stop] = out.astype(hidden.dtype)


def run_hidden(place, near, far, weights, experts):
    units = weights[0].shape[0] + weights[1].shape[0]
    model = weights[0].shape[1]
    rows = 2 * near.shape[0]
    vmem = pl.BlockSpec(memory_space=pltpu.VMEM)
    return pl.pallas_call(
        functools.partial(hidden_kernel, experts=experts),
        out_shape=jax.ShapeDtypeStruct((rows, units), jnp.bfloat16),
        in_specs=[pl.BlockSpec(memory_space=pltpu.SMEM)] + [vmem] * 6,
        out_specs=vmem,
        scratch_shapes=[pltpu.VMEM((rows, model), jnp.bfloat16)],
        compiler_params=pltpu.CompilerParams(vmem_limit_bytes=(6 if rows <= 64 else 24) * MIB),
        cost_estimate=pl.CostEstimate(
            flops=4 * rows * units * model, bytes_accessed=4 * units * model, transcendentals=rows * units
        ),
        name="hidden",
    )(place, near, far, *weights)


def send(x, axis, mask):
    return lax.ppermute(x, axis, [(i, i ^ mask) for i in range(lax.axis_size(axis))])


def send_order(size):
    order = list(range(size - 1, 0, -1))
    order[:2] = order[1::-1]
    return order


def exchange(parts, axis):
    return [send(parts[m], axis, m) for m in send_order(lax.axis_size(axis))]


def add(*terms):
    return sum(t.astype(jnp.float32) for t in terms)


def per_device(
    queries, new_kv, kv_cache, cache_len, residual, norm_gain, router, routes, gate_w, up_w, down_w
):
    sections, groups, tensors = (lax.axis_size(a) for a in ("section", "group", "tensor"))
    experts, block = router.shape
    tokens = queries.shape[0]
    place = lax.axis_index("tensor")
    where = jnp.stack([place, lax.axis_index("section") * tensors + place]).astype(jnp.int32)

    later, beside = unit_parts(gate_w.shape[1])

    fresh, gate_b, up_b = attend(
        cache_len, queries, new_kv, kv_cache, residual, routes, router, norm_gain, gate_w, up_w, beside
    )
    blocks = exchange([fresh] * tensors, "tensor") + [fresh]
    gate_a, token = load(fresh, gate_w, later)
    rows = norm_rows(where, token, blocks, experts)
    ranks = exchange([rows] * groups, "group") + [rows]
    up_a, token = load(rows, up_w, later)
    near = stack_rows(token, ranks)
    far = send(near, "section", 1)

    hidden = run_hidden(where, near, far, (gate_a, gate_b, up_a, up_b), experts)
    out = jnp.dot(hidden, down_w[0], preferred_element_type=jnp.float32).astype(jnp.bfloat16)
    half = out.shape[0] // 2
    both = add(out[:half], send(out[half:], "section", 1)).astype(jnp.bfloat16)
    both = both.reshape(groups, tokens, -1)
    others = [send(both[m], "group", m) for m in reversed(range(1, groups))]
    got = add(*others[1:], others[0], both[0]).astype(jnp.bfloat16)
    parts = [lax.dynamic_slice_in_dim(got, (place ^ m) * block, block, axis=1) for m in range(tensors)]
    mixed = add(*exchange(parts, "tensor"), parts[0], fresh[:, :block])
    return mixed.astype(jnp.bfloat16)


def solution(mesh):
    rows = P(("section", "group"), "tensor")
    weights = P(("section", "tensor"), "group", None)
    in_specs = (
        rows,
        rows,
        P(("section", "group"), None, "tensor"),
        P(("section", "group")),
        rows,
        P("tensor"),
        P(None, "tensor"),
        P(("section", "group"), None),
        weights,
        weights,
        weights,
    )
    return jax.shard_map(per_device, mesh=mesh, in_specs=in_specs, out_specs=rows, check_vma=False)
```
